32 devices in a mesh: outer: 4 (over z), inner: 8 (over y, x, core).
Axes of the slice: x: 2, y: 2, z: 4, core: 2. Of those that a mesh axis runs over, the one named last changes fastest.
Arguments:
- normals: bfloat16 [512, 128, 512], P('outer', 'inner'), may hold values from -6 to 6
- states: bfloat16 [512, 512], P('outer'), may hold values from -0.29882812 to 0.29882812
- loadings: bfloat16 [2048, 512], replicated, may hold values from -6 to 6
- strikes: float32 [2048], replicated, may hold values from -6 to 6
- hedge: float32 [2048], replicated, may hold values from -384 to 384
- sigma: float32 [512], replicated, may hold values from 0.02 to 0.1
- tail: int32 [128], replicated, may hold values from 0 to 511, as said below
Outputs:
- grad: float32 [2048, 512], P(('outer', 'inner'))
The draws below stay inside these ranges and needn't reach their ends.
Inputs may be any that keep to these rules, and one draw needn't show every extreme that they name: Increasing and distinct. Group g holds nodes g * 128 to (g + 1) * 128 - 1; at most 80 tail indices fall into one group, and some group holds exactly 80.
All inputs are finite; a program needn't handle non-finite values.
Results may differ from the reference program's by a relative error of at most 0.00057.
Values may be sent and summed in bfloat16 or wider, within the bound.
No kernel may reach another device: no remote copies, remote signals or barrier semaphores. Data moves between devices by JAX's collectives and lax.ppermute only.
A program may use at most 64 MiB of HBM per device.

```python
import math
import jax
import jax.numpy as jnp
from jax import lax

M = 2048
K = 512
GROUPS = 4
PATHS = 128
NODE_GRP = 128
NODES = 512
TAIL = 128
CAP = 80


def draw_tail(key, part):
    first_key, second_key, third_key = jax.random.split(jax.random.fold_in(key, 17), 3)
    heavy = jax.random.randint(first_key, (), 0, GROUPS)
    groups_idx = jnp.arange(GROUPS, dtype=jnp.int32)
    others = GROUPS - 1
    rank = (groups_idx - heavy - 1) % GROUPS
    remain = TAIL - CAP
    base = remain // others
    extra = remain % others
    drawn = base + (rank < extra).astype(jnp.int32)
    shifts = jax.random.randint(second_key, (GROUPS,), 0, base // 2 + 1)
    shifts = jnp.where(rank == others, 0, shifts)
    before = (heavy + 1 + (rank - 1) % others) % GROUPS
    counts = jnp.where(rank == others, CAP, drawn + shifts - shifts[before])
    offsets = jax.random.randint(third_key, (GROUPS,), 0, NODE_GRP - counts + 1)
    ends = jnp.cumsum(counts)
    begins = ends - counts
    places = jnp.arange(TAIL, dtype=jnp.int32)
    owner = jnp.sum((places[:, None] >= ends[None, :]).astype(jnp.int32), axis=1)
    return (owner * NODE_GRP + offsets[owner] + places - begins[owner]).astype(jnp.int32)


def level_of(stream_key, shape, shards, low, top_value):
    factor_of, own = 1.0, jax.random.fold_in(stream_key, 6)
    for position, shards_of in shards:
        heights = jnp.exp(jax.random.uniform(jax.random.fold_in(own, position), (shards_of,), jnp.float32, low / len(shards), top_value / len(shards)))
        factor_of = factor_of * jnp.repeat(heights, shape[position] // shards_of).reshape([-1 if axis == position else 1 for axis in range(len(shape))])
    return factor_of


def gaussian(own_key, dims, deviation, bound, shards=(), held_as=jnp.bfloat16):
    factor_of = level_of(own_key, dims, shards, -0.22, 0.18) if shards else 1.0
    entries = jax.random.normal(own_key, dims, jnp.float32) * deviation * factor_of
    return jnp.minimum(jnp.maximum(entries, -bound), bound).astype(held_as)


def setup_inputs(seed: int = 0) -> dict:
    key_of = jax.random.split(jax.random.key(seed), 8)
    normals = gaussian(key_of[0], (NODES, PATHS, K), 1.0, 6.0, ((0, 4), (1, 8)))
    states = gaussian(key_of[1], (NODES, K), 0.05, 0.29882812, ((0, 4),))
    loadings = gaussian(key_of[2], (M, K), 1.0, 6.0)
    strikes = gaussian(key_of[3], (M,), 1.0, 6.0, (), jnp.float32)
    hedge = gaussian(key_of[4], (M,), 64.0, 384.0, (), jnp.float32)
    sigma = jnp.clip(jnp.exp(jax.random.uniform(key_of[5], (K,), jnp.float32, math.log(0.02), math.log(0.1))), 0.02, 0.1)
    tail = draw_tail(jax.random.fold_in(key_of[7], 71), 0)
    return {"normals": normals, "states": states, "loadings": loadings, "strikes": strikes, "hedge": hedge, "sigma": sigma, "tail": tail}


EPSILON = 1e-06

def reference(normals, states, loadings, strikes, hedge, sigma, tail):
    width = math.gcd(TAIL, 8)
    starts = jnp.arange(0, TAIL, width).astype(jnp.int32)

    def block(total, start):
        nodes = lax.dynamic_slice_in_dim(tail, start, width, 0)
        values = jnp.take(normals, nodes, axis=0).astype(jnp.float32)
        center = lax.optimization_barrier(jnp.sum(values, axis=1)) / PATHS
        spread = lax.optimization_barrier(jnp.sum(values * values, axis=1)) / PATHS - center * center
        scaled = ((values - center[:, None, :]) * lax.rsqrt(spread + EPSILON)[:, None, :]).astype(jnp.bfloat16)
        levels = jnp.take(states, nodes, axis=0).astype(jnp.float32)
        factors = (levels[:, None, :] + sigma * scaled.astype(jnp.float32)).astype(jnp.bfloat16)
        factors = factors.reshape(width * PATHS, K)
        level = lax.dot_general(factors, loadings, (((1,), (1,)), ((), ())), preferred_element_type=jnp.float32) - strikes
        weight = (hedge * jax.nn.sigmoid(level)).astype(jnp.bfloat16)
        cross = lax.dot_general(weight, scaled.reshape(width * PATHS, K), (((0,), (0,)), ((), ())), preferred_element_type=jnp.float32)
        return (total + cross, None)
    total, unused = lax.scan(block, jnp.zeros((M, K), jnp.float32), starts)
    return loadings.astype(jnp.float32) * total / (TAIL * PATHS)
```

```python
import functools

import jax
import jax.numpy as jnp
from jax import lax
from jax.experimental import pallas as pl
from jax.experimental.pallas import tpu as pltpu
from jax.sharding import PartitionSpec as P

CAP = 80
EPSILON = 1e-06
VMEM = pl.BlockSpec(memory_space=pltpu.VMEM)
SMEM = pl.BlockSpec(memory_space=pltpu.SMEM)
HBM = pl.BlockSpec(memory_space=pl.ANY)
PARAMS = pltpu.CompilerParams(vmem_limit_bytes=32 << 20)
F32 = jnp.float32
BF16 = jnp.bfloat16
F16 = jnp.float16


def split_of(count, most):
    for size in range(min(count, most), 0, -1):
        if count % size == 0:
            return size
    return 1


def gather_kernel(
    part, place, tail, normals, states, chosen, levels, mine, other, live, onehot, sems
):
    node_count = normals.shape[0]
    tail_count = tail.shape[0]
    group, core = place[0], place[1]
    base = group * node_count
    first = jnp.int32(0)
    past = jnp.int32(0)
    for t in range(tail_count):
        node = tail[t]
        first += (node < base).astype(jnp.int32)
        past += (node < base + node_count).astype(jnp.int32)
    live[0] = past - first
    lanes = lax.broadcasted_iota(jnp.int32, (1, node_count), 1)
    parts = CAP // part

    def fetch(slot, sem):
        at = jnp.minimum(first + slot, tail_count - 1)
        node = jnp.clip(tail[at] - base, 0, node_count - 1)
        pltpu.make_async_copy(normals.at[node], chosen.at[slot], sem).start()
        onehot[pl.ds(slot, 1), :] = (lanes == node).astype(F32)

    for p in range(parts):
        for slot in range(p * part, (p + 1) * part):
            fetch(slot, sems.at[p])
    levels[...] = jnp.dot(
        onehot[...].astype(BF16), states[...], preferred_element_type=F32
    ).astype(BF16)
    half = CAP // 2
    for p in range(parts):
        piece = chosen.at[pl.ds(p * part, part)]
        pltpu.make_async_copy(piece, piece, sems.at[p]).wait()
        values = piece[...].astype(F32)
        sums = jnp.sum(values, axis=1)
        squares = jnp.sum(values * values, axis=1)
        which = p * part // half
        rows = pl.ds(p * part - which * half, part)

        @pl.when(core == which)
        def _():
            mine[0, rows, :] = sums
            mine[1, rows, :] = squares

        @pl.when(core != which)
        def _():
            other[0, rows, :] = sums
            other[1, rows, :] = squares


def gather_nodes(place, tail, normals, states):
    _, paths, factors_n = normals.shape
    part = split_of(CAP // 2, 8)
    sums = jax.ShapeDtypeStruct((2, CAP // 2, factors_n), F32)
    return pl.pallas_call(
        functools.partial(gather_kernel, part),
        in_specs=[SMEM, SMEM, HBM, VMEM],
        out_specs=[VMEM, VMEM, VMEM, VMEM, SMEM],
        out_shape=[
            jax.ShapeDtypeStruct((CAP, paths, factors_n), BF16),
            jax.ShapeDtypeStruct((CAP, factors_n), BF16),
            sums,
            sums,
            jax.ShapeDtypeStruct((1,), jnp.int32),
        ],
        scratch_shapes=[
            pltpu.VMEM((CAP, normals.shape[0]), F32),
            pltpu.SemaphoreType.DMA((CAP // part,)),
        ],
        compiler_params=PARAMS,
        name="gather_nodes",
    )(place, tail, normals, states)


def moments_kernel(paths, place, live, *refs):
    *sums, stats = refs
    half = stats.shape[1]
    total = sums[0][0]
    squares = sums[0][1]
    for ref in sums[1:]:
        total = total + ref[0]
        squares = squares + ref[1]
    center = total / paths
    spread = squares / paths - center * center
    slot = lax.broadcasted_iota(jnp.int32, center.shape, 0) + place[1] * half
    stats[0] = center
    stats[1] = jnp.where(slot < live[0], lax.rsqrt(spread + EPSILON), 0.0)


def moments(paths, place, live, sums):
    return pl.pallas_call(
        functools.partial(moments_kernel, paths),
        in_specs=[SMEM, SMEM] + [VMEM] * len(sums),
        out_specs=VMEM,
        out_shape=jax.ShapeDtypeStruct(sums[0].shape, F32),
        compiler_params=PARAMS,
        name="moments",
    )(place, live, *sums)


def order_kernel(bound, blocks, loadings, strikes, hedge, *outs):
    chunks, (steps, _, _) = len(outs) // 2, outs[0].shape
    rows = loadings.shape[1]
    eye = lax.broadcasted_iota(jnp.int32, (rows, rows), 0) == lax.broadcasted_iota(
        jnp.int32, (rows, rows), 1
    )

    def column(ref, block):
        return jnp.sum(
            jnp.where(eye, ref[pl.ds(block, 1), :], 0.0), axis=1, keepdims=True
        )

    for chunk in range(chunks):
        ordered, terms = outs[chunk], outs[chunks + chunk]
        for step in range(steps):
            block = blocks[chunk * steps + step]
            ordered[step] = (loadings[block].astype(F32) * 0.5).astype(BF16)
            size = column(hedge, block)
            scale = jnp.abs(size)
            terms[0, step] = column(strikes, block) * 0.5
            terms[1, step] = size * 0.5
            terms[2, step] = jnp.where(
                scale > 1e-30, bound / jnp.maximum(scale, 1e-30), 0.0
            )


def order(bound, chunks, steps, blocks, loadings, strikes, hedge):
    _, rows, factors_n = loadings.shape
    return pl.pallas_call(
        functools.partial(order_kernel, bound),
        in_specs=[SMEM, VMEM, VMEM, VMEM],
        out_specs=[VMEM] * (2 * chunks),
        out_shape=[jax.ShapeDtypeStruct((steps, rows, factors_n), BF16)] * chunks
        + [jax.ShapeDtypeStruct((3, steps, rows, 1), F32)] * chunks,
        compiler_params=PARAMS,
        name="order_instruments",
    )(blocks, loadings, strikes, hedge)


def cross_of(tile, scaled, factors, loadings, terms):
    strikes, hedge, scale = terms[0], terms[1], terms[2]
    part = loadings[...]
    count = scaled.shape[0] // tile

    def level(r):
        rows = factors[r * tile : (r + 1) * tile, :]
        return lax.dot_general(
            part, rows, (((1,), (1,)), ((), ())), preferred_element_type=F32
        )

    total = None
    current = level(0)
    for r in range(count):
        after = level(r + 1) if r + 1 < count else None
        weight = (jnp.tanh(current - strikes) * hedge + hedge).astype(BF16)
        cross = jnp.dot(
            weight, scaled[r * tile : (r + 1) * tile, :], preferred_element_type=F32
        )
        total = cross if total is None else total + cross
        current = after
    return total * scale


def first_kernel(
    tile, place, own, theirs, own_stats, their_stats, levels, sigma, loadings, terms,
    scaled, factors, out, stats,
):
    slots, paths, factors_n = own.shape
    half = slots // 2
    low, high = place[1] * half, (1 - place[1]) * half
    for kind in range(2):
        stats[kind, pl.ds(low, half), :] = own_stats[kind]
        stats[kind, pl.ds(high, half), :] = their_stats[kind]
    sigmas = sigma[...].reshape(1, 1, factors_n)
    step = split_of(slots, 16)
    for side, source in enumerate((own, theirs)):
        for begin in range(0, slots, step):
            here = slice(begin, begin + step)
            center = stats[0, here, :]
            rstd = stats[1, here, :]
            level = levels[here, :].astype(F32)
            values = source[here].astype(F32)
            unit = ((values - center[:, None, :]) * rstd[:, None, :]).astype(BF16)
            mixed = (level[:, None, :] + sigmas * unit.astype(F32)).astype(BF16)
            rows = pl.ds((side * slots + begin) * paths, step * paths)
            scaled[rows, :] = unit.reshape(step * paths, factors_n)
            factors[rows, :] = mixed.reshape(step * paths, factors_n)
    out[...] = cross_of(tile, scaled, factors, loadings, terms)


def next_kernel(tile, scaled, factors, loadings, terms, out):
    out[...] = cross_of(tile, scaled, factors, loadings, terms)


def cost_of(rows, count, factors_n):
    return pl.CostEstimate(
        flops=4 * rows * count * factors_n,
        bytes_accessed=4 * rows * factors_n,
        transcendentals=rows * count,
    )


def first_chunk(place, own, theirs, own_stats, their_stats, levels, sigma, ordered, terms):
    slots, paths, factors_n = own.shape
    rows = 2 * slots * paths
    count = ordered.shape[0]
    mixed = jax.ShapeDtypeStruct((rows, factors_n), BF16)
    return pl.pallas_call(
        functools.partial(first_kernel, split_of(rows, 512)),
        in_specs=[SMEM] + [VMEM] * 8,
        out_specs=[VMEM, VMEM, VMEM],
        out_shape=[mixed, mixed, jax.ShapeDtypeStruct((count, factors_n), F32)],
        scratch_shapes=[pltpu.VMEM((2, slots, factors_n), F32)],
        compiler_params=PARAMS,
        cost_estimate=cost_of(rows, count, factors_n),
        name="first_chunk",
    )(place, own, theirs, own_stats, their_stats, levels, sigma, ordered, terms)


def next_chunk(scaled, factors, ordered, terms):
    rows, factors_n = scaled.shape
    count = ordered.shape[0]
    return pl.pallas_call(
        functools.partial(next_kernel, split_of(rows, 512)),
        in_specs=[VMEM] * 4,
        out_specs=VMEM,
        out_shape=jax.ShapeDtypeStruct((count, factors_n), F32),
        compiler_params=PARAMS,
        cost_estimate=cost_of(rows, count, factors_n),
        name="next_chunk",
    )(scaled, factors, ordered, terms)


def body(normals, states, loadings, strikes, hedge, sigma, tail):
    groups = lax.axis_size("outer")
    inner = lax.axis_size("inner")
    chips = inner // 2
    group = lax.axis_index("outer")
    position = lax.axis_index("inner")
    chip, core = position // 2, position % 2
    node_count, per_node, factors_n = normals.shape
    instruments = loadings.shape[0]
    tail_count = tail.shape[0]
    paths = per_node * inner
    rows = instruments // (groups * inner)
    paired = chips & (chips - 1) == 0

    def partner(of, d):
        return of ^ d if paired else (of + d) % chips

    def to_core(x):
        return lax.ppermute(x, "inner", [(i, i ^ 1) for i in range(inner)])

    def to_chip(x, d):
        return lax.ppermute(
            x, "inner", [(i, partner(i // 2, d) * 2 + i % 2) for i in range(inner)]
        )

    def to_group(x, s):
        return lax.ppermute(x, "outer", [(g, (g + s) % groups) for g in range(groups)])

    place = jnp.stack([group, core]).astype(jnp.int32)
    blocks = jnp.stack(
        [
            ((group + s) % groups) * inner + partner(chip, d) * 2 + core
            for d in range(chips)
            for s in range(groups)
        ]
    ).astype(jnp.int32)
    bound = 32768.0 / (tail_count * paths)
    parts = order(
        bound,
        chips,
        groups,
        blocks,
        loadings.reshape(groups * inner, rows, factors_n),
        strikes.reshape(groups * inner, rows),
        hedge.reshape(groups * inner, rows),
    )
    ordered = [part.reshape(groups * rows, factors_n) for part in parts[:chips]]
    terms = [part.reshape(3, groups * rows, 1) for part in parts[chips:]]

    chosen, levels, mine, other, live = gather_nodes(place, tail, normals, states)
    pair_sums = mine + to_core(other)
    theirs = to_core(chosen)
    sums = [pair_sums] + [to_chip(pair_sums, d) for d in range(chips - 1, 0, -1)]
    stats = moments(paths, place, live, sums)
    their_stats = to_core(stats)

    arrived = []
    scaled = factors = kept = None
    for d in range(chips - 1, -1, -1):
        if scaled is None:
            scaled, factors, partial = first_chunk(
                place, chosen, theirs, stats, their_stats, levels,
                sigma.reshape(1, factors_n), ordered[d], terms[d],
            )
        else:
            partial = next_chunk(scaled, factors, ordered[d], terms[d])
        if d:
            arrived.append(to_chip(partial.astype(F16), d))
        else:
            kept = partial
    for item in arrived:
        kept = kept + item.astype(F32)
    owned = kept[:rows]
    for s in range(1, groups):
        owned = owned + to_group(kept[s * rows : (s + 1) * rows].astype(F16), s).astype(F32)

    block = group * inner + position
    own_loadings = lax.dynamic_slice_in_dim(loadings, block * rows, rows, 0).astype(F32)
    own_hedge = jnp.abs(lax.dynamic_slice_in_dim(hedge, block * rows, rows, 0))
    return own_loadings * owned * (own_hedge / (bound * tail_count * paths))[:, None]


def solution(mesh):
    placed = (P("outer", "inner", None), P("outer", None), P(), P(), P(), P(), P())
    return jax.shard_map(
        body, mesh=mesh, in_specs=placed, out_specs=P(("outer", "inner"), None), check_vma=False
    )
```

```python
import functools

import jax
import jax.numpy as jnp
from jax import lax
from jax.experimental import pallas as pl
from jax.experimental.pallas import tpu as pltpu
from jax.sharding import PartitionSpec as P

CAP = 80
EPSILON = 1e-06
VMEM = pl.BlockSpec(memory_space=pltpu.VMEM)
SMEM = pl.BlockSpec(memory_space=pltpu.SMEM)
HBM = pl.BlockSpec(memory_space=pltpu.HBM)
F32 = jnp.float32
BF16 = jnp.bfloat16
F16 = jnp.float16


def split_of(count, most):
    for size in range(min(count, most), 0, -1):
        if count % size == 0:
            return size
    return 1


def small(mebibytes):
    return pltpu.CompilerParams(vmem_limit_bytes=mebibytes << 20)


def gather_kernel(
    part, place, tail_hbm, normals, states_hbm, chosen, levels, mine, other, live,
    tail, states, onehot, sems, tail_sem, states_sem,
):
    node_count = normals.shape[0]
    tail_count = tail.shape[0]
    group, core = place[0], place[1]
    tail_copy = pltpu.make_async_copy(tail_hbm, tail, tail_sem)
    states_copy = pltpu.make_async_copy(states_hbm, states, states_sem)
    tail_copy.start()
    states_copy.start()
    base = group * node_count
    lanes = lax.broadcasted_iota(jnp.int32, (1, node_count), 1)
    tail_copy.wait()
    first = jnp.int32(0)
    past = jnp.int32(0)
    for t in range(tail_count):
        first += (tail[t] < base).astype(jnp.int32)
        past += (tail[t] < base + node_count).astype(jnp.int32)
    live[0] = past - first
    parts = CAP // part
    for p in range(parts):
        for slot in range(p * part, (p + 1) * part):
            at = jnp.minimum(first + slot, tail_count - 1)
            node = jnp.clip(tail[at] - base, 0, node_count - 1)
            pltpu.make_async_copy(normals.at[node], chosen.at[slot], sems.at[p]).start()
            onehot[pl.ds(slot, 1), :] = (lanes == node).astype(F32)
    half = CAP // 2
    for p in range(parts):
        piece = chosen.at[pl.ds(p * part, part)]
        pltpu.make_async_copy(piece, piece, sems.at[p]).wait()
        values = piece[...].astype(F32)
        sums = jnp.sum(values, axis=1)
        squares = jnp.sum(values * values, axis=1)
        which = p * part // half
        rows = pl.ds(p * part - which * half, part)

        @pl.when(core == which)
        def _():
            mine[0, rows, :] = sums
            mine[1, rows, :] = squares

        @pl.when(core != which)
        def _():
            other[0, rows, :] = sums
            other[1, rows, :] = squares

    states_copy.wait()
    levels[...] = jnp.dot(
        onehot[...].astype(BF16), states[...], preferred_element_type=F32
    )


def gather_nodes(place, tail, normals, states):
    _, paths, factors_n = normals.shape
    part = split_of(CAP // 2, 8)
    sums = jax.ShapeDtypeStruct((2, CAP // 2, factors_n), F32)
    return pl.pallas_call(
        functools.partial(gather_kernel, part),
        in_specs=[SMEM, HBM, HBM, HBM],
        out_specs=[VMEM, VMEM, VMEM, VMEM, SMEM],
        out_shape=[
            jax.ShapeDtypeStruct((CAP, paths, factors_n), BF16),
            jax.ShapeDtypeStruct((CAP, factors_n), F32),
            sums,
            sums,
            jax.ShapeDtypeStruct((1,), jnp.int32),
        ],
        scratch_shapes=[
            pltpu.SMEM(tail.shape, jnp.int32),
            pltpu.VMEM(states.shape, BF16),
            pltpu.VMEM((CAP, normals.shape[0]), F32),
            pltpu.SemaphoreType.DMA((CAP // part,)),
            pltpu.SemaphoreType.DMA,
            pltpu.SemaphoreType.DMA,
        ],
        compiler_params=small(8),
        cost_estimate=pl.CostEstimate(flops=0, bytes_accessed=0, transcendentals=0),
        name="gather_nodes",
    )(place, tail, normals, states)


def moments_kernel(paths, place, live, *refs):
    *sums, stats = refs
    half = stats.shape[1]
    total = sums[0][0]
    squares = sums[0][1]
    for ref in sums[1:]:
        total = total + ref[0]
        squares = squares + ref[1]
    center = total / paths
    spread = squares / paths - center * center
    slot = lax.broadcasted_iota(jnp.int32, center.shape, 0) + place[1] * half
    stats[0] = center
    stats[1] = jnp.where(slot < live[0], lax.rsqrt(spread + EPSILON), 0.0)


def moments(paths, place, live, sums):
    return pl.pallas_call(
        functools.partial(moments_kernel, paths),
        in_specs=[SMEM, SMEM] + [VMEM] * len(sums),
        out_specs=VMEM,
        out_shape=jax.ShapeDtypeStruct(sums[0].shape, F32),
        compiler_params=small(4),
        name="moments",
    )(place, live, *sums)


def order_kernel(unit, bound, blocks, loadings, strikes, hedge, gain, *outs):
    chunks, (steps, _, _) = len(outs) // 2, outs[0].shape
    rows = loadings.shape[1]
    eye = lax.broadcasted_iota(jnp.int32, (rows, rows), 0) == lax.broadcasted_iota(
        jnp.int32, (rows, rows), 1
    )

    def column(ref, block):
        return jnp.sum(
            jnp.where(eye, ref[pl.ds(block, 1), :], 0.0), axis=1, keepdims=True
        )

    for chunk in range(chunks):
        ordered, terms = outs[chunk], outs[chunks + chunk]
        for step in range(steps):
            block = blocks[chunk * steps + step]
            own = loadings[block].astype(F32)
            ordered[step] = (own * 0.5).astype(BF16)
            size = column(hedge, block)
            scale = jnp.abs(size)
            if chunk == 0 and step == 0:
                gain[...] = own * (scale * unit)
            terms[0, step] = column(strikes, block) * 0.5
            terms[1, step] = size * 0.5
            terms[2, step] = jnp.where(
                scale > 1e-30, bound / jnp.maximum(scale, 1e-30), 0.0
            )


def order(unit, bound, chunks, steps, blocks, loadings, strikes, hedge):
    _, rows, factors_n = loadings.shape
    return pl.pallas_call(
        functools.partial(order_kernel, unit, bound),
        in_specs=[SMEM, VMEM, VMEM, VMEM],
        out_specs=[VMEM] * (2 * chunks + 1),
        out_shape=[jax.ShapeDtypeStruct((rows, factors_n), F32)]
        + [jax.ShapeDtypeStruct((steps, rows, factors_n), BF16)] * chunks
        + [jax.ShapeDtypeStruct((3, steps, rows, 1), F32)] * chunks,
        compiler_params=small(12),
        name="order_instruments",
    )(blocks, loadings, strikes, hedge)


def cross_of(tile, scaled, factors, loadings, terms, prepare=None):
    strikes, hedge, scale = terms[0], terms[1], terms[2]
    part = loadings[...]
    count = scaled.shape[0] // tile

    def level(r):
        if prepare is not None:
            prepare(r)
        rows = factors[r * tile : (r + 1) * tile, :]
        return lax.dot_general(
            part, rows, (((1,), (1,)), ((), ())), preferred_element_type=F32
        )

    total = None
    current = level(0)
    for r in range(count):
        after = level(r + 1) if r + 1 < count else None
        weight = (jnp.tanh(current - strikes) * hedge + hedge).astype(BF16)
        cross = jnp.dot(
            weight, scaled[r * tile : (r + 1) * tile, :], preferred_element_type=F32
        )
        total = cross if total is None else total + cross
        current = after
    return total * scale


def first_kernel(
    tile, place, own, theirs, own_stats, their_stats, levels, sigma, loadings, terms,
    scaled, factors, out, stats,
):
    slots, paths, factors_n = own.shape
    half = slots // 2
    low, high = place[1] * half, (1 - place[1]) * half
    for kind in range(2):
        stats[kind, pl.ds(low, half), :] = own_stats[kind]
        stats[kind, pl.ds(high, half), :] = their_stats[kind]
    sigmas = jnp.broadcast_to(sigma[...], (paths, factors_n))
    step = tile // paths

    def prepare(r):
        for at in range(r * step, (r + 1) * step):
            source, slot = (own, at) if at < slots else (theirs, at - slots)
            shape = (paths, factors_n)
            center = jnp.broadcast_to(stats[0, slot : slot + 1, :], shape)
            rstd = jnp.broadcast_to(stats[1, slot : slot + 1, :], shape)
            level = jnp.broadcast_to(levels[slot : slot + 1, :], shape)
            unit = ((source[slot].astype(F32) - center) * rstd).astype(BF16)
            scaled[at * paths : (at + 1) * paths, :] = unit
            factors[at * paths : (at + 1) * paths, :] = (
                level + sigmas * unit.astype(F32)
            ).astype(BF16)

    out[...] = cross_of(tile, scaled, factors, loadings, terms, prepare)


def next_kernel(tile, scaled, factors, loadings, terms, out):
    out[...] = cross_of(tile, scaled, factors, loadings, terms)


def cost_of(rows, count, factors_n):
    return pl.CostEstimate(
        flops=4 * rows * count * factors_n,
        bytes_accessed=4 * count * factors_n,
        transcendentals=0,
    )


def first_chunk(place, own, theirs, own_stats, their_stats, levels, sigma, ordered, terms):
    slots, paths, factors_n = own.shape
    rows = 2 * slots * paths
    count = ordered.shape[0]
    mixed = jax.ShapeDtypeStruct((rows, factors_n), BF16)
    return pl.pallas_call(
        functools.partial(first_kernel, paths * split_of(2 * slots, 512 // paths)),
        in_specs=[SMEM] + [VMEM] * 8,
        out_specs=[VMEM, VMEM, VMEM],
        out_shape=[mixed, mixed, jax.ShapeDtypeStruct((count, factors_n), F32)],
        scratch_shapes=[pltpu.VMEM((2, slots, factors_n), F32)],
        compiler_params=small(16),
        cost_estimate=cost_of(rows, count, factors_n),
        name="first_chunk",
    )(place, own, theirs, own_stats, their_stats, levels, sigma, ordered, terms)


def next_chunk(scaled, factors, ordered, terms):
    rows, factors_n = scaled.shape
    count = ordered.shape[0]
    return pl.pallas_call(
        functools.partial(next_kernel, split_of(rows, 512)),
        in_specs=[VMEM] * 4,
        out_specs=VMEM,
        out_shape=jax.ShapeDtypeStruct((count, factors_n), F32),
        compiler_params=small(16),
        cost_estimate=cost_of(rows, count, factors_n),
        name="next_chunk",
    )(scaled, factors, ordered, terms)


def body(normals, states, loadings, strikes, hedge, sigma, tail):
    groups = lax.axis_size("outer")
    inner = lax.axis_size("inner")
    chips = inner // 2
    group = lax.axis_index("outer")
    position = lax.axis_index("inner")
    chip, core = position // 2, position % 2
    node_count, per_node, factors_n = normals.shape
    instruments = loadings.shape[0]
    tail_count = tail.shape[0]
    paths = per_node * inner
    rows = instruments // (groups * inner)
    paired = chips & (chips - 1) == 0

    def partner(of, d):
        return of ^ d if paired else (of + d) % chips

    def beyond(of, s):
        return of ^ s if groups & (groups - 1) == 0 else (of + s) % groups

    def to_core(x):
        return lax.ppermute(x, "inner", [(i, i ^ 1) for i in range(inner)])

    def to_chip(x, d):
        return lax.ppermute(
            x, "inner", [(i, partner(i // 2, d) * 2 + i % 2) for i in range(inner)]
        )

    def to_group(x, s):
        return lax.ppermute(x, "outer", [(g, beyond(g, s)) for g in range(groups)])

    place = jnp.stack([group, core]).astype(jnp.int32)
    blocks = jnp.stack(
        [
            beyond(group, s) * inner + partner(chip, d) * 2 + core
            for d in range(chips)
            for s in range(groups)
        ]
    ).astype(jnp.int32)
    bound = 32768.0 / (tail_count * paths)
    unit = 1.0 / (bound * tail_count * paths)

    chosen, levels, mine, other, live = gather_nodes(
        place, *(pltpu.with_memory_space_constraint(x, pltpu.HBM) for x in (tail, normals, states))
    )
    theirs_sums = to_core(other)
    pair_sums = mine + theirs_sums
    chosen, pair_sums, blocks = lax.optimization_barrier((chosen, pair_sums, blocks))
    sums = [pair_sums] + [to_chip(pair_sums, d) for d in range(chips - 1, 0, -1)]
    theirs = to_core(chosen)
    gain, *parts = order(
        unit,
        bound,
        chips,
        groups,
        blocks,
        loadings.reshape(groups * inner, rows, factors_n),
        strikes.reshape(groups * inner, rows),
        hedge.reshape(groups * inner, rows),
    )
    sums, gain, parts = lax.optimization_barrier((sums, gain, parts))
    ordered = [part.reshape(groups * rows, factors_n) for part in parts[:chips]]
    terms = [part.reshape(3, groups * rows, 1) for part in parts[chips:]]
    stats = moments(paths, place, live, sums)
    their_stats = to_core(stats)

    arrived = []
    scaled = factors = kept = None
    for d in range(chips - 1, -1, -1):
        if scaled is None:
            scaled, factors, partial = first_chunk(
                place, chosen, theirs, stats, their_stats, levels,
                sigma.reshape(1, factors_n), ordered[d], terms[d],
            )
            early = scaled
        else:
            if d == 0 and arrived:
                arrived[0], early = lax.optimization_barrier((arrived[0], early))
            partial = next_chunk(early, factors, ordered[d], terms[d])
        if d:
            sent = partial.astype(F16)
            sent, early = lax.optimization_barrier((sent, early))
            arrived.append(to_chip(sent, d))
        else:
            kept = partial
    for k, item in enumerate(arrived):
        if k and k == len(arrived) - 1:
            kept = lax.optimization_barrier(kept)
        kept = kept + item.astype(F32)
    owned = kept[:rows]
    for s in sorted(range(1, groups), key=lambda s: (s & -s) == s and -s):
        owned = owned + to_group(kept[s * rows : (s + 1) * rows].astype(F16), s).astype(F32)
    return gain * owned


def solution(mesh):
    placed = (P("outer", "inner", None), P("outer", None), P(), P(), P(), P(), P())
    return jax.shard_map(
        body, mesh=mesh, in_specs=placed, out_specs=P(("outer", "inner"), None), check_vma=False
    )
```

```python
import functools

import jax
import jax.numpy as jnp
from jax import lax
from jax.experimental import pallas as pl
from jax.experimental.pallas import tpu as pltpu
from jax.sharding import PartitionSpec as P

CAP = 80
EPSILON = 1e-06
VMEM = pl.BlockSpec(memory_space=pltpu.VMEM)
SMEM = pl.BlockSpec(memory_space=pltpu.SMEM)
HBM = pl.BlockSpec(memory_space=pltpu.HBM)
F32 = jnp.float32
BF16 = jnp.bfloat16
F16 = jnp.float16


def split_of(count, most):
    for size in range(min(count, most), 0, -1):
        if count % size == 0:
            return size
    return 1


def small(mebibytes):
    return pltpu.CompilerParams(vmem_limit_bytes=mebibytes << 20)


def gather_kernel(
    part, place, tail_hbm, normals, chosen_hbm, mine, other, nodes,
    tail, chosen, tail_sem, sems, out_sem,
):
    node_count = normals.shape[0]
    tail_count = tail.shape[0]
    half = CAP // 2
    tail_copy = pltpu.make_async_copy(tail_hbm, tail, tail_sem)
    tail_copy.start()
    base = place[0] * node_count
    shift = place[1] * half
    tail_copy.wait()
    first = jnp.int32(0)
    for bit in range(tail_count.bit_length() - 1, -1, -1):
        ahead = first + (1 << bit)
        below = tail[jnp.minimum(ahead, tail_count) - 1] < base
        first = jnp.where((ahead <= tail_count) & below, ahead, first)
    parts = CAP // part

    @pl.loop(0, parts)
    def _(p):
        for k in range(part):
            slot = p * part + k
            at = slot + shift
            at = first + jnp.where(at >= CAP, at - CAP, at)
            node = tail[jnp.minimum(at, tail_count - 1)] - base
            node = jnp.minimum(jnp.maximum(node, 0), node_count - 1)
            nodes[slot] = node
            pltpu.make_async_copy(normals.at[node], chosen.at[slot], sems.at[p]).start()

    for begin, sums in ((0, mine), (parts // 2, other)):

        @pl.loop(0, parts // 2)
        def _(p):
            piece = chosen.at[pl.ds((begin + p) * part, part)]
            pltpu.make_async_copy(piece, piece, sems.at[begin + p]).wait()
            values = piece[...].astype(F32)
            rows = pl.ds(pl.multiple_of(p * part, part), part)
            sums[0, rows, :] = jnp.sum(values, axis=1)
            sums[1, rows, :] = jnp.sum(values * values, axis=1)

    out_copy = pltpu.make_async_copy(chosen, chosen_hbm, out_sem)
    out_copy.start()
    out_copy.wait()


def gather_nodes(place, tail, normals):
    _, paths, factors_n = normals.shape
    part = split_of(CAP // 2, 8)
    sums = jax.ShapeDtypeStruct((2, CAP // 2, factors_n), F32)
    chosen = (CAP, paths, factors_n)
    return pl.pallas_call(
        functools.partial(gather_kernel, part),
        in_specs=[SMEM, HBM, HBM],
        out_specs=[HBM, VMEM, VMEM, SMEM],
        out_shape=[
            jax.ShapeDtypeStruct(chosen, BF16),
            sums,
            sums,
            jax.ShapeDtypeStruct((CAP,), jnp.int32),
        ],
        scratch_shapes=[
            pltpu.SMEM(tail.shape, jnp.int32),
            pltpu.VMEM(chosen, BF16),
            pltpu.SemaphoreType.DMA,
            pltpu.SemaphoreType.DMA((CAP // part,)),
            pltpu.SemaphoreType.DMA,
        ],
        compiler_params=small(8),
        cost_estimate=pl.CostEstimate(flops=0, bytes_accessed=0, transcendentals=0),
        name="gather_nodes",
    )(place, tail, normals)


def to_message(sums, squares, count):
    within = squares - sums * sums / count
    high = sums.astype(F16)
    low = (sums - high.astype(F32)).astype(F16)
    return jnp.stack([high, low, within.astype(F16)]), within


def moments(sums, within, arrived, count, live):
    chips = [(sums, within)]
    for message in arrived:
        high, low, squares = message.astype(F32)
        chips.append((high + low, squares))
    center = sum(s for s, _ in chips) / (count * len(chips))
    spread = sum(w + (s / count - center) ** 2 * count for s, w in chips)
    spread = spread / (count * len(chips))
    return jnp.stack([center, jnp.where(live, lax.rsqrt(spread + EPSILON), 0.0)])


def order_kernel(
    unit, bound, blocks, nodes, states, loadings, strikes, hedge, levels, gain, *refs
):
    *outs, onehot = refs
    chunks, (steps, _, _) = len(outs) // 2, outs[0].shape
    lanes = lax.broadcasted_iota(jnp.int32, (1, states.shape[0]), 1)
    for slot in range(CAP):
        onehot[slot : slot + 1, :] = (lanes == nodes[slot]).astype(F32)
    levels[...] = jnp.dot(
        onehot[...].astype(BF16), states[...], preferred_element_type=F32
    )
    rows = loadings.shape[1]
    eye = lax.broadcasted_iota(jnp.int32, (rows, rows), 0) == lax.broadcasted_iota(
        jnp.int32, (rows, rows), 1
    )

    def column(ref, block):
        return jnp.sum(
            jnp.where(eye, ref[pl.ds(block, 1), :], 0.0), axis=1, keepdims=True
        )

    for chunk in range(chunks):
        ordered, terms = outs[chunk], outs[chunks + chunk]
        for step in range(steps):
            block = blocks[chunk * steps + step]
            own = loadings[block].astype(F32)
            ordered[step] = (own * 0.5).astype(BF16)
            size = column(hedge, block)
            scale = jnp.abs(size)
            if chunk == 0 and step == 0:
                gain[...] = own * (scale * unit)
            terms[0, step] = column(strikes, block) * 0.5
            terms[1, step] = size * 0.5
            terms[2, step] = jnp.where(
                scale > 1e-30, bound / jnp.maximum(scale, 1e-30), 0.0
            )


def order(unit, bound, chunks, steps, blocks, nodes, states, loadings, strikes, hedge):
    _, rows, factors_n = loadings.shape
    return pl.pallas_call(
        functools.partial(order_kernel, unit, bound),
        in_specs=[SMEM, SMEM] + [VMEM] * 4,
        out_specs=[VMEM] * (2 * chunks + 2),
        out_shape=[jax.ShapeDtypeStruct((count, factors_n), F32) for count in (CAP, rows)]
        + [jax.ShapeDtypeStruct((steps, rows, factors_n), BF16)] * chunks
        + [jax.ShapeDtypeStruct((3, steps, rows, 1), F32)] * chunks,
        scratch_shapes=[pltpu.VMEM((CAP, states.shape[0]), F32)],
        compiler_params=small(12),
        name="order_instruments",
    )(blocks, nodes, states, loadings, strikes, hedge)


def cross_of(tile, scaled, factors, loadings, terms, prepare=None):
    strikes, hedge, scale = terms[0], terms[1], terms[2]
    part = loadings[...]
    count = scaled.shape[0] // tile

    def level(r):
        if prepare is not None:
            prepare(r)
        rows = factors[r * tile : (r + 1) * tile, :]
        return lax.dot_general(
            part, rows, (((1,), (1,)), ((), ())), preferred_element_type=F32
        )

    total = None
    current = level(0)
    for r in range(count):
        after = level(r + 1) if r + 1 < count else None
        weight = (jnp.tanh(current - strikes) * hedge + hedge).astype(BF16)
        cross = jnp.dot(
            weight, scaled[r * tile : (r + 1) * tile, :], preferred_element_type=F32
        )
        total = cross if total is None else total + cross
        current = after
    return total * scale


def first_kernel(
    tile, own, theirs, own_stats, their_stats, levels, sigma,
    loadings, terms, scaled, factors, out,
):
    slots, paths, factors_n = own.shape
    half = slots // 2
    sigmas = jnp.broadcast_to(sigma[...], (paths, factors_n))
    step = tile // paths

    def prepare(r):
        for at in range(r * step, (r + 1) * step):
            mine, slot = at < slots, at % slots
            source = own if mine else theirs
            place = slot if mine else (slot + half) % slots
            stats = own_stats if mine == (slot < half) else their_stats
            row = slot % half
            shape = (paths, factors_n)
            center = jnp.broadcast_to(stats[0, row : row + 1, :], shape)
            rstd = jnp.broadcast_to(stats[1, row : row + 1, :], shape)
            level = jnp.broadcast_to(levels[place : place + 1, :], shape)
            unit = ((source[slot].astype(F32) - center) * rstd).astype(BF16)
            scaled[at * paths : (at + 1) * paths, :] = unit
            factors[at * paths : (at + 1) * paths, :] = (
                level + sigmas * unit.astype(F32)
            ).astype(BF16)

    out[...] = cross_of(tile, scaled, factors, loadings, terms, prepare)


def next_kernel(tile, scaled, factors, loadings, terms, out):
    out[...] = cross_of(tile, scaled, factors, loadings, terms)


def cost_of(rows, count, factors_n):
    return pl.CostEstimate(
        flops=4 * rows * count * factors_n,
        bytes_accessed=4 * count * factors_n,
        transcendentals=0,
    )


def first_chunk(own, theirs, own_stats, their_stats, levels, sigma, ordered, terms):
    slots, paths, factors_n = own.shape
    rows = 2 * slots * paths
    count = ordered.shape[0]
    mixed = jax.ShapeDtypeStruct((rows, factors_n), BF16)
    return pl.pallas_call(
        functools.partial(first_kernel, paths * split_of(2 * slots, 512 // paths)),
        in_specs=[VMEM] * 8,
        out_specs=[VMEM, VMEM, VMEM],
        out_shape=[mixed, mixed, jax.ShapeDtypeStruct((count, factors_n), F32)],
        compiler_params=small(16),
        cost_estimate=cost_of(rows, count, factors_n),
        name="first_chunk",
    )(own, theirs, own_stats, their_stats, levels, sigma, ordered, terms)


def next_chunk(scaled, factors, ordered, terms):
    rows, factors_n = scaled.shape
    count = ordered.shape[0]
    return pl.pallas_call(
        functools.partial(next_kernel, split_of(rows, 512)),
        in_specs=[VMEM] * 4,
        out_specs=VMEM,
        out_shape=jax.ShapeDtypeStruct((count, factors_n), F32),
        compiler_params=small(16),
        cost_estimate=cost_of(rows, count, factors_n),
        name="next_chunk",
    )(scaled, factors, ordered, terms)


def body(normals, states, loadings, strikes, hedge, sigma, tail):
    groups = lax.axis_size("outer")
    inner = lax.axis_size("inner")
    chips = inner // 2
    group = lax.axis_index("outer")
    position = lax.axis_index("inner")
    chip, core = position // 2, position % 2
    node_count, per_node, factors_n = normals.shape
    instruments = loadings.shape[0]
    tail_count = tail.shape[0]
    paths = per_node * inner
    rows = instruments // (groups * inner)
    paired = chips & (chips - 1) == 0

    def partner(of, d):
        return of ^ d if paired else (of + d) % chips

    def beyond(of, s):
        return of ^ s if groups & (groups - 1) == 0 else (of + s) % groups

    def to_core(x):
        return lax.ppermute(x, "inner", [(i, i ^ 1) for i in range(inner)])

    def to_chip(x, d):
        return lax.ppermute(
            x, "inner", [(i, partner(i // 2, d) * 2 + i % 2) for i in range(inner)]
        )

    def to_group(x, s):
        return lax.ppermute(x, "outer", [(g, beyond(g, s)) for g in range(groups)])

    place = jnp.stack([group, core]).astype(jnp.int32)
    blocks = jnp.stack(
        [
            beyond(group, s) * inner + partner(chip, d) * 2 + core
            for d in range(chips)
            for s in range(groups)
        ]
    ).astype(jnp.int32)
    bound = 32768.0 / (tail_count * paths)
    unit = 1.0 / (bound * tail_count * paths)

    tail_in, normals_in = (
        pltpu.with_memory_space_constraint(x, pltpu.HBM) for x in (tail, normals)
    )
    chosen, mine, other, nodes = gather_nodes(place, tail_in, normals_in)
    count = jnp.sum((tail // node_count == group).astype(jnp.int32))
    slots = core * (CAP // 2) + jnp.arange(CAP // 2, dtype=jnp.int32)
    live = (slots < count)[:, None]
    sums, squares = mine + to_core(other)
    message, within = to_message(sums, squares, 2 * per_node)
    chosen, message, blocks = lax.optimization_barrier((chosen, message, blocks))
    arrived = [to_chip(message, d) for d in range(chips - 1, 0, -1)]
    theirs = to_core(chosen)
    levels, gain, *parts = order(
        unit,
        bound,
        chips,
        groups,
        blocks,
        nodes,
        states,
        loadings.reshape(groups * inner, rows, factors_n),
        strikes.reshape(groups * inner, rows),
        hedge.reshape(groups * inner, rows),
    )
    arrived, theirs, levels, gain, parts = lax.optimization_barrier(
        (arrived, theirs, levels, gain, parts)
    )
    stats = moments(sums, within, arrived, 2 * per_node, live)
    their_stats = to_core(stats)
    ordered = [part.reshape(groups * rows, factors_n) for part in parts[:chips]]
    terms = [part.reshape(3, groups * rows, 1) for part in parts[chips:]]

    arrived = []
    scaled = factors = kept = None
    for d in range(chips - 1, -1, -1):
        if scaled is None:
            scaled, factors, partial = first_chunk(
                chosen, theirs, stats, their_stats, levels,
                sigma.reshape(1, factors_n), ordered[d], terms[d],
            )
            early = scaled
        else:
            if d == 0 and arrived:
                arrived[0], early = lax.optimization_barrier((arrived[0], early))
            partial = next_chunk(early, factors, ordered[d], terms[d])
        if d:
            sent = partial.astype(F16)
            sent, early = lax.optimization_barrier((sent, early))
            arrived.append(to_chip(sent, d))
        else:
            kept = partial
    for k, item in enumerate(arrived):
        if k and k == len(arrived) - 1:
            kept = lax.optimization_barrier(kept)
        kept = kept + item.astype(F32)
    owned = kept[:rows]
    for s in sorted(range(1, groups), key=lambda s: (s & -s) == s and -s):
        owned = owned + to_group(kept[s * rows : (s + 1) * rows].astype(F16), s).astype(F32)
    return gain * owned


def solution(mesh):
    placed = (P("outer", "inner", None), P("outer", None), P(), P(), P(), P(), P())
    return jax.shard_map(
        body, mesh=mesh, in_specs=placed, out_specs=P(("outer", "inner"), None), check_vma=False
    )
```

```python
import functools

import jax
import jax.numpy as jnp
from jax import lax
from jax.experimental import pallas as pl
from jax.experimental.pallas import tpu as pltpu
from jax.sharding import PartitionSpec as P

CAP = 80
EPSILON = 1e-06
VMEM = pl.BlockSpec(memory_space=pltpu.VMEM)
SMEM = pl.BlockSpec(memory_space=pltpu.SMEM)
HBM = pl.BlockSpec(memory_space=pltpu.HBM)
F32 = jnp.float32
BF16 = jnp.bfloat16
F16 = jnp.float16


def split_of(count, most):
    for size in range(min(count, most), 0, -1):
        if count % size == 0:
            return size
    return 1


def small(mebibytes):
    return pltpu.CompilerParams(vmem_limit_bytes=mebibytes << 20)


def gather_kernel(
    part, tail_hbm, normals, chosen_hbm, mine, other, nodes,
    tail, chosen, tail_sem, sems, out_sem,
):
    node_count = normals.shape[0]
    tail_count = tail.shape[0]
    half = CAP // 2
    tail_copy = pltpu.make_async_copy(tail_hbm, tail, tail_sem)
    tail_copy.start()
    base = lax.axis_index("outer") * node_count
    shift = lax.rem(lax.axis_index("inner"), 2) * half
    tail_copy.wait()
    first = jnp.int32(0)
    for bit in range(tail_count.bit_length() - 1, -1, -1):
        ahead = first + (1 << bit)
        below = tail[jnp.minimum(ahead, tail_count) - 1] < base
        first = jnp.where((ahead <= tail_count) & below, ahead, first)
    parts = CAP // part

    @pl.loop(0, parts)
    def _(p):
        for k in range(part):
            slot = p * part + k
            at = slot + shift
            at = first + jnp.where(at >= CAP, at - CAP, at)
            node = tail[jnp.minimum(at, tail_count - 1)] - base
            node = jnp.minimum(jnp.maximum(node, 0), node_count - 1)
            nodes[slot] = node
            pltpu.make_async_copy(normals.at[node], chosen.at[slot], sems.at[p]).start()

    out_copy = pltpu.make_async_copy(chosen, chosen_hbm, out_sem)
    for begin, sums in ((0, mine), (parts // 2, other)):

        @pl.loop(0, parts // 2)
        def _(p):
            piece = chosen.at[pl.ds((begin + p) * part, part)]
            pltpu.make_async_copy(piece, piece, sems.at[begin + p]).wait()
            there = chosen_hbm.at[pl.ds((begin + p) * part, part)]
            pltpu.make_async_copy(piece, there, out_sem).start()
            values = piece[...].astype(F32)
            rows = pl.ds(pl.multiple_of(p * part, part), part)
            sums[0, rows, :] = jnp.sum(values, axis=1)
            sums[1, rows, :] = jnp.sum(values * values, axis=1)

    out_copy.wait()


def gather_nodes(tail, normals):
    _, paths, factors_n = normals.shape
    part = split_of(CAP // 2, 8)
    sums = jax.ShapeDtypeStruct((2, CAP // 2, factors_n), F32)
    chosen = (CAP, paths, factors_n)
    return pl.pallas_call(
        functools.partial(gather_kernel, part),
        in_specs=[HBM, HBM],
        out_specs=[HBM, VMEM, VMEM, SMEM],
        out_shape=[
            pltpu.HBM(chosen, BF16),
            sums,
            sums,
            jax.ShapeDtypeStruct((CAP,), jnp.int32),
        ],
        scratch_shapes=[
            pltpu.SMEM(tail.shape, jnp.int32),
            pltpu.VMEM(chosen, BF16),
            pltpu.SemaphoreType.DMA,
            pltpu.SemaphoreType.DMA((CAP // part,)),
            pltpu.SemaphoreType.DMA,
        ],
        compiler_params=small(8),
        cost_estimate=pl.CostEstimate(flops=0, bytes_accessed=0, transcendentals=0),
        name="gather_nodes",
    )(tail, normals)


def to_message(sums, squares, count):
    within = squares - sums * sums / count
    high = sums.astype(F16)
    low = (sums - high.astype(F32)).astype(F16)
    return jnp.stack([high, low, within.astype(F16)]), within


def moments(sums, within, arrived, count, live):
    chips = [(sums, within)]
    for message in arrived:
        high, low, squares = message.astype(F32)
        chips.append((high + low, squares))
    center = sum(s for s, _ in chips) / (count * len(chips))
    spread = sum(w + (s / count - center) ** 2 * count for s, w in chips)
    spread = spread / (count * len(chips))
    return jnp.stack([center, jnp.where(live, lax.rsqrt(spread + EPSILON), 0.0)])


def order_kernel(
    unit, bound, blocks, nodes, states, loadings, strikes, hedge, levels, gain, *refs
):
    *outs, onehot = refs
    chunks, (steps, _, _) = len(outs) // 2, outs[0].shape
    lanes = lax.broadcasted_iota(jnp.int32, (1, states.shape[0]), 1)
    for slot in range(CAP):
        onehot[slot : slot + 1, :] = (lanes == nodes[slot]).astype(F32)
    levels[...] = jnp.dot(
        onehot[...].astype(BF16), states[...], preferred_element_type=F32
    )
    rows = loadings.shape[1]
    eye = lax.broadcasted_iota(jnp.int32, (rows, rows), 0) == lax.broadcasted_iota(
        jnp.int32, (rows, rows), 1
    )

    def column(ref, block):
        return jnp.sum(
            jnp.where(eye, ref[pl.ds(block, 1), :], 0.0), axis=1, keepdims=True
        )

    for chunk in range(chunks):
        ordered, terms = outs[chunk], outs[chunks + chunk]
        for step in range(steps):
            block = blocks[chunk * steps + step]
            own = loadings[block].astype(F32)
            ordered[step] = (own * 0.5).astype(BF16)
            size = column(hedge, block)
            scale = jnp.abs(size)
            if chunk == 0 and step == 0:
                gain[...] = own * (scale * unit)
            terms[0, step] = column(strikes, block) * 0.5
            terms[1, step] = size * 0.5
            terms[2, step] = jnp.where(
                scale > 1e-30, bound / jnp.maximum(scale, 1e-30), 0.0
            )


def order(unit, bound, chunks, steps, blocks, nodes, states, loadings, strikes, hedge):
    _, rows, factors_n = loadings.shape
    return pl.pallas_call(
        functools.partial(order_kernel, unit, bound),
        in_specs=[SMEM, SMEM] + [VMEM] * 4,
        out_specs=[VMEM] * (2 * chunks + 2),
        out_shape=[jax.ShapeDtypeStruct((count, factors_n), F32) for count in (CAP, rows)]
        + [jax.ShapeDtypeStruct((steps, rows, factors_n), BF16)] * chunks
        + [jax.ShapeDtypeStruct((3, steps, rows, 1), F32)] * chunks,
        scratch_shapes=[pltpu.VMEM((CAP, states.shape[0]), F32)],
        compiler_params=small(12),
        name="order_instruments",
    )(blocks, nodes, states, loadings, strikes, hedge)


def prepare(own, theirs, stats, levels, sigma, scaled, factors, ready, begin, end):
    slots, paths, factors_n = own.shape
    half = slots // 2
    shape = (paths, factors_n)
    sigmas = jnp.broadcast_to(sigma[...], shape)
    for at in range(begin, end):
        mine, row = at < half, at % half
        slot = row if mine == ready else row + half
        source = own if mine else theirs
        place = slot if mine else (slot + half) % slots
        center = jnp.broadcast_to(stats[0, row : row + 1, :], shape)
        rstd = jnp.broadcast_to(stats[1, row : row + 1, :], shape)
        level = jnp.broadcast_to(levels[place : place + 1, :], shape)
        unit = ((source[slot].astype(F32) - center) * rstd).astype(BF16)
        rows = slice(at * paths, (at + 1) * paths)
        scaled[rows, :] = unit
        factors[rows, :] = (level + sigmas * unit.astype(F32)).astype(BF16)


def ready_kernel(own, theirs, stats, levels, sigma, scaled, factors):
    prepare(own, theirs, stats, levels, sigma, scaled, factors, True, 0, own.shape[0])


def ready_rows(own, theirs, stats, levels, sigma):
    slots, paths, factors_n = own.shape
    half = jax.ShapeDtypeStruct((slots * paths, factors_n), BF16)
    return pl.pallas_call(
        ready_kernel,
        in_specs=[VMEM] * 5,
        out_specs=[VMEM] * 2,
        out_shape=[half] * 2,
        compiler_params=small(12),
        cost_estimate=pl.CostEstimate(
            flops=8 * slots * paths * factors_n,
            bytes_accessed=8 * slots * paths * factors_n,
            transcendentals=0,
        ),
        name="ready_rows",
    )(own, theirs, stats, levels, sigma)


def cross_of(tile, halves, loadings, terms, before=None):
    strikes, hedge, scale = terms[0], terms[1], terms[2]
    part = loadings[...]
    each = halves[0][0].shape[0] // tile
    places = [(half, r * tile) for half in (0, 1) for r in range(each)]

    def level(half, at):
        if before is not None and half == 1:
            before(at // tile)
        rows = halves[half][1][at : at + tile, :]
        return lax.dot_general(
            part, rows, (((1,), (1,)), ((), ())), preferred_element_type=F32
        )

    total = None
    current = level(*places[0])
    for k, (half, at) in enumerate(places):
        after = level(*places[k + 1]) if k + 1 < len(places) else None
        weight = (jnp.tanh(current - strikes) * hedge + hedge).astype(BF16)
        cross = jnp.dot(
            weight, halves[half][0][at : at + tile, :], preferred_element_type=F32
        )
        total = cross if total is None else total + cross
        current = after
    return total * scale


def first_kernel(
    tile, own, theirs, stats, levels, sigma, ready_scaled, ready_factors,
    loadings, terms, scaled, factors, out,
):
    step = tile // own.shape[1]

    def before(r):
        prepare(
            own, theirs, stats, levels, sigma, scaled, factors, False,
            r * step, (r + 1) * step,
        )

    halves = ((ready_scaled, ready_factors), (scaled, factors))
    out[...] = cross_of(tile, halves, loadings, terms, before)


def next_kernel(tile, s0, f0, s1, f1, loadings, terms, out):
    out[...] = cross_of(tile, ((s0, f0), (s1, f1)), loadings, terms)


def cost_of(rows, count, factors_n):
    return pl.CostEstimate(
        flops=4 * rows * count * factors_n,
        bytes_accessed=4 * count * factors_n,
        transcendentals=0,
    )


def tile_of(slots, paths):
    return paths * split_of(slots, max(1, 640 // paths))


def first_chunk(own, theirs, stats, levels, sigma, ready, ordered, terms):
    slots, paths, factors_n = own.shape
    count = ordered.shape[0]
    half = jax.ShapeDtypeStruct((slots * paths, factors_n), BF16)
    return pl.pallas_call(
        functools.partial(first_kernel, tile_of(slots, paths)),
        in_specs=[VMEM] * 9,
        out_specs=[VMEM] * 3,
        out_shape=[half, half, jax.ShapeDtypeStruct((count, factors_n), F32)],
        compiler_params=small(16),
        cost_estimate=cost_of(2 * slots * paths, count, factors_n),
        name="first_chunk",
    )(own, theirs, stats, levels, sigma, *ready, ordered, terms)


def next_chunk(tile, ready, rest, ordered, terms):
    rows, factors_n = ready[0].shape
    count = ordered.shape[0]
    return pl.pallas_call(
        functools.partial(next_kernel, tile),
        in_specs=[VMEM] * 6,
        out_specs=VMEM,
        out_shape=jax.ShapeDtypeStruct((count, factors_n), F32),
        compiler_params=small(16),
        cost_estimate=cost_of(2 * rows, count, factors_n),
        name="next_chunk",
    )(*ready, *rest, ordered, terms)


def body(normals, states, loadings, strikes, hedge, sigma, tail):
    groups = lax.axis_size("outer")
    inner = lax.axis_size("inner")
    chips = inner // 2
    group = lax.axis_index("outer")
    position = lax.axis_index("inner")
    chip, core = position // 2, position % 2
    node_count, per_node, factors_n = normals.shape
    instruments = loadings.shape[0]
    tail_count = tail.shape[0]
    paths = per_node * inner
    rows = instruments // (groups * inner)
    paired = chips & (chips - 1) == 0

    def partner(of, d):
        return of ^ d if paired else (of + d) % chips

    def beyond(of, s):
        return of ^ s if groups & (groups - 1) == 0 else (of + s) % groups

    def to_core(x):
        return lax.ppermute(x, "inner", [(i, i ^ 1) for i in range(inner)])

    def to_chip(x, d):
        return lax.ppermute(
            x, "inner", [(i, partner(i // 2, d) * 2 + i % 2) for i in range(inner)]
        )

    def to_group(x, s):
        return lax.ppermute(x, "outer", [(g, beyond(g, s)) for g in range(groups)])

    blocks = jnp.stack(
        [
            beyond(group, s) * inner + partner(chip, d) * 2 + core
            for d in range(chips)
            for s in range(groups)
        ]
    ).astype(jnp.int32)
    bound = 32768.0 / (tail_count * paths)
    unit = 1.0 / (bound * tail_count * paths)

    tail_in, normals_in = (
        pltpu.with_memory_space_constraint(x, pltpu.HBM) for x in (tail, normals)
    )
    chosen, mine, other, nodes = gather_nodes(tail_in, normals_in)
    count = jnp.sum((tail // node_count == group).astype(jnp.int32))
    slots = core * (CAP // 2) + jnp.arange(CAP // 2, dtype=jnp.int32)
    live = (slots < count)[:, None]
    sums, squares = mine + to_core(other)
    message, within = to_message(sums, squares, 2 * per_node)
    chosen, message, blocks = lax.optimization_barrier((chosen, message, blocks))
    arrived = [to_chip(message, d) for d in range(chips - 1, 0, -1)]
    theirs = to_core(chosen)
    levels, gain, *parts = order(
        unit,
        bound,
        chips,
        groups,
        blocks,
        nodes,
        states,
        loadings.reshape(groups * inner, rows, factors_n),
        strikes.reshape(groups * inner, rows),
        hedge.reshape(groups * inner, rows),
    )
    arrived, theirs, levels, gain, parts = lax.optimization_barrier(
        (arrived, theirs, levels, gain, parts)
    )
    stats = moments(sums, within, arrived, 2 * per_node, live)
    their_stats = to_core(stats)
    ordered = [part.reshape(groups * rows, factors_n) for part in parts[:chips]]
    terms = [part.reshape(3, groups * rows, 1) for part in parts[chips:]]

    sigmas = sigma.reshape(1, factors_n)
    ready = ready_rows(chosen, theirs, stats, levels, sigmas)

    arrived = []
    rest = kept = None
    for d in range(chips - 1, -1, -1):
        if rest is None:
            *rest, partial = first_chunk(
                chosen, theirs, their_stats, levels, sigmas, ready, ordered[d], terms[d]
            )
        else:
            if d == 0 and arrived:
                arrived[0], rest = lax.optimization_barrier((arrived[0], rest))
            partial = next_chunk(tile_of(CAP, per_node), ready, rest, ordered[d], terms[d])
        if d:
            sent = partial.astype(F16)
            sent, rest = lax.optimization_barrier((sent, rest))
            arrived.append(to_chip(sent, d))
        else:
            kept = partial
    for k, item in enumerate(arrived):
        if k and k == len(arrived) - 1:
            kept = lax.optimization_barrier(kept)
        kept = kept + item.astype(F32)
    owned = kept[:rows]
    for s in sorted(range(1, groups), key=lambda s: (s & -s) == s and -s):
        owned = owned + to_group(kept[s * rows : (s + 1) * rows].astype(F16), s).astype(F32)
    return gain * owned


def solution(mesh):
    placed = (P("outer", "inner", None), P("outer", None), P(), P(), P(), P(), P())
    return jax.shard_map(
        body, mesh=mesh, in_specs=placed, out_specs=P(("outer", "inner"), None), check_vma=False
    )
```

```python
import functools

import jax
import jax.numpy as jnp
from jax import lax
from jax.experimental import pallas as pl
from jax.experimental.pallas import tpu as pltpu
from jax.sharding import PartitionSpec as P

CAP = 80
EPSILON = 1e-06
VMEM = pl.BlockSpec(memory_space=pltpu.VMEM)
SMEM = pl.BlockSpec(memory_space=pltpu.SMEM)
HBM = pl.BlockSpec(memory_space=pltpu.HBM)
F32 = jnp.float32
BF16 = jnp.bfloat16
F16 = jnp.float16


def split_of(count, most):
    for size in range(min(count, most), 0, -1):
        if count % size == 0:
            return size
    return 1


def small(mebibytes):
    return pltpu.CompilerParams(vmem_limit_bytes=mebibytes << 20)


def first_of(tail, base):
    count = tail.shape[0]
    first = jnp.int32(0)
    for bit in range(count.bit_length() - 1, -1, -1):
        ahead = first + (1 << bit)
        below = tail[jnp.minimum(ahead, count) - 1] < base
        first = jnp.where((ahead <= count) & below, ahead, first)
    return first


def place_of(tail, first, base, slot):
    at = slot + lax.rem(lax.axis_index("inner"), 2) * (CAP // 2)
    at = first + jnp.where(at >= CAP, at - CAP, at)
    node = tail[jnp.minimum(at, tail.shape[0] - 1)] - base
    return node, at < tail.shape[0]


def gather_kernel(
    part, tail_hbm, normals, chosen_hbm, mine, other,
    tail, chosen, tail_sem, sems, out_sem,
):
    node_count = normals.shape[0]
    tail_copy = pltpu.make_async_copy(tail_hbm, tail, tail_sem)
    tail_copy.start()
    base = lax.axis_index("outer") * node_count
    tail_copy.wait()
    first = first_of(tail, base)
    parts = CAP // part

    @pl.loop(0, parts)
    def _(p):
        for k in range(part):
            slot = p * part + k
            node, _ = place_of(tail, first, base, slot)
            node = jnp.minimum(jnp.maximum(node, 0), node_count - 1)
            pltpu.make_async_copy(normals.at[node], chosen.at[slot], sems.at[p]).start()

    out_copy = pltpu.make_async_copy(chosen, chosen_hbm, out_sem)
    for begin, sums in ((0, mine), (parts // 2, other)):

        @pl.loop(0, parts // 2)
        def _(p):
            piece = chosen.at[pl.ds((begin + p) * part, part)]
            pltpu.make_async_copy(piece, piece, sems.at[begin + p]).wait()
            there = chosen_hbm.at[pl.ds((begin + p) * part, part)]
            pltpu.make_async_copy(piece, there, out_sem).start()
            values = piece[...].astype(F32)
            rows = pl.ds(pl.multiple_of(p * part, part), part)
            sums[0, rows, :] = jnp.sum(values, axis=1)
            sums[1, rows, :] = jnp.sum(values * values, axis=1)

    out_copy.wait()


def gather_nodes(tail, normals):
    _, paths, factors_n = normals.shape
    part = split_of(CAP // 2, 8)
    sums = jax.ShapeDtypeStruct((2, CAP // 2, factors_n), F32)
    chosen = (CAP, paths, factors_n)
    return pl.pallas_call(
        functools.partial(gather_kernel, part),
        in_specs=[HBM, HBM],
        out_specs=[HBM, VMEM, VMEM],
        out_shape=[
            pltpu.HBM(chosen, BF16),
            sums,
            sums,
        ],
        scratch_shapes=[
            pltpu.SMEM(tail.shape, jnp.int32),
            pltpu.VMEM(chosen, BF16),
            pltpu.SemaphoreType.DMA,
            pltpu.SemaphoreType.DMA((CAP // part,)),
            pltpu.SemaphoreType.DMA,
        ],
        compiler_params=small(8),
        cost_estimate=pl.CostEstimate(flops=0, bytes_accessed=0, transcendentals=0),
        name="gather_nodes",
    )(tail, normals)


def to_message(sums, squares, count):
    within = squares - sums * sums / count
    high = sums.astype(F16)
    low = (sums - high.astype(F32)).astype(F16)
    return jnp.stack([high, low, within.astype(F16)]), within


def moments(sums, within, arrived, count, live):
    chips = [(sums, within)]
    for message in arrived:
        high, low, squares = message.astype(F32)
        chips.append((high + low, squares))
    center = sum(s for s, _ in chips) / (count * len(chips))
    spread = sum(w + (s / count - center) ** 2 * count for s, w in chips)
    spread = spread / (count * len(chips))
    return jnp.stack([center, live * lax.rsqrt(spread + EPSILON)])


def order_kernel(
    unit, bound, shape, far, tail_hbm, states_hbm, loadings_hbm, strikes, hedge,
    levels, live, gain, *refs,
):
    chunks, steps, rows = shape
    ordered, terms = refs[:chunks], refs[chunks : 2 * chunks]
    tail, states, onehot, own, tail_sem, states_sem, sems = refs[2 * chunks :]
    node_count = states.shape[0]
    position = lax.axis_index("inner")
    group, chip, core = lax.axis_index("outer"), position // 2, lax.rem(position, 2)
    tail_copy = pltpu.make_async_copy(tail_hbm, tail, tail_sem)
    states_copy = pltpu.make_async_copy(states_hbm, states, states_sem)
    tail_copy.start()
    states_copy.start()
    blocks, copies = [], []
    for chunk in range(chunks):
        for step in range(steps):
            to_chip, to_group = far(chip, chunk, group, step)
            block = (to_group * chunks + to_chip) * 2 + core
            k = chunk * steps + step
            copy = pltpu.make_async_copy(loadings_hbm.at[block], own.at[k], sems.at[k])
            copy.start()
            blocks.append(block)
            copies.append(copy)
    wide = strikes.shape[1]
    lanes = lax.broadcasted_iota(jnp.int32, (rows, wide), 1)
    lines = lax.broadcasted_iota(jnp.int32, (rows, wide), 0)

    def column(ref, block):
        line = ref[pl.ds(block * rows // wide, 1), :]
        here = lanes == lines + lax.rem(block * rows, wide)
        return jnp.sum(jnp.where(here, line, 0.0), axis=1, keepdims=True)

    for k, block in enumerate(blocks):
        chunk, step = k // steps, k % steps
        at = slice(step * rows, (step + 1) * rows)
        size = column(hedge, block)
        scale = jnp.abs(size)
        terms[chunk][at, 0:1] = column(strikes, block) * 0.5
        terms[chunk][at, 1:2] = size * 0.5
        terms[chunk][at, 2:3] = jnp.where(
            scale > 1e-30, bound / jnp.maximum(scale, 1e-30), 0.0
        )
        if k == 0:
            owned = scale * unit
    tail_copy.wait()
    base = group * node_count
    first = first_of(tail, base)
    nodes = lax.broadcasted_iota(jnp.int32, (1, node_count), 1)
    for slot in range(CAP):
        node, inside = place_of(tail, first, base, slot)
        used = inside & (node >= 0) & (node < node_count)
        onehot[slot : slot + 1, :] = ((nodes == node) & used).astype(F32)
        if slot < CAP // 2:
            live[slot : slot + 1, :] = jnp.full((1, live.shape[1]), used.astype(F32))
    states_copy.wait()
    levels[...] = jnp.dot(
        onehot[...].astype(BF16), states[...], preferred_element_type=F32
    )
    for k, copy in enumerate(copies):
        copy.wait()
        values = own[k].astype(F32)
        if k == 0:
            gain[...] = values * owned
        ordered[k // steps][k % steps] = (values * 0.5).astype(BF16)


def order(unit, bound, shape, far, tail, states, loadings, strikes, hedge):
    chunks, steps, rows = shape
    factors_n = states.shape[1]
    return pl.pallas_call(
        functools.partial(order_kernel, unit, bound, shape, far),
        in_specs=[HBM] * 3 + [VMEM] * 2,
        out_specs=[VMEM] * (2 * chunks + 3),
        out_shape=[
            jax.ShapeDtypeStruct((count, factors_n), F32) for count in (CAP, CAP // 2, rows)
        ]
        + [jax.ShapeDtypeStruct((steps, rows, factors_n), BF16)] * chunks
        + [jax.ShapeDtypeStruct((steps * rows, 3), F32)] * chunks,
        scratch_shapes=[
            pltpu.SMEM(tail.shape, jnp.int32),
            pltpu.VMEM(states.shape, BF16),
            pltpu.VMEM((CAP, states.shape[0]), F32),
            pltpu.VMEM((chunks * steps, rows, factors_n), BF16),
            pltpu.SemaphoreType.DMA,
            pltpu.SemaphoreType.DMA,
            pltpu.SemaphoreType.DMA((chunks * steps,)),
        ],
        compiler_params=small(12),
        cost_estimate=pl.CostEstimate(flops=0, bytes_accessed=1 << 20, transcendentals=0),
        name="order_instruments",
    )(tail, states, loadings, strikes, hedge)


def prepare(own, theirs, stats, levels, sigma, scaled, factors, ready, begin, end):
    slots, paths, factors_n = own.shape
    half = slots // 2
    shape = (paths, factors_n)
    sigmas = jnp.broadcast_to(sigma[...], shape)
    for at in range(begin, end):
        mine, row = at < half, at % half
        slot = row if mine == ready else row + half
        source = own if mine else theirs
        place = slot if mine else (slot + half) % slots
        center = jnp.broadcast_to(stats[0, row : row + 1, :], shape)
        rstd = jnp.broadcast_to(stats[1, row : row + 1, :], shape)
        level = jnp.broadcast_to(levels[place : place + 1, :], shape)
        unit = ((source[slot].astype(F32) - center) * rstd).astype(BF16)
        rows = slice(at * paths, (at + 1) * paths)
        scaled[rows, :] = unit
        factors[rows, :] = (level + sigmas * unit.astype(F32)).astype(BF16)


def ready_kernel(own, theirs, stats, levels, sigma, scaled, factors):
    prepare(own, theirs, stats, levels, sigma, scaled, factors, True, 0, own.shape[0])


def ready_rows(own, theirs, stats, levels, sigma):
    slots, paths, factors_n = own.shape
    half = jax.ShapeDtypeStruct((slots * paths, factors_n), BF16)
    return pl.pallas_call(
        ready_kernel,
        in_specs=[VMEM] * 5,
        out_specs=[VMEM] * 2,
        out_shape=[half] * 2,
        compiler_params=small(12),
        cost_estimate=pl.CostEstimate(
            flops=8 * slots * paths * factors_n,
            bytes_accessed=8 * slots * paths * factors_n,
            transcendentals=0,
        ),
        name="ready_rows",
    )(own, theirs, stats, levels, sigma)


def cross_of(tile, halves, loadings, terms, before=None):
    strikes, hedge, scale = terms[:, 0:1], terms[:, 1:2], terms[:, 2:3]
    part = loadings[...]
    each = halves[0][0].shape[0] // tile
    places = [(half, r * tile) for half in (0, 1) for r in range(each)]

    def level(half, at):
        if before is not None and half == 1:
            before(at // tile)
        rows = halves[half][1][at : at + tile, :]
        return lax.dot_general(
            part, rows, (((1,), (1,)), ((), ())), preferred_element_type=F32
        )

    total = None
    current = level(*places[0])
    for k, (half, at) in enumerate(places):
        after = level(*places[k + 1]) if k + 1 < len(places) else None
        weight = (jnp.tanh(current - strikes) * hedge + hedge).astype(BF16)
        cross = jnp.dot(
            weight, halves[half][0][at : at + tile, :], preferred_element_type=F32
        )
        total = cross if total is None else total + cross
        current = after
    return total * scale


def first_kernel(
    tile, own, theirs, stats, levels, sigma, ready_scaled, ready_factors,
    loadings, terms, scaled, factors, out,
):
    step = tile // own.shape[1]

    def before(r):
        prepare(
            own, theirs, stats, levels, sigma, scaled, factors, False,
            r * step, (r + 1) * step,
        )

    halves = ((ready_scaled, ready_factors), (scaled, factors))
    out[...] = cross_of(tile, halves, loadings, terms, before)


def next_kernel(tile, s0, f0, s1, f1, loadings, terms, out):
    out[...] = cross_of(tile, ((s0, f0), (s1, f1)), loadings, terms)


def cost_of(rows, count, factors_n):
    return pl.CostEstimate(
        flops=4 * rows * count * factors_n,
        bytes_accessed=4 * count * factors_n,
        transcendentals=0,
    )


def tile_of(slots, paths):
    return paths * split_of(slots, max(1, 1280 // paths))


def first_chunk(own, theirs, stats, levels, sigma, ready, ordered, terms):
    slots, paths, factors_n = own.shape
    count = ordered.shape[0]
    half = jax.ShapeDtypeStruct((slots * paths, factors_n), BF16)
    return pl.pallas_call(
        functools.partial(first_kernel, tile_of(slots, paths)),
        in_specs=[VMEM] * 9,
        out_specs=[VMEM] * 3,
        out_shape=[half, half, jax.ShapeDtypeStruct((count, factors_n), F32)],
        compiler_params=small(16),
        cost_estimate=cost_of(2 * slots * paths, count, factors_n),
        name="first_chunk",
    )(own, theirs, stats, levels, sigma, *ready, ordered, terms)


def next_chunk(tile, ready, rest, ordered, terms):
    rows, factors_n = ready[0].shape
    count = ordered.shape[0]
    return pl.pallas_call(
        functools.partial(next_kernel, tile),
        in_specs=[VMEM] * 6,
        out_specs=VMEM,
        out_shape=jax.ShapeDtypeStruct((count, factors_n), F32),
        compiler_params=small(16),
        cost_estimate=cost_of(2 * rows, count, factors_n),
        name="next_chunk",
    )(*ready, *rest, ordered, terms)


def body(normals, states, loadings, strikes, hedge, sigma, tail):
    groups = lax.axis_size("outer")
    inner = lax.axis_size("inner")
    chips = inner // 2
    _, per_node, factors_n = normals.shape
    instruments = loadings.shape[0]
    tail_count = tail.shape[0]
    paths = per_node * inner
    rows = instruments // (groups * inner)
    paired = chips & (chips - 1) == 0

    def partner(of, d):
        return of ^ d if paired else (of + d) % chips

    def beyond(of, s):
        return of ^ s if groups & (groups - 1) == 0 else (of + s) % groups

    def to_core(x):
        return lax.ppermute(x, "inner", [(i, i ^ 1) for i in range(inner)])

    def to_chip(x, d):
        return lax.ppermute(
            x, "inner", [(i, partner(i // 2, d) * 2 + i % 2) for i in range(inner)]
        )

    def to_group(x, s):
        return lax.ppermute(x, "outer", [(g, beyond(g, s)) for g in range(groups)])

    bound = 32768.0 / (tail_count * paths)
    unit = 1.0 / (bound * tail_count * paths)

    tail, normals, states, loadings = (
        pltpu.with_memory_space_constraint(x, pltpu.HBM)
        for x in (tail, normals, states, loadings.reshape(groups * inner, rows, factors_n))
    )
    wide = 128 if 128 % rows == 0 else rows
    strikes, hedge = strikes.reshape(-1, wide), hedge.reshape(-1, wide)

    chosen, mine, other = gather_nodes(tail, normals)
    sums, squares = mine + to_core(other)
    message, within = to_message(sums, squares, 2 * per_node)
    chosen, message, strikes = lax.optimization_barrier((chosen, message, strikes))
    arrived = [to_chip(message, d) for d in range(chips - 1, 0, -1)]
    theirs = to_core(chosen)
    far = lambda chip, d, group, s: (partner(chip, d), beyond(group, s))
    levels, live, gain, *parts = order(
        unit, bound, (chips, groups, rows), far, tail, states, loadings, strikes, hedge
    )
    ordered = [part.reshape(groups * rows, factors_n) for part in parts[:chips]]
    terms = parts[chips:]
    arrived, theirs, levels, live, gain, ordered, terms = lax.optimization_barrier(
        (arrived, theirs, levels, live, gain, ordered, terms)
    )
    stats = moments(sums, within, arrived, 2 * per_node, live)
    their_stats = to_core(stats)

    sigmas = sigma.reshape(1, factors_n)
    ready = ready_rows(chosen, theirs, stats, levels, sigmas)

    arrived = []
    rest = kept = None
    for d in range(chips - 1, -1, -1):
        if rest is None:
            *rest, partial = first_chunk(
                chosen, theirs, their_stats, levels, sigmas, ready, ordered[d], terms[d]
            )
        else:
            if d == 0 and arrived:
                arrived[0], rest = lax.optimization_barrier((arrived[0], rest))
            partial = next_chunk(tile_of(CAP, per_node), ready, rest, ordered[d], terms[d])
        if d:
            sent = partial.astype(F16)
            sent, rest = lax.optimization_barrier((sent, rest))
            arrived.append(to_chip(sent, d))
        else:
            kept = partial
    for k, item in enumerate(arrived):
        if k and k == len(arrived) - 1:
            kept = lax.optimization_barrier(kept)
        kept = kept + item.astype(F32)
    owned = kept[:rows]
    for s in sorted(range(1, groups), key=lambda s: (s & -s) == s and -s):
        owned = owned + to_group(kept[s * rows : (s + 1) * rows].astype(F16), s).astype(F32)
    return gain * owned


def solution(mesh):
    placed = (P("outer", "inner", None), P("outer", None), P(), P(), P(), P(), P())
    return jax.shard_map(
        body, mesh=mesh, in_specs=placed, out_specs=P(("outer", "inner"), None), check_vma=False
    )
```

```python
import functools

import jax
import jax.numpy as jnp
from jax import lax
from jax.experimental import pallas as pl
from jax.experimental.pallas import tpu as pltpu
from jax.sharding import PartitionSpec as P

CAP = 80
EPSILON = 1e-06
VMEM = pl.BlockSpec(memory_space=pltpu.VMEM)
SMEM = pl.BlockSpec(memory_space=pltpu.SMEM)
HBM = pl.BlockSpec(memory_space=pltpu.HBM)
F32 = jnp.float32
BF16 = jnp.bfloat16
F16 = jnp.float16


def split_of(count, most):
    for size in range(min(count, most), 0, -1):
        if count % size == 0:
            return size
    return 1


def small(mebibytes):
    return pltpu.CompilerParams(vmem_limit_bytes=mebibytes << 20)


def first_of(tail, base):
    count = tail.shape[0]
    first = jnp.int32(0)
    for bit in range(count.bit_length() - 1, -1, -1):
        ahead = first + (1 << bit)
        below = tail[jnp.minimum(ahead, count) - 1] < base
        first = jnp.where((ahead <= count) & below, ahead, first)
    return first


def place_of(tail, first, base, slot):
    at = slot + lax.rem(lax.axis_index("inner"), 2) * (CAP // 2)
    at = first + jnp.where(at >= CAP, at - CAP, at)
    node = tail[jnp.minimum(at, tail.shape[0] - 1)] - base
    return node, at < tail.shape[0]


def gather_kernel(
    part, tail_hbm, normals, chosen_hbm, mine, other,
    tail, chosen, tail_sem, sems, out_sem,
):
    node_count = normals.shape[0]
    tail_copy = pltpu.make_async_copy(tail_hbm, tail, tail_sem)
    tail_copy.start()
    base = lax.axis_index("outer") * node_count
    tail_copy.wait()
    first = first_of(tail, base)
    parts = CAP // part

    @pl.loop(0, parts)
    def _(p):
        for k in range(part):
            slot = p * part + k
            node, _ = place_of(tail, first, base, slot)
            node = jnp.minimum(jnp.maximum(node, 0), node_count - 1)
            pltpu.make_async_copy(normals.at[node], chosen.at[slot], sems.at[p]).start()

    out_copy = pltpu.make_async_copy(chosen, chosen_hbm, out_sem)
    for begin, sums in ((0, mine), (parts // 2, other)):

        @pl.loop(0, parts // 2)
        def _(p):
            piece = chosen.at[pl.ds((begin + p) * part, part)]
            pltpu.make_async_copy(piece, piece, sems.at[begin + p]).wait()
            there = chosen_hbm.at[pl.ds((begin + p) * part, part)]
            pltpu.make_async_copy(piece, there, out_sem).start()
            values = piece[...].astype(F32)
            rows = pl.ds(pl.multiple_of(p * part, part), part)
            sums[0, rows, :] = jnp.sum(values, axis=1)
            sums[1, rows, :] = jnp.sum(values * values, axis=1)

    out_copy.wait()


def gather_nodes(tail, normals):
    _, paths, factors_n = normals.shape
    part = split_of(CAP // 2, 8)
    sums = jax.ShapeDtypeStruct((2, CAP // 2, factors_n), F32)
    chosen = (CAP, paths, factors_n)
    return pl.pallas_call(
        functools.partial(gather_kernel, part),
        in_specs=[HBM, HBM],
        out_specs=[HBM, VMEM, VMEM],
        out_shape=[
            pltpu.HBM(chosen, BF16),
            sums,
            sums,
        ],
        scratch_shapes=[
            pltpu.SMEM(tail.shape, jnp.int32),
            pltpu.VMEM(chosen, BF16),
            pltpu.SemaphoreType.DMA,
            pltpu.SemaphoreType.DMA((CAP // part,)),
            pltpu.SemaphoreType.DMA,
        ],
        compiler_params=small(8),
        cost_estimate=pl.CostEstimate(flops=0, bytes_accessed=0, transcendentals=0),
        name="gather_nodes",
    )(tail, normals)


def to_message(sums, squares, count):
    within = squares - sums * sums / count
    high = sums.astype(F16)
    low = (sums - high.astype(F32)).astype(F16)
    return jnp.stack([high, low, within.astype(F16)]), within


def moments(sums, within, arrived, count, live):
    chips = [(sums, within)]
    for message in arrived:
        high, low, squares = message.astype(F32)
        chips.append((high + low, squares))
    center = sum(s for s, _ in chips) / (count * len(chips))
    spread = sum(w + (s / count - center) ** 2 * count for s, w in chips)
    spread = spread / (count * len(chips))
    return jnp.stack([center, live * lax.rsqrt(spread + EPSILON)])


def order_kernel(
    unit, bound, plan, far, tail_hbm, states_hbm, loadings_hbm, strikes, hedge,
    levels, live, gain, *refs,
):
    chunks, steps, rows = len(plan), len(plan[0]), gain.shape[0]
    ordered, terms = refs[:chunks], refs[chunks : 2 * chunks]
    tail, states, onehot, own, tail_sem, states_sem, sems = refs[2 * chunks :]
    node_count = states.shape[0]
    position = lax.axis_index("inner")
    group, chip, core = lax.axis_index("outer"), position // 2, lax.rem(position, 2)
    tail_copy = pltpu.make_async_copy(tail_hbm, tail, tail_sem)
    states_copy = pltpu.make_async_copy(states_hbm, states, states_sem)
    tail_copy.start()
    states_copy.start()
    blocks, copies = [], []
    for chunk in range(chunks):
        for step in range(steps):
            d, away = plan[chunk][step]
            to_chip, to_group = far(chip, d, group, away)
            block = (to_group * chunks + to_chip) * 2 + core
            k = chunk * steps + step
            copy = pltpu.make_async_copy(loadings_hbm.at[block], own.at[k], sems.at[k])
            copy.start()
            blocks.append(block)
            copies.append(copy)
    wide = strikes.shape[1]
    lanes = lax.broadcasted_iota(jnp.int32, (rows, wide), 1)
    lines = lax.broadcasted_iota(jnp.int32, (rows, wide), 0)

    def column(ref, block):
        line = ref[pl.ds(block * rows // wide, 1), :]
        here = lanes == lines + lax.rem(block * rows, wide)
        return jnp.sum(jnp.where(here, line, 0.0), axis=1, keepdims=True)

    for k, block in enumerate(blocks):
        chunk, step = k // steps, k % steps
        at = slice(step * rows, (step + 1) * rows)
        size = column(hedge, block)
        scale = jnp.abs(size)
        terms[chunk][at, 0:1] = column(strikes, block) * 0.5
        terms[chunk][at, 1:2] = size * 0.5
        terms[chunk][at, 2:3] = jnp.where(
            scale > 1e-30, bound / jnp.maximum(scale, 1e-30), 0.0
        )
        if plan[chunk][step] == (0, 0):
            owned = scale * unit
    tail_copy.wait()
    base = group * node_count
    first = first_of(tail, base)
    nodes = lax.broadcasted_iota(jnp.int32, (1, node_count), 1)
    for slot in range(CAP):
        node, inside = place_of(tail, first, base, slot)
        used = inside & (node >= 0) & (node < node_count)
        onehot[slot : slot + 1, :] = ((nodes == node) & used).astype(F32)
        if slot < CAP // 2:
            live[slot : slot + 1, :] = jnp.full((1, live.shape[1]), used.astype(F32))
    states_copy.wait()
    levels[...] = jnp.dot(
        onehot[...].astype(BF16), states[...], preferred_element_type=F32
    )
    for k, copy in enumerate(copies):
        copy.wait()
        values = own[k].astype(F32)
        if plan[k // steps][k % steps] == (0, 0):
            gain[...] = values * owned
        ordered[k // steps][k % steps] = (values * 0.5).astype(BF16)


def order(unit, bound, plan, far, tail, states, loadings, strikes, hedge):
    chunks, steps = len(plan), len(plan[0])
    _, rows, factors_n = loadings.shape
    return pl.pallas_call(
        functools.partial(order_kernel, unit, bound, plan, far),
        in_specs=[HBM] * 3 + [VMEM] * 2,
        out_specs=[VMEM] * (2 * chunks + 3),
        out_shape=[
            jax.ShapeDtypeStruct((count, factors_n), F32) for count in (CAP, CAP // 2, rows)
        ]
        + [jax.ShapeDtypeStruct((steps, rows, factors_n), BF16)] * chunks
        + [jax.ShapeDtypeStruct((steps * rows, 3), F32)] * chunks,
        scratch_shapes=[
            pltpu.SMEM(tail.shape, jnp.int32),
            pltpu.VMEM(states.shape, BF16),
            pltpu.VMEM((CAP, states.shape[0]), F32),
            pltpu.VMEM((chunks * steps, rows, factors_n), BF16),
            pltpu.SemaphoreType.DMA,
            pltpu.SemaphoreType.DMA,
            pltpu.SemaphoreType.DMA((chunks * steps,)),
        ],
        compiler_params=small(12),
        cost_estimate=pl.CostEstimate(flops=0, bytes_accessed=1 << 20, transcendentals=0),
        name="order_instruments",
    )(tail, states, loadings, strikes, hedge)


def prepare(own, theirs, stats, levels, sigma, scaled, factors, ready, begin, end):
    slots, paths, factors_n = own.shape
    half = slots // 2
    shape = (paths, factors_n)
    sigmas = jnp.broadcast_to(sigma[...], shape)
    for at in range(begin, end):
        mine, row = at < half, at % half
        slot = row if mine == ready else row + half
        source = own if mine else theirs
        place = slot if mine else (slot + half) % slots
        center = jnp.broadcast_to(stats[0, row : row + 1, :], shape)
        rstd = jnp.broadcast_to(stats[1, row : row + 1, :], shape)
        level = jnp.broadcast_to(levels[place : place + 1, :], shape)
        unit = ((source[slot].astype(F32) - center) * rstd).astype(BF16)
        rows = slice(at * paths, (at + 1) * paths)
        scaled[rows, :] = unit
        factors[rows, :] = (level + sigmas * unit.astype(F32)).astype(BF16)


def ready_kernel(own, theirs, stats, levels, sigma, scaled, factors):
    prepare(own, theirs, stats, levels, sigma, scaled, factors, True, 0, own.shape[0])


def ready_rows(own, theirs, stats, levels, sigma):
    slots, paths, factors_n = own.shape
    half = jax.ShapeDtypeStruct((slots * paths, factors_n), BF16)
    return pl.pallas_call(
        ready_kernel,
        in_specs=[VMEM] * 5,
        out_specs=[VMEM] * 2,
        out_shape=[half] * 2,
        compiler_params=small(12),
        cost_estimate=pl.CostEstimate(
            flops=8 * slots * paths * factors_n,
            bytes_accessed=8 * slots * paths * factors_n,
            transcendentals=0,
        ),
        name="ready_rows",
    )(own, theirs, stats, levels, sigma)


def cross_of(tile, halves, loadings, terms, before=None):
    strikes, hedge, scale = terms[:, 0:1], terms[:, 1:2], terms[:, 2:3]
    part = loadings[...]
    each = halves[0][0].shape[0] // tile
    places = [(half, r * tile) for half in (0, 1) for r in range(each)]

    def level(half, at):
        if before is not None and half == 1:
            before(at // tile)
        rows = halves[half][1][at : at + tile, :]
        return lax.dot_general(
            part, rows, (((1,), (1,)), ((), ())), preferred_element_type=F32
        )

    total = None
    current = level(*places[0])
    for k, (half, at) in enumerate(places):
        after = level(*places[k + 1]) if k + 1 < len(places) else None
        weight = (jnp.tanh(current - strikes) * hedge + hedge).astype(BF16)
        cross = jnp.dot(
            weight, halves[half][0][at : at + tile, :], preferred_element_type=F32
        )
        total = cross if total is None else total + cross
        current = after
    return total * scale


def first_kernel(
    tile, own, theirs, stats, levels, sigma, ready_scaled, ready_factors,
    loadings, terms, scaled, factors, low, high,
):
    step = tile // own.shape[1]

    def before(r):
        prepare(
            own, theirs, stats, levels, sigma, scaled, factors, False,
            r * step, (r + 1) * step,
        )

    halves = ((ready_scaled, ready_factors), (scaled, factors))
    give(cross_of(tile, halves, loadings, terms, before), low, high)


def next_kernel(tile, s0, f0, s1, f1, loadings, terms, low, high):
    give(cross_of(tile, ((s0, f0), (s1, f1)), loadings, terms), low, high)


def give(sums, low, high):
    half = low.shape[0]
    low[...] = sums[:half]
    high[...] = sums[half:]


def halves_of(count, factors_n):
    return [
        jax.ShapeDtypeStruct((size, factors_n), F32) for size in (count // 2, count - count // 2)
    ]


def cost_of(rows, count, factors_n):
    return pl.CostEstimate(
        flops=2 * rows * count * factors_n,
        bytes_accessed=4 * count * factors_n,
        transcendentals=0,
    )


def tile_of(slots, paths):
    return paths * split_of(slots, max(1, 1280 // paths))


def first_chunk(own, theirs, stats, levels, sigma, ready, ordered, terms):
    slots, paths, factors_n = own.shape
    count = ordered.shape[0]
    half = jax.ShapeDtypeStruct((slots * paths, factors_n), BF16)
    return pl.pallas_call(
        functools.partial(first_kernel, tile_of(slots, paths)),
        in_specs=[VMEM] * 9,
        out_specs=[VMEM] * 4,
        out_shape=[half, half, *halves_of(count, factors_n)],
        compiler_params=small(16),
        cost_estimate=cost_of(2 * slots * paths, count, factors_n),
        name="first_chunk",
    )(own, theirs, stats, levels, sigma, *ready, ordered, terms)


def next_chunk(tile, ready, rest, ordered, terms):
    rows, factors_n = ready[0].shape
    count = ordered.shape[0]
    return pl.pallas_call(
        functools.partial(next_kernel, tile),
        in_specs=[VMEM] * 6,
        out_specs=[VMEM] * 2,
        out_shape=halves_of(count, factors_n),
        compiler_params=small(16),
        cost_estimate=cost_of(2 * rows, count, factors_n),
        name="next_chunk",
    )(*ready, *rest, ordered, terms)


def body(normals, states, loadings, strikes, hedge, sigma, tail):
    groups = lax.axis_size("outer")
    inner = lax.axis_size("inner")
    chips = inner // 2
    _, per_node, factors_n = normals.shape
    instruments = loadings.shape[0]
    tail_count = tail.shape[0]
    paths = per_node * inner
    rows = instruments // (groups * inner)
    paired = chips & (chips - 1) == 0

    def partner(of, d):
        return of ^ d if paired else (of + d) % chips

    def beyond(of, s):
        return of ^ s if groups & (groups - 1) == 0 else (of + s) % groups

    def to_core(x):
        return lax.ppermute(x, "inner", [(i, i ^ 1) for i in range(inner)])

    def to_chip(x, d):
        return lax.ppermute(
            x, "inner", [(i, partner(i // 2, d) * 2 + i % 2) for i in range(inner)]
        )

    def to_group(x, s):
        return lax.ppermute(x, "outer", [(g, beyond(g, s)) for g in range(groups)])

    bound = 32768.0 / (tail_count * paths)
    unit = 1.0 / (bound * tail_count * paths)

    tail, normals, states, loadings = (
        pltpu.with_memory_space_constraint(x, pltpu.HBM)
        for x in (tail, normals, states, loadings.reshape(groups * inner, rows, factors_n))
    )
    wide = 128 if 128 % rows == 0 else rows
    strikes, hedge = strikes.reshape(-1, wide), hedge.reshape(-1, wide)

    chosen, mine, other = gather_nodes(tail, normals)
    sums, squares = mine + to_core(other)
    message, within = to_message(sums, squares, 2 * per_node)
    chosen, message, strikes = lax.optimization_barrier((chosen, message, strikes))
    arrived = [to_chip(message, d) for d in range(chips - 1, 0, -1)]
    theirs = to_core(chosen)
    steps = range(groups)
    relayed = chips == 4 and groups % 2 == 0
    if relayed:
        low, high = steps[: groups // 2], steps[groups // 2 :]
        plan = [
            [(3, s) for s in steps],
            [(1, s) for s in high] + [(2, s) for s in low],
            [(1, s) for s in low] + [(2, s) for s in high],
            [(0, s) for s in steps],
        ]
    else:
        plan = [[(d, s) for s in steps] for d in range(chips - 1, -1, -1)]
    far = lambda chip, d, group, s: (partner(chip, d), beyond(group, s))
    levels, live, gain, *parts = order(
        unit, bound, plan, far, tail, states, loadings, strikes, hedge
    )
    ordered = [part.reshape(groups * rows, factors_n) for part in parts[: len(plan)]]
    terms = parts[len(plan) :]
    arrived, theirs, levels, live, gain, ordered, terms = lax.optimization_barrier(
        (arrived, theirs, levels, live, gain, ordered, terms)
    )
    stats = moments(sums, within, arrived, 2 * per_node, live)
    their_stats = to_core(stats)

    sigmas = sigma.reshape(1, factors_n)
    ready = ready_rows(chosen, theirs, stats, levels, sigmas)

    tile = tile_of(CAP, per_node)
    *rest, low, high = first_chunk(
        chosen, theirs, their_stats, levels, sigmas, ready, ordered[0], terms[0]
    )

    def chunk(k, *after):
        kept, _ = lax.optimization_barrier((tuple(rest), after))
        return next_chunk(tile, ready, kept, ordered[k], terms[k])

    def plus(x, y):
        return x + y.astype(F32)

    if relayed:
        a3, b3 = low.astype(F16), high.astype(F16)
        from_a3, from_b3 = to_chip(a3, 2), to_chip(b3, 1)
        b1, a2 = (x.astype(F16) for x in chunk(1, a3, b3))
        from_b1, from_a2 = to_chip(b1, 1), to_chip(a2, 2)
        a1, b2 = chunk(2, b1, a2, from_a3, from_b3)
        a1, b2 = plus(a1, from_a3).astype(F16), plus(b2, from_b3).astype(F16)
        from_a1, from_b2 = to_chip(a1, 1), to_chip(b2, 2)
        a0, b0 = chunk(3, from_b1, from_a2, a1, b2)
        a0, b0 = plus(a0, from_a2), plus(b0, from_b1)
        kept = jnp.concatenate([plus(a0, from_a1), plus(b0, from_b2)])
    else:
        arrived = []
        for k in range(1, chips):
            sent = jnp.concatenate([low, high]).astype(F16)
            arrived.append(to_chip(sent, chips - k))
            low, high = chunk(k, sent)
        kept = jnp.concatenate([low, high])
        for item in arrived:
            kept = plus(kept, item)
    owned = kept[:rows]
    for s in sorted(range(1, groups), key=lambda s: (s & -s) == s and -s):
        owned = owned + to_group(kept[s * rows : (s + 1) * rows].astype(F16), s).astype(F32)
    return gain * owned


def solution(mesh):
    placed = (P("outer", "inner", None), P("outer", None), P(), P(), P(), P(), P())
    return jax.shard_map(
        body, mesh=mesh, in_specs=placed, out_specs=P(("outer", "inner"), None), check_vma=False
    )
```

```python
import functools

import jax
import jax.numpy as jnp
from jax import lax
from jax.experimental import pallas as pl
from jax.experimental.pallas import tpu as pltpu
from jax.sharding import PartitionSpec as P

CAP = 80
EPSILON = 1e-06
VMEM = pl.BlockSpec(memory_space=pltpu.VMEM)
SMEM = pl.BlockSpec(memory_space=pltpu.SMEM)
HBM = pl.BlockSpec(memory_space=pltpu.HBM)
F32 = jnp.float32
BF16 = jnp.bfloat16
F16 = jnp.float16


def split_of(count, most):
    for size in range(min(count, most), 0, -1):
        if count % size == 0:
            return size
    return 1


def small(mebibytes):
    return pltpu.CompilerParams(vmem_limit_bytes=mebibytes << 20)


def first_of(tail, base):
    count = tail.shape[0]
    first = jnp.int32(0)
    for bit in range(count.bit_length() - 1, -1, -1):
        ahead = first + (1 << bit)
        below = tail[jnp.minimum(ahead, count) - 1] < base
        first = jnp.where((ahead <= count) & below, ahead, first)
    return first


def place_of(tail, first, base, slot):
    at = slot + lax.rem(lax.axis_index("inner"), 2) * (CAP // 2)
    at = first + jnp.where(at >= CAP, at - CAP, at)
    node = tail[jnp.minimum(at, tail.shape[0] - 1)] - base
    return node, at < tail.shape[0]


def gather_kernel(
    part, tail_hbm, normals, chosen_hbm, mine, other,
    tail, chosen, tail_sem, sems, out_sem,
):
    node_count = normals.shape[0]
    tail_copy = pltpu.make_async_copy(tail_hbm, tail, tail_sem)
    tail_copy.start()
    base = lax.axis_index("outer") * node_count
    tail_copy.wait()
    first = first_of(tail, base)
    parts = CAP // part

    @pl.loop(0, parts)
    def _(p):
        for k in range(part):
            slot = p * part + k
            node, _ = place_of(tail, first, base, slot)
            node = jnp.minimum(jnp.maximum(node, 0), node_count - 1)
            pltpu.make_async_copy(normals.at[node], chosen.at[slot], sems.at[p]).start()

    out_copy = pltpu.make_async_copy(chosen, chosen_hbm, out_sem)
    for begin, sums in ((0, mine), (parts // 2, other)):

        @pl.loop(0, parts // 2)
        def _(p):
            piece = chosen.at[pl.ds((begin + p) * part, part)]
            pltpu.make_async_copy(piece, piece, sems.at[begin + p]).wait()
            there = chosen_hbm.at[pl.ds((begin + p) * part, part)]
            pltpu.make_async_copy(piece, there, out_sem).start()
            values = piece[...].astype(F32)
            rows = pl.ds(pl.multiple_of(p * part, part), part)
            sums[0, rows, :] = jnp.sum(values, axis=1)
            sums[1, rows, :] = jnp.sum(values * values, axis=1)

    out_copy.wait()


def gather_nodes(tail, normals):
    _, paths, factors_n = normals.shape
    part = split_of(CAP // 2, 8)
    sums = jax.ShapeDtypeStruct((2, CAP // 2, factors_n), F32)
    chosen = (CAP, paths, factors_n)
    return pl.pallas_call(
        functools.partial(gather_kernel, part),
        in_specs=[HBM, HBM],
        out_specs=[HBM, VMEM, VMEM],
        out_shape=[
            pltpu.HBM(chosen, BF16),
            sums,
            sums,
        ],
        scratch_shapes=[
            pltpu.SMEM(tail.shape, jnp.int32),
            pltpu.VMEM(chosen, BF16),
            pltpu.SemaphoreType.DMA,
            pltpu.SemaphoreType.DMA((CAP // part,)),
            pltpu.SemaphoreType.DMA,
        ],
        compiler_params=small(8),
        cost_estimate=pl.CostEstimate(flops=0, bytes_accessed=0, transcendentals=0),
        name="gather_nodes",
    )(tail, normals)


def to_message(sums, squares, count):
    within = squares - sums * sums / count
    high = sums.astype(F16)
    low = (sums - high.astype(F32)).astype(F16)
    return jnp.stack([high, low, within.astype(F16)]), within


def moments(sums, within, arrived, count, live):
    chips = [(sums, within)]
    for message in arrived:
        high, low, squares = message.astype(F32)
        chips.append((high + low, squares))
    center = sum(s for s, _ in chips) / (count * len(chips))
    spread = sum(w + (s / count - center) ** 2 * count for s, w in chips)
    spread = spread / (count * len(chips))
    return jnp.stack([center, live * lax.rsqrt(spread + EPSILON)])


def order_kernel(
    unit, bound, plan, far, tail_hbm, states_hbm, loadings_hbm, strikes, hedge,
    levels, live, gain, *refs,
):
    chunks, steps, rows = len(plan), len(plan[0]), gain.shape[0]
    ordered, terms = refs[:chunks], refs[chunks : 2 * chunks]
    tail, states, onehot, own, tail_sem, states_sem, sems = refs[2 * chunks :]
    node_count = states.shape[0]
    position = lax.axis_index("inner")
    group, chip, core = lax.axis_index("outer"), position // 2, lax.rem(position, 2)
    tail_copy = pltpu.make_async_copy(tail_hbm, tail, tail_sem)
    states_copy = pltpu.make_async_copy(states_hbm, states, states_sem)
    tail_copy.start()
    states_copy.start()
    blocks, copies = [], []
    for chunk in range(chunks):
        for step in range(steps):
            d, away = plan[chunk][step]
            to_chip, to_group = far(chip, d, group, away)
            block = (to_group * chunks + to_chip) * 2 + core
            k = chunk * steps + step
            copy = pltpu.make_async_copy(loadings_hbm.at[block], own.at[k], sems.at[k])
            copy.start()
            blocks.append(block)
            copies.append(copy)
    wide = strikes.shape[1]
    lanes = lax.broadcasted_iota(jnp.int32, (rows, wide), 1)
    lines = lax.broadcasted_iota(jnp.int32, (rows, wide), 0)

    def column(ref, block):
        line = ref[pl.ds(block * rows // wide, 1), :]
        here = lanes == lines + lax.rem(block * rows, wide)
        return jnp.sum(jnp.where(here, line, 0.0), axis=1, keepdims=True)

    for k, block in enumerate(blocks):
        chunk, step = k // steps, k % steps
        at = slice(step * rows, (step + 1) * rows)
        size = column(hedge, block)
        scale = jnp.abs(size)
        terms[chunk][at, 0:1] = column(strikes, block) * 0.5
        terms[chunk][at, 1:2] = size * 0.5
        terms[chunk][at, 2:3] = jnp.where(
            scale > 1e-30, bound / jnp.maximum(scale, 1e-30), 0.0
        )
        if plan[chunk][step] == (0, 0):
            owned = scale * unit
    tail_copy.wait()
    base = group * node_count
    first = first_of(tail, base)
    nodes = lax.broadcasted_iota(jnp.int32, (1, node_count), 1)
    for slot in range(CAP):
        node, inside = place_of(tail, first, base, slot)
        used = inside & (node >= 0) & (node < node_count)
        onehot[slot : slot + 1, :] = ((nodes == node) & used).astype(F32)
        if slot < CAP // 2:
            live[slot : slot + 1, :] = jnp.full((1, live.shape[1]), used.astype(F32))
    states_copy.wait()
    levels[...] = jnp.dot(
        onehot[...].astype(BF16), states[...], preferred_element_type=F32
    )
    for k, copy in enumerate(copies):
        copy.wait()
        values = own[k].astype(F32)
        if plan[k // steps][k % steps] == (0, 0):
            gain[...] = values * owned
        ordered[k // steps][k % steps] = (values * 0.5).astype(BF16)


def order(unit, bound, plan, far, tail, states, loadings, strikes, hedge):
    chunks, steps = len(plan), len(plan[0])
    _, rows, factors_n = loadings.shape
    return pl.pallas_call(
        functools.partial(order_kernel, unit, bound, plan, far),
        in_specs=[HBM] * 3 + [VMEM] * 2,
        out_specs=[VMEM] * (2 * chunks + 3),
        out_shape=[
            jax.ShapeDtypeStruct((count, factors_n), F32) for count in (CAP, CAP // 2, rows)
        ]
        + [jax.ShapeDtypeStruct((steps, rows, factors_n), BF16)] * chunks
        + [jax.ShapeDtypeStruct((steps * rows, 3), F32)] * chunks,
        scratch_shapes=[
            pltpu.SMEM(tail.shape, jnp.int32),
            pltpu.VMEM(states.shape, BF16),
            pltpu.VMEM((CAP, states.shape[0]), F32),
            pltpu.VMEM((chunks * steps, rows, factors_n), BF16),
            pltpu.SemaphoreType.DMA,
            pltpu.SemaphoreType.DMA,
            pltpu.SemaphoreType.DMA((chunks * steps,)),
        ],
        compiler_params=small(12),
        cost_estimate=pl.CostEstimate(flops=0, bytes_accessed=1 << 20, transcendentals=0),
        name="order_instruments",
    )(tail, states, loadings, strikes, hedge)


def prepare(own, theirs, stats, levels, sigma, scaled, factors, ready, begin, end):
    slots, paths, factors_n = own.shape
    half = slots // 2
    shape = (paths, factors_n)
    sigmas = jnp.broadcast_to(sigma[...], shape)
    for at in range(begin, end):
        mine, row = at < half, at % half
        slot = row if mine == ready else row + half
        source = own if mine else theirs
        place = slot if mine else (slot + half) % slots
        center = jnp.broadcast_to(stats[0, row : row + 1, :], shape)
        rstd = jnp.broadcast_to(stats[1, row : row + 1, :], shape)
        level = jnp.broadcast_to(levels[place : place + 1, :], shape)
        unit = ((source[slot].astype(F32) - center) * rstd).astype(BF16)
        rows = slice(at * paths, (at + 1) * paths)
        scaled[rows, :] = unit
        factors[rows, :] = (level + sigmas * unit.astype(F32)).astype(BF16)


def ready_kernel(own, theirs, stats, levels, sigma, scaled, factors):
    prepare(own, theirs, stats, levels, sigma, scaled, factors, True, 0, own.shape[0])


def ready_rows(own, theirs, stats, levels, sigma):
    slots, paths, factors_n = own.shape
    half = jax.ShapeDtypeStruct((slots * paths, factors_n), BF16)
    return pl.pallas_call(
        ready_kernel,
        in_specs=[VMEM] * 5,
        out_specs=[VMEM] * 2,
        out_shape=[half] * 2,
        compiler_params=small(12),
        cost_estimate=pl.CostEstimate(
            flops=8 * slots * paths * factors_n,
            bytes_accessed=8 * slots * paths * factors_n,
            transcendentals=0,
        ),
        name="ready_rows",
    )(own, theirs, stats, levels, sigma)


def cross_of(tile, halves, loadings, terms, before=None):
    strikes, hedge, scale = terms[:, 0:1], terms[:, 1:2], terms[:, 2:3]
    part = loadings[...]
    each = halves[0][0].shape[0] // tile
    places = [(half, r * tile) for half in (0, 1) for r in range(each)]

    def level(half, at):
        if before is not None and half == 1:
            before(at // tile)
        rows = halves[half][1][at : at + tile, :]
        return lax.dot_general(
            part, rows, (((1,), (1,)), ((), ())), preferred_element_type=F32
        )

    total = None
    current = level(*places[0])
    for k, (half, at) in enumerate(places):
        after = level(*places[k + 1]) if k + 1 < len(places) else None
        weight = (jnp.tanh(current - strikes) * hedge + hedge).astype(BF16)
        cross = jnp.dot(
            weight, halves[half][0][at : at + tile, :], preferred_element_type=F32
        )
        total = cross if total is None else total + cross
        current = after
    return total * scale


def first_kernel(
    tile, own, theirs, stats, levels, sigma, ready_scaled, ready_factors,
    loadings, terms, scaled, factors, low, high,
):
    step = tile // own.shape[1]

    def before(r):
        prepare(
            own, theirs, stats, levels, sigma, scaled, factors, False,
            r * step, (r + 1) * step,
        )

    halves = ((ready_scaled, ready_factors), (scaled, factors))
    give(cross_of(tile, halves, loadings, terms, before), low, high)


def next_kernel(tile, s0, f0, s1, f1, loadings, terms, low, high):
    give(cross_of(tile, ((s0, f0), (s1, f1)), loadings, terms), low, high)


def give(sums, low, high):
    half = low.shape[0]
    low[...] = sums[:half]
    high[...] = sums[half:]


def halves_of(count, factors_n):
    return [
        jax.ShapeDtypeStruct((size, factors_n), F32) for size in (count // 2, count - count // 2)
    ]


def cost_of(rows, count, factors_n):
    return pl.CostEstimate(
        flops=2 * rows * count * factors_n,
        bytes_accessed=4 * count * factors_n,
        transcendentals=0,
    )


def tile_of(slots, paths):
    return paths * split_of(slots, max(1, 1280 // paths))


def first_chunk(own, theirs, stats, levels, sigma, ready, ordered, terms):
    slots, paths, factors_n = own.shape
    count = ordered.shape[0]
    half = jax.ShapeDtypeStruct((slots * paths, factors_n), BF16)
    return pl.pallas_call(
        functools.partial(first_kernel, tile_of(slots, paths)),
        in_specs=[VMEM] * 9,
        out_specs=[VMEM] * 4,
        out_shape=[half, half, *halves_of(count, factors_n)],
        compiler_params=small(16),
        cost_estimate=cost_of(2 * slots * paths, count, factors_n),
        name="first_chunk",
    )(own, theirs, stats, levels, sigma, *ready, ordered, terms)


def next_chunk(tile, ready, rest, ordered, terms):
    rows, factors_n = ready[0].shape
    count = ordered.shape[0]
    return pl.pallas_call(
        functools.partial(next_kernel, tile),
        in_specs=[VMEM] * 6,
        out_specs=[VMEM] * 2,
        out_shape=halves_of(count, factors_n),
        compiler_params=small(16),
        cost_estimate=cost_of(2 * rows, count, factors_n),
        name="next_chunk",
    )(*ready, *rest, ordered, terms)


def body(normals, states, loadings, strikes, hedge, sigma, tail):
    groups = lax.axis_size("outer")
    inner = lax.axis_size("inner")
    chips = inner // 2
    _, per_node, factors_n = normals.shape
    instruments = loadings.shape[0]
    tail_count = tail.shape[0]
    paths = per_node * inner
    rows = instruments // (groups * inner)
    paired = chips & (chips - 1) == 0

    def partner(of, d):
        return of ^ d if paired else (of + d) % chips

    def beyond(of, s):
        return of ^ s if groups & (groups - 1) == 0 else (of + s) % groups

    def to_core(x):
        return lax.ppermute(x, "inner", [(i, i ^ 1) for i in range(inner)])

    def to_chip(x, d):
        return lax.ppermute(
            x, "inner", [(i, partner(i // 2, d) * 2 + i % 2) for i in range(inner)]
        )

    def to_group(x, s):
        return lax.ppermute(x, "outer", [(g, beyond(g, s)) for g in range(groups)])

    bound = 32768.0 / (tail_count * paths)
    unit = 1.0 / (bound * tail_count * paths)

    tail, normals, states, loadings = (
        pltpu.with_memory_space_constraint(x, pltpu.HBM)
        for x in (tail, normals, states, loadings.reshape(groups * inner, rows, factors_n))
    )
    wide = 128 if 128 % rows == 0 else rows
    strikes, hedge = strikes.reshape(-1, wide), hedge.reshape(-1, wide)

    chosen, mine, other = gather_nodes(tail, normals)
    sums, squares = mine + to_core(other)
    message, within = to_message(sums, squares, 2 * per_node)
    chosen, message, strikes = lax.optimization_barrier((chosen, message, strikes))
    arrived = [to_chip(message, d) for d in range(chips - 1, 0, -1)]
    theirs = to_core(chosen)
    steps = range(groups)
    relayed = chips == 4 and groups % 2 == 0
    if relayed:
        half = groups // 2
        low, high = steps[:half], steps[half:]
        plan = [
            [(3, s) for s in steps],
            [(1, s) for s in high] + [(2, s) for s in high],
            [(0, s) for s in steps],
            [(2, s) for s in low] + [(1, s) for s in low],
        ]
    else:
        plan = [[(d, s) for s in steps] for d in range(chips - 1, -1, -1)]
    far = lambda chip, d, group, s: (partner(chip, d), beyond(group, s))
    levels, live, gain, *parts = order(
        unit, bound, plan, far, tail, states, loadings, strikes, hedge
    )
    ordered = [part.reshape(groups * rows, factors_n) for part in parts[: len(plan)]]
    terms = parts[len(plan) :]
    arrived, theirs, levels, live, gain, ordered, terms = lax.optimization_barrier(
        (arrived, theirs, levels, live, gain, ordered, terms)
    )
    stats = moments(sums, within, arrived, 2 * per_node, live)
    their_stats = to_core(stats)

    sigmas = sigma.reshape(1, factors_n)
    ready = ready_rows(chosen, theirs, stats, levels, sigmas)

    tile = tile_of(CAP, per_node)
    *rest, low, high = first_chunk(
        chosen, theirs, their_stats, levels, sigmas, ready, ordered[0], terms[0]
    )

    def chunk(k, *after):
        kept, _ = lax.optimization_barrier((tuple(rest), after))
        return next_chunk(tile, ready, kept, ordered[k], terms[k])

    def plus(x, y):
        return x + y.astype(F32)

    if relayed:
        a3, b3 = low.astype(F16), high.astype(F16)
        from_b3, from_a3 = to_chip(b3, 1), to_chip(a3, 2)
        b1, b2 = chunk(1, a3, b3)
        b1, b2 = b1.astype(F16), plus(b2, from_b3).astype(F16)
        from_b1, from_b2 = to_chip(b1, 1), to_chip(b2, 2)
        a0, b0 = chunk(2, b1, b2)
        a2, a1 = chunk(3, a0, b0, from_a3)
        a2, a1 = a2.astype(F16), plus(a1, from_a3).astype(F16)
        from_a2, from_a1 = to_chip(a2, 2), to_chip(a1, 1)
        b0, _ = lax.optimization_barrier((b0, (a2, a1)))
        kept = (plus(plus(a0, from_a2), from_a1), plus(plus(b0, from_b1), from_b2))
        part = lambda s: kept[s // half][s % half * rows :][:rows]
    else:
        arrived = []
        for k in range(1, chips):
            sent = jnp.concatenate([low, high]).astype(F16)
            arrived.append(to_chip(sent, chips - k))
            low, high = chunk(k, sent)
        kept = jnp.concatenate([low, high])
        for item in arrived:
            kept = plus(kept, item)
        part = lambda s: kept[s * rows :][:rows]
    owned = part(0)
    for s in sorted(range(1, groups), key=lambda s: (s < groups // 2, s)):
        owned = plus(owned, to_group(part(s).astype(F16), s))
    return gain * owned


def solution(mesh):
    placed = (P("outer", "inner", None), P("outer", None), P(), P(), P(), P(), P())
    return jax.shard_map(
        body, mesh=mesh, in_specs=placed, out_specs=P(("outer", "inner"), None), check_vma=False
    )
```

```python
import functools

import jax
import jax.numpy as jnp
from jax import lax
from jax.experimental import pallas as pl
from jax.experimental.pallas import tpu as pltpu
from jax.sharding import PartitionSpec as P

CAP = 80
EPSILON = 1e-06
VMEM = pl.BlockSpec(memory_space=pltpu.VMEM)
SMEM = pl.BlockSpec(memory_space=pltpu.SMEM)
HBM = pl.BlockSpec(memory_space=pltpu.HBM)
F32 = jnp.float32
BF16 = jnp.bfloat16
F16 = jnp.float16


def split_of(count, most):
    for size in range(min(count, most), 0, -1):
        if count % size == 0:
            return size
    return 1


def small(mebibytes):
    return pltpu.CompilerParams(vmem_limit_bytes=mebibytes << 20)


def first_of(tail, base):
    count = tail.shape[0]
    first = jnp.int32(0)
    for bit in range(count.bit_length() - 1, -1, -1):
        ahead = first + (1 << bit)
        below = tail[jnp.minimum(ahead, count) - 1] < base
        first = jnp.where((ahead <= count) & below, ahead, first)
    return first


def place_of(tail, first, base, slot):
    at = slot + lax.rem(lax.axis_index("inner"), 2) * (CAP // 2)
    at = first + jnp.where(at >= CAP, at - CAP, at)
    node = tail[jnp.minimum(at, tail.shape[0] - 1)] - base
    return node, at < tail.shape[0]


def gather_kernel(
    part, tail_hbm, normals, chosen_hbm, mine, other,
    tail, chosen, tail_sem, sems, out_sem,
):
    node_count = normals.shape[0]
    tail_copy = pltpu.make_async_copy(tail_hbm, tail, tail_sem)
    tail_copy.start()
    base = lax.axis_index("outer") * node_count
    tail_copy.wait()
    first = first_of(tail, base)
    parts = CAP // part

    @pl.loop(0, parts)
    def _(p):
        for k in range(part):
            slot = p * part + k
            node, _ = place_of(tail, first, base, slot)
            node = jnp.minimum(jnp.maximum(node, 0), node_count - 1)
            pltpu.make_async_copy(normals.at[node], chosen.at[slot], sems.at[p]).start()

    out_copy = pltpu.make_async_copy(chosen, chosen_hbm, out_sem)
    for begin, sums in ((0, mine), (parts // 2, other)):

        @pl.loop(0, parts // 2)
        def _(p):
            piece = chosen.at[pl.ds((begin + p) * part, part)]
            pltpu.make_async_copy(piece, piece, sems.at[begin + p]).wait()
            there = chosen_hbm.at[pl.ds((begin + p) * part, part)]
            pltpu.make_async_copy(piece, there, out_sem).start()
            values = piece[...].astype(F32)
            rows = pl.ds(pl.multiple_of(p * part, part), part)
            sums[0, rows, :] = jnp.sum(values, axis=1)
            sums[1, rows, :] = jnp.sum(values * values, axis=1)

    out_copy.wait()


def gather_nodes(tail, normals):
    _, paths, factors_n = normals.shape
    part = split_of(CAP // 2, 8)
    sums = jax.ShapeDtypeStruct((2, CAP // 2, factors_n), F32)
    chosen = (CAP, paths, factors_n)
    return pl.pallas_call(
        functools.partial(gather_kernel, part),
        in_specs=[HBM, HBM],
        out_specs=[HBM, VMEM, VMEM],
        out_shape=[
            pltpu.HBM(chosen, BF16),
            sums,
            sums,
        ],
        scratch_shapes=[
            pltpu.SMEM(tail.shape, jnp.int32),
            pltpu.VMEM(chosen, BF16),
            pltpu.SemaphoreType.DMA,
            pltpu.SemaphoreType.DMA((CAP // part,)),
            pltpu.SemaphoreType.DMA,
        ],
        compiler_params=small(8),
        cost_estimate=pl.CostEstimate(flops=0, bytes_accessed=0, transcendentals=0),
        name="gather_nodes",
    )(tail, normals)


def to_message(sums, squares, count):
    within = squares - sums * sums / count
    high = sums.astype(F16)
    low = (sums - high.astype(F32)).astype(F16)
    return jnp.stack([high, low, within.astype(F16)]), within


def moments(sums, within, arrived, count, live):
    chips = [(sums, within)]
    for message in arrived:
        high, low, squares = message.astype(F32)
        chips.append((high + low, squares))
    center = sum(s for s, _ in chips) / (count * len(chips))
    spread = sum(w + (s / count - center) ** 2 * count for s, w in chips)
    spread = spread / (count * len(chips))
    return jnp.stack([center, live * lax.rsqrt(spread + EPSILON)])


def order_kernel(
    unit, bound, plan, far, tail_hbm, states_hbm, loadings_hbm, strikes, hedge,
    levels, live, gain, *refs,
):
    chunks, steps, rows = len(plan), len(plan[0]), gain.shape[0]
    ordered, terms = refs[:chunks], refs[chunks : 2 * chunks]
    tail, states, onehot, own, tail_sem, states_sem, sems = refs[2 * chunks :]
    node_count = states.shape[0]
    position = lax.axis_index("inner")
    group, chip, core = lax.axis_index("outer"), position // 2, lax.rem(position, 2)
    tail_copy = pltpu.make_async_copy(tail_hbm, tail, tail_sem)
    states_copy = pltpu.make_async_copy(states_hbm, states, states_sem)
    tail_copy.start()
    states_copy.start()
    blocks, copies = [], []
    for chunk in range(chunks):
        for step in range(steps):
            d, away = plan[chunk][step]
            to_chip, to_group = far(chip, core, d, group, away)
            block = (to_group * chunks + to_chip) * 2 + core
            k = chunk * steps + step
            copy = pltpu.make_async_copy(loadings_hbm.at[block], own.at[k], sems.at[k])
            copy.start()
            blocks.append(block)
            copies.append(copy)
    wide = strikes.shape[1]
    lanes = lax.broadcasted_iota(jnp.int32, (rows, wide), 1)
    lines = lax.broadcasted_iota(jnp.int32, (rows, wide), 0)

    def column(ref, block):
        line = ref[pl.ds(block * rows // wide, 1), :]
        here = lanes == lines + lax.rem(block * rows, wide)
        return jnp.sum(jnp.where(here, line, 0.0), axis=1, keepdims=True)

    for k, block in enumerate(blocks):
        chunk, step = k // steps, k % steps
        at = slice(step * rows, (step + 1) * rows)
        size = column(hedge, block)
        scale = jnp.abs(size)
        terms[chunk][at, 0:1] = column(strikes, block) * 0.5
        terms[chunk][at, 1:2] = size * 0.5
        terms[chunk][at, 2:3] = jnp.where(
            scale > 1e-30, bound / jnp.maximum(scale, 1e-30), 0.0
        )
        if plan[chunk][step] == (0, 0):
            owned = scale * unit
    tail_copy.wait()
    base = group * node_count
    first = first_of(tail, base)
    nodes = lax.broadcasted_iota(jnp.int32, (1, node_count), 1)
    for slot in range(CAP):
        node, inside = place_of(tail, first, base, slot)
        used = inside & (node >= 0) & (node < node_count)
        onehot[slot : slot + 1, :] = ((nodes == node) & used).astype(F32)
        if slot < CAP // 2:
            live[slot : slot + 1, :] = jnp.full((1, live.shape[1]), used.astype(F32))
    states_copy.wait()
    levels[...] = jnp.dot(
        onehot[...].astype(BF16), states[...], preferred_element_type=F32
    )
    for k, copy in enumerate(copies):
        copy.wait()
        values = own[k].astype(F32)
        if plan[k // steps][k % steps] == (0, 0):
            gain[...] = values * owned
        ordered[k // steps][k % steps] = (values * 0.5).astype(BF16)


def order(unit, bound, plan, far, tail, states, loadings, strikes, hedge):
    chunks, steps = len(plan), len(plan[0])
    _, rows, factors_n = loadings.shape
    return pl.pallas_call(
        functools.partial(order_kernel, unit, bound, plan, far),
        in_specs=[HBM] * 3 + [VMEM] * 2,
        out_specs=[VMEM] * (2 * chunks + 3),
        out_shape=[
            jax.ShapeDtypeStruct((count, factors_n), F32) for count in (CAP, CAP // 2, rows)
        ]
        + [jax.ShapeDtypeStruct((steps, rows, factors_n), BF16)] * chunks
        + [jax.ShapeDtypeStruct((steps * rows, 3), F32)] * chunks,
        scratch_shapes=[
            pltpu.SMEM(tail.shape, jnp.int32),
            pltpu.VMEM(states.shape, BF16),
            pltpu.VMEM((CAP, states.shape[0]), F32),
            pltpu.VMEM((chunks * steps, rows, factors_n), BF16),
            pltpu.SemaphoreType.DMA,
            pltpu.SemaphoreType.DMA,
            pltpu.SemaphoreType.DMA((chunks * steps,)),
        ],
        compiler_params=small(12),
        cost_estimate=pl.CostEstimate(flops=0, bytes_accessed=1 << 20, transcendentals=0),
        name="order_instruments",
    )(tail, states, loadings, strikes, hedge)


def prepare(own, theirs, stats, levels, sigma, scaled, factors, ready, begin, end):
    slots, paths, factors_n = own.shape
    half = slots // 2
    shape = (paths, factors_n)
    sigmas = jnp.broadcast_to(sigma[...], shape)
    for at in range(begin, end):
        mine, row = at < half, at % half
        slot = row if mine == ready else row + half
        source = own if mine else theirs
        place = slot if mine else (slot + half) % slots
        center = jnp.broadcast_to(stats[0, row : row + 1, :], shape)
        rstd = jnp.broadcast_to(stats[1, row : row + 1, :], shape)
        level = jnp.broadcast_to(levels[place : place + 1, :], shape)
        unit = ((source[slot].astype(F32) - center) * rstd).astype(BF16)
        rows = slice(at * paths, (at + 1) * paths)
        scaled[rows, :] = unit
        factors[rows, :] = (level + sigmas * unit.astype(F32)).astype(BF16)


def ready_kernel(own, theirs, stats, levels, sigma, scaled, factors):
    prepare(own, theirs, stats, levels, sigma, scaled, factors, True, 0, own.shape[0])


def ready_rows(own, theirs, stats, levels, sigma):
    slots, paths, factors_n = own.shape
    half = jax.ShapeDtypeStruct((slots * paths, factors_n), BF16)
    return pl.pallas_call(
        ready_kernel,
        in_specs=[VMEM] * 5,
        out_specs=[VMEM] * 2,
        out_shape=[half] * 2,
        compiler_params=small(12),
        cost_estimate=pl.CostEstimate(
            flops=8 * slots * paths * factors_n,
            bytes_accessed=8 * slots * paths * factors_n,
            transcendentals=0,
        ),
        name="ready_rows",
    )(own, theirs, stats, levels, sigma)


def cross_of(tile, halves, loadings, terms, before=None):
    strikes, hedge, scale = terms[:, 0:1], terms[:, 1:2], terms[:, 2:3]
    part = loadings[...]
    each = halves[0][0].shape[0] // tile
    places = [(half, r * tile) for half in (0, 1) for r in range(each)]

    def level(half, at):
        if before is not None and half == 1:
            before(at // tile)
        rows = halves[half][1][at : at + tile, :]
        return lax.dot_general(
            part, rows, (((1,), (1,)), ((), ())), preferred_element_type=F32
        )

    total = None
    current = level(*places[0])
    for k, (half, at) in enumerate(places):
        after = level(*places[k + 1]) if k + 1 < len(places) else None
        weight = (jnp.tanh(current - strikes) * hedge + hedge).astype(BF16)
        cross = jnp.dot(
            weight, halves[half][0][at : at + tile, :], preferred_element_type=F32
        )
        total = cross if total is None else total + cross
        current = after
    return total * scale


def first_kernel(
    tile, own, theirs, stats, levels, sigma, ready_scaled, ready_factors,
    loadings, terms, scaled, factors, low, high,
):
    step = tile // own.shape[1]

    def before(r):
        prepare(
            own, theirs, stats, levels, sigma, scaled, factors, False,
            r * step, (r + 1) * step,
        )

    halves = ((ready_scaled, ready_factors), (scaled, factors))
    give(cross_of(tile, halves, loadings, terms, before), low, high)


def next_kernel(tile, s0, f0, s1, f1, loadings, terms, low, high):
    give(cross_of(tile, ((s0, f0), (s1, f1)), loadings, terms), low, high)


def give(sums, low, high):
    half = low.shape[0]
    low[...] = sums[:half]
    high[...] = sums[half:]


def halves_of(count, factors_n):
    return [
        jax.ShapeDtypeStruct((size, factors_n), F32) for size in (count // 2, count - count // 2)
    ]


def cost_of(rows, count, factors_n):
    return pl.CostEstimate(
        flops=2 * rows * count * factors_n,
        bytes_accessed=4 * count * factors_n,
        transcendentals=0,
    )


def tile_of(slots, paths):
    return paths * split_of(slots, max(1, 1280 // paths))


def first_chunk(own, theirs, stats, levels, sigma, ready, ordered, terms):
    slots, paths, factors_n = own.shape
    count = ordered.shape[0]
    half = jax.ShapeDtypeStruct((slots * paths, factors_n), BF16)
    return pl.pallas_call(
        functools.partial(first_kernel, tile_of(slots, paths)),
        in_specs=[VMEM] * 9,
        out_specs=[VMEM] * 4,
        out_shape=[half, half, *halves_of(count, factors_n)],
        compiler_params=small(16),
        cost_estimate=cost_of(2 * slots * paths, count, factors_n),
        name="first_chunk",
    )(own, theirs, stats, levels, sigma, *ready, ordered, terms)


def next_chunk(tile, ready, rest, ordered, terms):
    rows, factors_n = ready[0].shape
    count = ordered.shape[0]
    return pl.pallas_call(
        functools.partial(next_kernel, tile),
        in_specs=[VMEM] * 6,
        out_specs=[VMEM] * 2,
        out_shape=halves_of(count, factors_n),
        compiler_params=small(16),
        cost_estimate=cost_of(2 * rows, count, factors_n),
        name="next_chunk",
    )(*ready, *rest, ordered, terms)


def body(normals, states, loadings, strikes, hedge, sigma, tail):
    groups = lax.axis_size("outer")
    inner = lax.axis_size("inner")
    chips = inner // 2
    _, per_node, factors_n = normals.shape
    instruments = loadings.shape[0]
    tail_count = tail.shape[0]
    paths = per_node * inner
    rows = instruments // (groups * inner)
    paired = chips & (chips - 1) == 0

    relayed = chips == 4 and groups % 2 == 0

    def partner(of, core, d):
        if relayed and d in (1, 2):
            d = d + (3 - 2 * d) * core
        return of ^ d if paired else (of + d) % chips

    def beyond(of, s):
        return of ^ s if groups & (groups - 1) == 0 else (of + s) % groups

    def to_core(x):
        return lax.ppermute(x, "inner", [(i, i ^ 1) for i in range(inner)])

    def to_chip(x, d):
        return lax.ppermute(
            x, "inner", [(i, partner(i // 2, i % 2, d) * 2 + i % 2) for i in range(inner)]
        )

    def to_group(x, s):
        return lax.ppermute(x, "outer", [(g, beyond(g, s)) for g in range(groups)])

    bound = 32768.0 / (tail_count * paths)
    unit = 1.0 / (bound * tail_count * paths)

    tail, normals, states, loadings = (
        pltpu.with_memory_space_constraint(x, pltpu.HBM)
        for x in (tail, normals, states, loadings.reshape(groups * inner, rows, factors_n))
    )
    wide = 128 if 128 % rows == 0 else rows
    strikes, hedge = strikes.reshape(-1, wide), hedge.reshape(-1, wide)

    chosen, mine, other = gather_nodes(tail, normals)
    sums, squares = mine + to_core(other)
    message, within = to_message(sums, squares, 2 * per_node)
    chosen, message, strikes = lax.optimization_barrier((chosen, message, strikes))
    arrived = [to_chip(message, d) for d in range(chips - 1, 0, -1)]
    theirs = to_core(chosen)
    steps = range(groups)
    if relayed:
        half = groups // 2
        low, high = steps[:half], steps[half:]
        plan = [
            [(3, s) for s in steps],
            [(1, s) for s in high] + [(2, s) for s in high],
            [(0, s) for s in steps],
            [(2, s) for s in low] + [(1, s) for s in low],
        ]
    else:
        plan = [[(d, s) for s in steps] for d in range(chips - 1, -1, -1)]
    far = lambda chip, core, d, group, s: (partner(chip, core, d), beyond(group, s))
    levels, live, gain, *parts = order(
        unit, bound, plan, far, tail, states, loadings, strikes, hedge
    )
    ordered = [part.reshape(groups * rows, factors_n) for part in parts[: len(plan)]]
    terms = parts[len(plan) :]
    arrived, theirs, levels, live, gain, ordered, terms = lax.optimization_barrier(
        (arrived, theirs, levels, live, gain, ordered, terms)
    )
    stats = moments(sums, within, arrived, 2 * per_node, live)
    their_stats = to_core(stats)

    sigmas = sigma.reshape(1, factors_n)
    ready = ready_rows(chosen, theirs, stats, levels, sigmas)

    tile = tile_of(CAP, per_node)
    *rest, low, high = first_chunk(
        chosen, theirs, their_stats, levels, sigmas, ready, ordered[0], terms[0]
    )

    def chunk(k, *after):
        kept, _ = lax.optimization_barrier((tuple(rest), after))
        return next_chunk(tile, ready, kept, ordered[k], terms[k])

    def plus(x, y):
        return x + y.astype(F32)

    if relayed:
        a3, b3 = low.astype(F16), high.astype(F16)
        from_b3, from_a3 = to_chip(b3, 1), to_chip(a3, 2)
        b1, b2 = chunk(1, a3, b3)
        b1, b2 = b1.astype(F16), plus(b2, from_b3).astype(F16)
        from_b2, from_b1 = to_chip(b2, 2), to_chip(b1, 1)
        a0, b0 = chunk(2, b1, b2)
        a2, a1 = chunk(3, a0, b0, from_a3)
        a2, a1 = a2.astype(F16), plus(a1, from_a3).astype(F16)
        from_a2, from_a1 = to_chip(a2, 2), to_chip(a1, 1)
        b0, _ = lax.optimization_barrier((b0, (a2, a1)))
        kept = (plus(plus(a0, from_a2), from_a1), plus(plus(b0, from_b1), from_b2))
        part = lambda s: kept[s // half][s % half * rows :][:rows]
    else:
        arrived = []
        for k in range(1, chips):
            sent = jnp.concatenate([low, high]).astype(F16)
            arrived.append(to_chip(sent, chips - k))
            low, high = chunk(k, sent)
        kept = jnp.concatenate([low, high])
        for item in arrived:
            kept = plus(kept, item)
        part = lambda s: kept[s * rows :][:rows]
    owned = part(0)
    for s in sorted(range(1, groups), key=lambda s: (s < groups // 2, s)):
        owned = plus(owned, to_group(part(s).astype(F16), s))
    return gain * owned


def solution(mesh):
    placed = (P("outer", "inner", None), P("outer", None), P(), P(), P(), P(), P())
    return jax.shard_map(
        body, mesh=mesh, in_specs=placed, out_specs=P(("outer", "inner"), None), check_vma=False
    )
```

```python
import functools

import jax
import jax.numpy as jnp
from jax import lax
from jax.experimental import pallas as pl
from jax.experimental.pallas import tpu as pltpu
from jax.sharding import PartitionSpec as P

CAP = 80
EPSILON = 1e-06
VMEM = pl.BlockSpec(memory_space=pltpu.VMEM)
SMEM = pl.BlockSpec(memory_space=pltpu.SMEM)
HBM = pl.BlockSpec(memory_space=pltpu.HBM)
F32 = jnp.float32
BF16 = jnp.bfloat16
F16 = jnp.float16


def split_of(count, most):
    for size in range(min(count, most), 0, -1):
        if count % size == 0:
            return size
    return 1


def small(mebibytes):
    return pltpu.CompilerParams(vmem_limit_bytes=mebibytes << 20)


def first_of(tail, base):
    count = tail.shape[0]
    first = jnp.int32(0)
    for bit in range(count.bit_length() - 1, -1, -1):
        ahead = first + (1 << bit)
        below = tail[jnp.minimum(ahead, count) - 1] < base
        first = jnp.where((ahead <= count) & below, ahead, first)
    return first


def place_of(tail, first, base, slot):
    at = slot + lax.rem(lax.axis_index("inner"), 2) * (CAP // 2)
    at = first + jnp.where(at >= CAP, at - CAP, at)
    node = tail[jnp.minimum(at, tail.shape[0] - 1)] - base
    return node, at < tail.shape[0]


def gather_kernel(
    part, tail_hbm, normals, chosen_hbm, mine, other,
    tail, chosen, tail_sem, sems, out_sem,
):
    node_count = normals.shape[0]
    tail_copy = pltpu.make_async_copy(tail_hbm, tail, tail_sem)
    tail_copy.start()
    base = lax.axis_index("outer") * node_count
    tail_copy.wait()
    first = first_of(tail, base)
    parts = CAP // part

    @pl.loop(0, parts)
    def _(p):
        for k in range(part):
            slot = p * part + k
            node, _ = place_of(tail, first, base, slot)
            node = jnp.minimum(jnp.maximum(node, 0), node_count - 1)
            pltpu.make_async_copy(normals.at[node], chosen.at[slot], sems.at[p]).start()

    out_copy = pltpu.make_async_copy(chosen, chosen_hbm, out_sem)
    for begin, sums in ((0, mine), (parts // 2, other)):

        @pl.loop(0, parts // 2)
        def _(p):
            piece = chosen.at[pl.ds((begin + p) * part, part)]
            pltpu.make_async_copy(piece, piece, sems.at[begin + p]).wait()
            there = chosen_hbm.at[pl.ds((begin + p) * part, part)]
            pltpu.make_async_copy(piece, there, out_sem).start()
            values = piece[...].astype(F32)
            rows = pl.ds(pl.multiple_of(p * part, part), part)
            sums[0, rows, :] = jnp.sum(values, axis=1)
            sums[1, rows, :] = jnp.sum(values * values, axis=1)

    out_copy.wait()


def gather_nodes(tail, normals):
    _, paths, factors_n = normals.shape
    part = split_of(CAP // 2, 8)
    sums = jax.ShapeDtypeStruct((2, CAP // 2, factors_n), F32)
    chosen = (CAP, paths, factors_n)
    return pl.pallas_call(
        functools.partial(gather_kernel, part),
        in_specs=[HBM, HBM],
        out_specs=[HBM, VMEM, VMEM],
        out_shape=[
            pltpu.HBM(chosen, BF16),
            sums,
            sums,
        ],
        scratch_shapes=[
            pltpu.SMEM(tail.shape, jnp.int32),
            pltpu.VMEM(chosen, BF16),
            pltpu.SemaphoreType.DMA,
            pltpu.SemaphoreType.DMA((CAP // part,)),
            pltpu.SemaphoreType.DMA,
        ],
        compiler_params=small(8),
        cost_estimate=pl.CostEstimate(flops=0, bytes_accessed=0, transcendentals=0),
        name="gather_nodes",
    )(tail, normals)


def to_message(sums, within):
    high = sums.astype(F16)
    low = (sums - high.astype(F32)).astype(F16)
    return jnp.stack([high, low, within.astype(F16)])


def pooled(parts, count):
    total = sum(s for s, _ in parts)
    center = total / (count * len(parts))
    return total, sum(w + (s / count - center) ** 2 * count for s, w in parts)


def of_message(message):
    high, low, within = message.astype(F32)
    return high + low, within


def order_kernel(
    unit, bound, plan, far, tail_hbm, states_hbm, loadings_hbm, strikes, hedge,
    levels, live, gain, *refs,
):
    chunks, steps, rows = len(plan), len(plan[0]), gain.shape[0]
    ordered, terms = refs[:chunks], refs[chunks : 2 * chunks]
    tail, states, onehot, own, tail_sem, states_sem, sems = refs[2 * chunks :]
    node_count = states.shape[0]
    position = lax.axis_index("inner")
    group, chip, core = lax.axis_index("outer"), position // 2, lax.rem(position, 2)
    tail_copy = pltpu.make_async_copy(tail_hbm, tail, tail_sem)
    states_copy = pltpu.make_async_copy(states_hbm, states, states_sem)
    tail_copy.start()
    states_copy.start()
    blocks, copies = [], []
    for chunk in range(chunks):
        for step in range(steps):
            d, away = plan[chunk][step]
            to_chip, to_group = far(chip, d, group, away)
            block = (to_group * chunks + to_chip) * 2 + core
            k = chunk * steps + step
            copy = pltpu.make_async_copy(loadings_hbm.at[block], own.at[k], sems.at[k])
            copy.start()
            blocks.append(block)
            copies.append(copy)
    wide = strikes.shape[1]
    lanes = lax.broadcasted_iota(jnp.int32, (rows, wide), 1)
    lines = lax.broadcasted_iota(jnp.int32, (rows, wide), 0)

    def column(ref, block):
        line = ref[pl.ds(block * rows // wide, 1), :]
        here = lanes == lines + lax.rem(block * rows, wide)
        return jnp.sum(jnp.where(here, line, 0.0), axis=1, keepdims=True)

    for k, block in enumerate(blocks):
        chunk, step = k // steps, k % steps
        at = slice(step * rows, (step + 1) * rows)
        size = column(hedge, block)
        scale = jnp.abs(size)
        terms[chunk][at, 0:1] = column(strikes, block) * 0.5
        terms[chunk][at, 1:2] = size * 0.5
        terms[chunk][at, 2:3] = jnp.where(
            scale > 1e-30, bound / jnp.maximum(scale, 1e-30), 0.0
        )
        if plan[chunk][step] == (0, 0):
            owned = scale * unit
    tail_copy.wait()
    base = group * node_count
    first = first_of(tail, base)
    nodes = lax.broadcasted_iota(jnp.int32, (1, node_count), 1)
    for slot in range(CAP):
        node, inside = place_of(tail, first, base, slot)
        used = inside & (node >= 0) & (node < node_count)
        onehot[slot : slot + 1, :] = ((nodes == node) & used).astype(F32)
        if slot < CAP // 2:
            live[slot : slot + 1, :] = jnp.full((1, live.shape[1]), used.astype(F32))
    states_copy.wait()
    levels[...] = jnp.dot(
        onehot[...].astype(BF16), states[...], preferred_element_type=F32
    )
    for k, copy in enumerate(copies):
        copy.wait()
        values = own[k].astype(F32)
        if plan[k // steps][k % steps] == (0, 0):
            gain[...] = values * owned
        ordered[k // steps][k % steps] = (values * 0.5).astype(BF16)


def order(unit, bound, plan, far, tail, states, loadings, strikes, hedge):
    chunks, steps = len(plan), len(plan[0])
    _, rows, factors_n = loadings.shape
    return pl.pallas_call(
        functools.partial(order_kernel, unit, bound, plan, far),
        in_specs=[HBM] * 3 + [VMEM] * 2,
        out_specs=[VMEM] * (2 * chunks + 3),
        out_shape=[
            jax.ShapeDtypeStruct((count, factors_n), F32) for count in (CAP, CAP // 2, rows)
        ]
        + [jax.ShapeDtypeStruct((steps, rows, factors_n), BF16)] * chunks
        + [jax.ShapeDtypeStruct((steps * rows, 3), F32)] * chunks,
        scratch_shapes=[
            pltpu.SMEM(tail.shape, jnp.int32),
            pltpu.VMEM(states.shape, BF16),
            pltpu.VMEM((CAP, states.shape[0]), F32),
            pltpu.VMEM((chunks * steps, rows, factors_n), BF16),
            pltpu.SemaphoreType.DMA,
            pltpu.SemaphoreType.DMA,
            pltpu.SemaphoreType.DMA((chunks * steps,)),
        ],
        compiler_params=small(12),
        cost_estimate=pl.CostEstimate(flops=0, bytes_accessed=1 << 20, transcendentals=0),
        name="order_instruments",
    )(tail, states, loadings, strikes, hedge)


def prepare(own, theirs, stats, levels, sigma, scaled, factors, ready, begin, end):
    slots, paths, factors_n = own.shape
    half = slots // 2
    shape = (paths, factors_n)
    sigmas = jnp.broadcast_to(sigma[...], shape)
    for at in range(begin, end):
        mine, row = at < half, at % half
        slot = row if mine == ready else row + half
        source = own if mine else theirs
        place = slot if mine else (slot + half) % slots
        center = jnp.broadcast_to(stats[0, row : row + 1, :], shape)
        rstd = jnp.broadcast_to(stats[1, row : row + 1, :], shape)
        level = jnp.broadcast_to(levels[place : place + 1, :], shape)
        unit = ((source[slot].astype(F32) - center) * rstd).astype(BF16)
        rows = slice(at * paths, (at + 1) * paths)
        scaled[rows, :] = unit
        factors[rows, :] = (level + sigmas * unit.astype(F32)).astype(BF16)


def ready_kernel(own, theirs, stats, levels, sigma, loadings, terms, scaled, factors, out):
    slots, paths, _ = own.shape
    prepare(own, theirs, stats, levels, sigma, scaled, factors, True, 0, slots)
    out[...] = cross_of(slots * paths, ((scaled, factors),), loadings, terms)


def ready_rows(own, theirs, stats, levels, sigma, ordered, terms):
    slots, paths, factors_n = own.shape
    rows = slots * paths
    count = ordered.shape[0]
    half = jax.ShapeDtypeStruct((rows, factors_n), BF16)
    return pl.pallas_call(
        ready_kernel,
        in_specs=[VMEM] * 7,
        out_specs=[VMEM] * 3,
        out_shape=[half, half, jax.ShapeDtypeStruct((count, factors_n), F32)],
        compiler_params=small(16),
        cost_estimate=cost_of(rows, count, factors_n),
        name="ready_rows",
    )(own, theirs, stats, levels, sigma, ordered, terms)


def cross_of(tile, halves, loadings, terms):
    strikes, hedge, scale = terms[:, 0:1], terms[:, 1:2], terms[:, 2:3]
    part = loadings[...]
    each = halves[0][0].shape[0] // tile
    places = [(half, r * tile) for half in range(len(halves)) for r in range(each)]

    def level(half, at):
        rows = halves[half][1][at : at + tile, :]
        return lax.dot_general(
            part, rows, (((1,), (1,)), ((), ())), preferred_element_type=F32
        )

    total = None
    current = level(*places[0])
    for k, (half, at) in enumerate(places):
        after = level(*places[k + 1]) if k + 1 < len(places) else None
        weight = (jnp.tanh(current - strikes) * hedge + hedge).astype(BF16)
        cross = jnp.dot(
            weight, halves[half][0][at : at + tile, :], preferred_element_type=F32
        )
        total = cross if total is None else total + cross
        current = after
    return total * scale


def first_kernel(
    own, theirs, stats, levels, sigma, done, loadings, terms, scaled, factors, low, high
):
    slots, paths, _ = own.shape
    prepare(own, theirs, stats, levels, sigma, scaled, factors, False, 0, slots)
    sums = cross_of(slots * paths, ((scaled, factors),), loadings, terms)
    give(done[...] + sums, low, high)


def next_kernel(tile, s0, f0, s1, f1, loadings, terms, low, high):
    give(cross_of(tile, ((s0, f0), (s1, f1)), loadings, terms), low, high)


def give(sums, low, high):
    half = low.shape[0]
    low[...] = sums[:half]
    high[...] = sums[half:]


def halves_of(count, factors_n):
    return [
        jax.ShapeDtypeStruct((size, factors_n), F32) for size in (count // 2, count - count // 2)
    ]


def cost_of(rows, count, factors_n):
    return pl.CostEstimate(
        flops=2 * rows * count * factors_n,
        bytes_accessed=4 * count * factors_n,
        transcendentals=0,
    )


def tile_of(slots, paths):
    return paths * split_of(slots, max(1, 1280 // paths))


def first_chunk(own, theirs, stats, levels, sigma, done, ordered, terms):
    slots, paths, factors_n = own.shape
    count = ordered.shape[0]
    half = jax.ShapeDtypeStruct((slots * paths, factors_n), BF16)
    return pl.pallas_call(
        first_kernel,
        in_specs=[VMEM] * 8,
        out_specs=[VMEM] * 4,
        out_shape=[half, half, *halves_of(count, factors_n)],
        compiler_params=small(16),
        cost_estimate=cost_of(slots * paths, count, factors_n),
        name="first_chunk",
    )(own, theirs, stats, levels, sigma, done, ordered, terms)


def next_chunk(tile, ready, rest, ordered, terms):
    rows, factors_n = ready[0].shape
    count = ordered.shape[0]
    return pl.pallas_call(
        functools.partial(next_kernel, tile),
        in_specs=[VMEM] * 6,
        out_specs=[VMEM] * 2,
        out_shape=halves_of(count, factors_n),
        compiler_params=small(16),
        cost_estimate=cost_of(2 * rows, count, factors_n),
        name="next_chunk",
    )(*ready, *rest, ordered, terms)


def body(normals, states, loadings, strikes, hedge, sigma, tail):
    groups = lax.axis_size("outer")
    inner = lax.axis_size("inner")
    chips = inner // 2
    _, per_node, factors_n = normals.shape
    instruments = loadings.shape[0]
    tail_count = tail.shape[0]
    paths = per_node * inner
    rows = instruments // (groups * inner)
    paired = chips & (chips - 1) == 0

    def partner(of, d):
        return of ^ d if paired else (of + d) % chips

    def beyond(of, s):
        return of ^ s if groups & (groups - 1) == 0 else (of + s) % groups

    def to_core(x):
        return lax.ppermute(x, "inner", [(i, i ^ 1) for i in range(inner)])

    def to_chip(x, d, mirror=0):
        return lax.ppermute(
            x,
            "inner",
            [(i, partner(i // 2, d + mirror * (i % 2)) * 2 + i % 2) for i in range(inner)],
        )

    def to_group(x, s):
        return lax.ppermute(x, "outer", [(g, beyond(g, s)) for g in range(groups)])

    bound = 32768.0 / (tail_count * paths)
    unit = 1.0 / (bound * tail_count * paths)

    tail, normals, states, loadings = (
        pltpu.with_memory_space_constraint(x, pltpu.HBM)
        for x in (tail, normals, states, loadings.reshape(groups * inner, rows, factors_n))
    )
    wide = 128 if 128 % rows == 0 else rows
    strikes, hedge = strikes.reshape(-1, wide), hedge.reshape(-1, wide)

    chosen, mine, other = gather_nodes(tail, normals)
    sums, squares = mine + to_core(other)
    count = 2 * per_node
    within = squares - sums * sums / count
    message = to_message(sums, within)
    chosen, message, strikes = lax.optimization_barrier((chosen, message, strikes))
    rounds = [1 << k for k in range(chips.bit_length() - 1)] if paired else []
    if not paired:
        arrived = [of_message(to_chip(message, d)) for d in range(chips - 1, 0, -1)]
        sums, within = pooled([(sums, within), *arrived], count)
        count *= chips
    for d in rounds:
        mirror = 3 - 2 * d if chips == 4 else 0
        arrived = to_chip(message, d, mirror)
        sums, within = pooled([(sums, within), of_message(arrived)], count)
        count *= 2
        if d != rounds[-1]:
            message = to_message(sums, within)
    theirs = to_core(chosen)
    steps = range(groups)
    relayed = chips == 4 and groups % 2 == 0
    if relayed:
        half = groups // 2
        low, high = steps[:half], steps[half:]
        plan = [
            [(3, s) for s in steps],
            [(1, s) for s in high] + [(2, s) for s in high],
            [(0, s) for s in steps],
            [(2, s) for s in low] + [(1, s) for s in low],
        ]
    else:
        plan = [[(d, s) for s in steps] for d in range(chips - 1, -1, -1)]
    far = lambda chip, d, group, s: (partner(chip, d), beyond(group, s))
    levels, live, gain, *parts = order(
        unit, bound, plan, far, tail, states, loadings, strikes, hedge
    )
    ordered = [part.reshape(groups * rows, factors_n) for part in parts[: len(plan)]]
    terms = parts[len(plan) :]
    sums, within, theirs, levels, live, gain, ordered, terms = lax.optimization_barrier(
        (sums, within, theirs, levels, live, gain, ordered, terms)
    )
    stats = jnp.stack([sums / count, live * lax.rsqrt(within / count + EPSILON)])
    their_stats = to_core(stats)

    sigmas = sigma.reshape(1, factors_n)
    *ready, done = ready_rows(chosen, theirs, stats, levels, sigmas, ordered[0], terms[0])

    tile = tile_of(CAP, per_node)
    *rest, low, high = first_chunk(
        chosen, theirs, their_stats, levels, sigmas, done, ordered[0], terms[0]
    )

    def chunk(k, *after):
        kept, _ = lax.optimization_barrier((tuple(rest), after))
        return next_chunk(tile, ready, kept, ordered[k], terms[k])

    def plus(x, y):
        return x + y.astype(F32)

    if relayed:
        a3, b3 = low.astype(F16), high.astype(F16)
        from_b3, from_a3 = to_chip(b3, 1), to_chip(a3, 2)
        b1, b2 = chunk(1, a3, b3)
        b1, b2 = b1.astype(F16), plus(b2, from_b3).astype(F16)
        from_b1, from_b2 = to_chip(b1, 1), to_chip(b2, 2)
        a0, b0 = chunk(2, b1, b2)
        a2, a1 = chunk(3, a0, b0, from_a3)
        a2, a1 = a2.astype(F16), plus(a1, from_a3).astype(F16)
        from_a2, from_a1 = to_chip(a2, 2), to_chip(a1, 1)
        b0, _ = lax.optimization_barrier((b0, (a2, a1)))
        kept = (plus(plus(a0, from_a2), from_a1), plus(plus(b0, from_b1), from_b2))
        part = lambda s: kept[s // half][s % half * rows :][:rows]
    else:
        arrived = []
        for k in range(1, chips):
            sent = jnp.concatenate([low, high]).astype(F16)
            arrived.append(to_chip(sent, chips - k))
            low, high = chunk(k, sent)
        kept = jnp.concatenate([low, high])
        for item in arrived:
            kept = plus(kept, item)
        part = lambda s: kept[s * rows :][:rows]
    owned = part(0)
    for s in sorted(range(1, groups), key=lambda s: (s < groups // 2, s)):
        owned = plus(owned, to_group(part(s).astype(F16), s))
    return gain * owned


def solution(mesh):
    placed = (P("outer", "inner", None), P("outer", None), P(), P(), P(), P(), P())
    return jax.shard_map(
        body, mesh=mesh, in_specs=placed, out_specs=P(("outer", "inner"), None), check_vma=False
    )
```

```python
import functools

import jax
import jax.numpy as jnp
from jax import lax
from jax.experimental import pallas as pl
from jax.experimental.pallas import tpu as pltpu
from jax.sharding import PartitionSpec as P

CAP = 80
EPSILON = 1e-06
VMEM = pl.BlockSpec(memory_space=pltpu.VMEM)
SMEM = pl.BlockSpec(memory_space=pltpu.SMEM)
HBM = pl.BlockSpec(memory_space=pltpu.HBM)
F32 = jnp.float32
BF16 = jnp.bfloat16
F16 = jnp.float16


def split_of(count, most):
    for size in range(min(count, most), 0, -1):
        if count % size == 0:
            return size
    return 1


def small(mebibytes):
    return pltpu.CompilerParams(vmem_limit_bytes=mebibytes << 20)


def first_of(tail, base):
    count = tail.shape[0]
    first = jnp.int32(0)
    for bit in range(count.bit_length() - 1, -1, -1):
        ahead = first + (1 << bit)
        below = tail[jnp.minimum(ahead, count) - 1] < base
        first = jnp.where((ahead <= count) & below, ahead, first)
    return first


def place_of(tail, first, base, slot):
    at = slot + lax.rem(lax.axis_index("inner"), 2) * (CAP // 2)
    at = first + jnp.where(at >= CAP, at - CAP, at)
    node = tail[jnp.minimum(at, tail.shape[0] - 1)] - base
    return node, at < tail.shape[0]


def gather_kernel(
    part, tail_hbm, normals, chosen_hbm, mine, other,
    tail, chosen, tail_sem, sems, out_sem,
):
    node_count = normals.shape[0]
    tail_copy = pltpu.make_async_copy(tail_hbm, tail, tail_sem)
    tail_copy.start()
    base = lax.axis_index("outer") * node_count
    tail_copy.wait()
    first = first_of(tail, base)
    parts = CAP // part

    @pl.loop(0, parts)
    def _(p):
        for k in range(part):
            slot = p * part + k
            node, _ = place_of(tail, first, base, slot)
            node = jnp.minimum(jnp.maximum(node, 0), node_count - 1)
            pltpu.make_async_copy(normals.at[node], chosen.at[slot], sems.at[p]).start()

    out_copy = pltpu.make_async_copy(chosen, chosen_hbm, out_sem)
    for begin, sums in ((0, mine), (parts // 2, other)):

        @pl.loop(0, parts // 2)
        def _(p):
            piece = chosen.at[pl.ds((begin + p) * part, part)]
            pltpu.make_async_copy(piece, piece, sems.at[begin + p]).wait()
            there = chosen_hbm.at[pl.ds((begin + p) * part, part)]
            pltpu.make_async_copy(piece, there, out_sem).start()
            values = piece[...].astype(F32)
            rows = pl.ds(pl.multiple_of(p * part, part), part)
            sums[0, rows, :] = jnp.sum(values, axis=1)
            sums[1, rows, :] = jnp.sum(values * values, axis=1)

    out_copy.wait()


def gather_nodes(tail, normals):
    _, paths, factors_n = normals.shape
    part = split_of(CAP // 2, 8)
    sums = jax.ShapeDtypeStruct((2, CAP // 2, factors_n), F32)
    chosen = (CAP, paths, factors_n)
    return pl.pallas_call(
        functools.partial(gather_kernel, part),
        in_specs=[HBM, HBM],
        out_specs=[HBM, VMEM, VMEM],
        out_shape=[
            pltpu.HBM(chosen, BF16),
            sums,
            sums,
        ],
        scratch_shapes=[
            pltpu.SMEM(tail.shape, jnp.int32),
            pltpu.VMEM(chosen, BF16),
            pltpu.SemaphoreType.DMA,
            pltpu.SemaphoreType.DMA((CAP // part,)),
            pltpu.SemaphoreType.DMA,
        ],
        compiler_params=small(8),
        cost_estimate=pl.CostEstimate(flops=0, bytes_accessed=0, transcendentals=0),
        name="gather_nodes",
    )(tail, normals)


def to_message(sums, within):
    high = sums.astype(F16)
    low = (sums - high.astype(F32)).astype(F16)
    return jnp.stack([high, low, within.astype(F16)])


def pooled(parts, count):
    total = sum(s for s, _ in parts)
    center = total / (count * len(parts))
    return total, sum(w + (s / count - center) ** 2 * count for s, w in parts)


def of_message(message):
    high, low, within = message.astype(F32)
    return high + low, within


def order_kernel(
    unit, bound, plan, far, tail_hbm, states_hbm, loadings_hbm, strikes, hedge,
    levels, live, gain, *refs,
):
    chunks, steps, rows = len(plan), len(plan[0]), gain.shape[0]
    ordered, terms = refs[:chunks], refs[chunks : 2 * chunks]
    tail, states, onehot, own, tail_sem, states_sem, sems = refs[2 * chunks :]
    node_count = states.shape[0]
    position = lax.axis_index("inner")
    group, chip, core = lax.axis_index("outer"), position // 2, lax.rem(position, 2)
    tail_copy = pltpu.make_async_copy(tail_hbm, tail, tail_sem)
    states_copy = pltpu.make_async_copy(states_hbm, states, states_sem)
    tail_copy.start()
    states_copy.start()
    blocks, copies = [], []
    for chunk in range(chunks):
        for step in range(steps):
            d, away = plan[chunk][step]
            to_chip, to_group = far(chip, d, group, away)
            block = (to_group * chunks + to_chip) * 2 + core
            k = chunk * steps + step
            copy = pltpu.make_async_copy(loadings_hbm.at[block], own.at[k], sems.at[k])
            copy.start()
            blocks.append(block)
            copies.append(copy)
    wide = strikes.shape[1]
    lanes = lax.broadcasted_iota(jnp.int32, (rows, wide), 1)
    lines = lax.broadcasted_iota(jnp.int32, (rows, wide), 0)

    def column(ref, block):
        line = ref[pl.ds(block * rows // wide, 1), :]
        here = lanes == lines + lax.rem(block * rows, wide)
        return jnp.sum(jnp.where(here, line, 0.0), axis=1, keepdims=True)

    for k, block in enumerate(blocks):
        chunk, step = k // steps, k % steps
        at = slice(step * rows, (step + 1) * rows)
        size = column(hedge, block)
        scale = jnp.abs(size)
        terms[chunk][at, 0:1] = column(strikes, block) * 0.5
        terms[chunk][at, 1:2] = size * 0.5
        terms[chunk][at, 2:3] = jnp.where(
            scale > 1e-30, bound / jnp.maximum(scale, 1e-30), 0.0
        )
        if plan[chunk][step] == (0, 0):
            owned = scale * unit
    tail_copy.wait()
    base = group * node_count
    first = first_of(tail, base)
    nodes = lax.broadcasted_iota(jnp.int32, (1, node_count), 1)
    for slot in range(CAP):
        node, inside = place_of(tail, first, base, slot)
        used = inside & (node >= 0) & (node < node_count)
        onehot[slot : slot + 1, :] = ((nodes == node) & used).astype(F32)
        if slot < CAP // 2:
            live[slot : slot + 1, :] = jnp.full((1, live.shape[1]), used.astype(F32))
    states_copy.wait()
    levels[...] = jnp.dot(
        onehot[...].astype(BF16), states[...], preferred_element_type=F32
    )
    for k, copy in enumerate(copies):
        copy.wait()
        values = own[k].astype(F32)
        if plan[k // steps][k % steps] == (0, 0):
            gain[...] = values * owned
        ordered[k // steps][k % steps] = (values * 0.5).astype(BF16)


def order(unit, bound, plan, far, tail, states, loadings, strikes, hedge):
    chunks, steps = len(plan), len(plan[0])
    _, rows, factors_n = loadings.shape
    return pl.pallas_call(
        functools.partial(order_kernel, unit, bound, plan, far),
        in_specs=[HBM] * 3 + [VMEM] * 2,
        out_specs=[VMEM] * (2 * chunks + 3),
        out_shape=[
            jax.ShapeDtypeStruct((count, factors_n), F32) for count in (CAP, CAP // 2, rows)
        ]
        + [jax.ShapeDtypeStruct((steps, rows, factors_n), BF16)] * chunks
        + [jax.ShapeDtypeStruct((steps * rows, 3), F32)] * chunks,
        scratch_shapes=[
            pltpu.SMEM(tail.shape, jnp.int32),
            pltpu.VMEM(states.shape, BF16),
            pltpu.VMEM((CAP, states.shape[0]), F32),
            pltpu.VMEM((chunks * steps, rows, factors_n), BF16),
            pltpu.SemaphoreType.DMA,
            pltpu.SemaphoreType.DMA,
            pltpu.SemaphoreType.DMA((chunks * steps,)),
        ],
        compiler_params=small(12),
        cost_estimate=pl.CostEstimate(flops=0, bytes_accessed=1 << 20, transcendentals=0),
        name="order_instruments",
    )(tail, states, loadings, strikes, hedge)


def prepare(own, theirs, stats, levels, sigma, scaled, factors, ready, begin, end):
    slots, paths, factors_n = own.shape
    half = slots // 2
    shape = (paths, factors_n)
    sigmas = jnp.broadcast_to(sigma[...], shape)
    for at in range(begin, end):
        mine, row = at < half, at % half
        slot = row if mine == ready else row + half
        source = own if mine else theirs
        place = slot if mine else (slot + half) % slots
        center = jnp.broadcast_to(stats[0, row : row + 1, :], shape)
        rstd = jnp.broadcast_to(stats[1, row : row + 1, :], shape)
        level = jnp.broadcast_to(levels[place : place + 1, :], shape)
        unit = ((source[slot].astype(F32) - center) * rstd).astype(BF16)
        rows = slice(at * paths, (at + 1) * paths)
        scaled[rows, :] = unit
        factors[rows, :] = (level + sigmas * unit.astype(F32)).astype(BF16)


def ready_kernel(own, theirs, stats, levels, sigma, loadings, terms, scaled, factors, out):
    slots, paths, _ = own.shape
    prepare(own, theirs, stats, levels, sigma, scaled, factors, True, 0, slots)
    out[...] = cross_of(slots * paths, ((scaled, factors),), loadings, terms)


def ready_rows(own, theirs, stats, levels, sigma, ordered, terms):
    slots, paths, factors_n = own.shape
    rows = slots * paths
    count = ordered.shape[0]
    half = jax.ShapeDtypeStruct((rows, factors_n), BF16)
    return pl.pallas_call(
        ready_kernel,
        in_specs=[VMEM] * 7,
        out_specs=[VMEM] * 3,
        out_shape=[half, half, jax.ShapeDtypeStruct((count, factors_n), F32)],
        compiler_params=small(16),
        cost_estimate=cost_of(rows, count, factors_n),
        name="ready_rows",
    )(own, theirs, stats, levels, sigma, ordered, terms)


def cross_of(tile, halves, loadings, terms):
    strikes, hedge, scale = terms[:, 0:1], terms[:, 1:2], terms[:, 2:3]
    part = loadings[...]
    each = halves[0][0].shape[0] // tile
    places = [(half, r * tile) for half in range(len(halves)) for r in range(each)]

    def level(half, at):
        rows = halves[half][1][at : at + tile, :]
        return lax.dot_general(
            part, rows, (((1,), (1,)), ((), ())), preferred_element_type=F32
        )

    total = None
    current = level(*places[0])
    for k, (half, at) in enumerate(places):
        after = level(*places[k + 1]) if k + 1 < len(places) else None
        weight = (jnp.tanh(current - strikes) * hedge + hedge).astype(BF16)
        cross = jnp.dot(
            weight, halves[half][0][at : at + tile, :], preferred_element_type=F32
        )
        total = cross if total is None else total + cross
        current = after
    return total * scale


def first_kernel(
    own, theirs, stats, levels, sigma, done, loadings, terms, scaled, factors, low, high
):
    slots, paths, _ = own.shape
    prepare(own, theirs, stats, levels, sigma, scaled, factors, False, 0, slots)
    sums = cross_of(slots * paths, ((scaled, factors),), loadings, terms)
    give(done[...] + sums, low, high)


def next_kernel(tile, s0, f0, s1, f1, loadings, terms, low, high):
    give(cross_of(tile, ((s0, f0), (s1, f1)), loadings, terms), low, high)


def give(sums, low, high):
    half = low.shape[0]
    low[...] = sums[:half]
    high[...] = sums[half:]


def halves_of(count, factors_n):
    return [
        jax.ShapeDtypeStruct((size, factors_n), F32) for size in (count // 2, count - count // 2)
    ]


def cost_of(rows, count, factors_n):
    return pl.CostEstimate(
        flops=2 * rows * count * factors_n,
        bytes_accessed=4 * count * factors_n,
        transcendentals=0,
    )


def tile_of(slots, paths):
    return paths * split_of(slots, max(1, 1280 // paths))


def first_chunk(own, theirs, stats, levels, sigma, done, ordered, terms):
    slots, paths, factors_n = own.shape
    count = ordered.shape[0]
    half = jax.ShapeDtypeStruct((slots * paths, factors_n), BF16)
    return pl.pallas_call(
        first_kernel,
        in_specs=[VMEM] * 8,
        out_specs=[VMEM] * 4,
        out_shape=[half, half, *halves_of(count, factors_n)],
        compiler_params=small(16),
        cost_estimate=cost_of(slots * paths, count, factors_n),
        name="first_chunk",
    )(own, theirs, stats, levels, sigma, done, ordered, terms)


def next_chunk(tile, ready, rest, ordered, terms):
    rows, factors_n = ready[0].shape
    count = ordered.shape[0]
    return pl.pallas_call(
        functools.partial(next_kernel, tile),
        in_specs=[VMEM] * 6,
        out_specs=[VMEM] * 2,
        out_shape=halves_of(count, factors_n),
        compiler_params=small(16),
        cost_estimate=cost_of(2 * rows, count, factors_n),
        name="next_chunk",
    )(*ready, *rest, ordered, terms)


def body(normals, states, loadings, strikes, hedge, sigma, tail):
    groups = lax.axis_size("outer")
    inner = lax.axis_size("inner")
    chips = inner // 2
    _, per_node, factors_n = normals.shape
    instruments = loadings.shape[0]
    tail_count = tail.shape[0]
    paths = per_node * inner
    rows = instruments // (groups * inner)
    paired = chips & (chips - 1) == 0

    def partner(of, d):
        return of ^ d if paired else (of + d) % chips

    def beyond(of, s):
        return of ^ s if groups & (groups - 1) == 0 else (of + s) % groups

    def to_core(x):
        return lax.ppermute(x, "inner", [(i, i ^ 1) for i in range(inner)])

    def to_chip(x, d):
        return lax.ppermute(
            x, "inner", [(i, partner(i // 2, d) * 2 + i % 2) for i in range(inner)]
        )

    def to_group(x, s):
        return lax.ppermute(x, "outer", [(g, beyond(g, s)) for g in range(groups)])

    bound = 32768.0 / (tail_count * paths)
    unit = 1.0 / (bound * tail_count * paths)

    tail, normals, states, loadings = (
        pltpu.with_memory_space_constraint(x, pltpu.HBM)
        for x in (tail, normals, states, loadings.reshape(groups * inner, rows, factors_n))
    )
    wide = 128 if 128 % rows == 0 else rows
    strikes, hedge = strikes.reshape(-1, wide), hedge.reshape(-1, wide)

    chosen, mine, other = gather_nodes(tail, normals)
    sums, squares = mine + to_core(other)
    count = 2 * per_node
    within = squares - sums * sums / count
    message = to_message(sums, within)
    chosen, message, strikes = lax.optimization_barrier((chosen, message, strikes))
    rounds = [1 << k for k in range(chips.bit_length() - 1)] if paired and chips > 4 else []
    if not rounds:
        arrived = [of_message(to_chip(message, d)) for d in range(chips - 1, 0, -1)]
        sums, within = pooled([(sums, within), *arrived], count)
        count *= chips
    for d in rounds:
        arrived = to_chip(message, d)
        sums, within = pooled([(sums, within), of_message(arrived)], count)
        count *= 2
        if d != rounds[-1]:
            message = to_message(sums, within)
    theirs = to_core(chosen)
    steps = range(groups)
    relayed = chips == 4 and groups % 2 == 0
    if relayed:
        half = groups // 2
        low, high = steps[:half], steps[half:]
        plan = [
            [(3, s) for s in steps],
            [(1, s) for s in high] + [(2, s) for s in high],
            [(0, s) for s in steps],
            [(2, s) for s in low] + [(1, s) for s in low],
        ]
    else:
        plan = [[(d, s) for s in steps] for d in range(chips - 1, -1, -1)]
    far = lambda chip, d, group, s: (partner(chip, d), beyond(group, s))
    levels, live, gain, *parts = order(
        unit, bound, plan, far, tail, states, loadings, strikes, hedge
    )
    ordered = [part.reshape(groups * rows, factors_n) for part in parts[: len(plan)]]
    terms = parts[len(plan) :]
    sums, within, theirs, levels, live, gain, ordered, terms = lax.optimization_barrier(
        (sums, within, theirs, levels, live, gain, ordered, terms)
    )
    stats = jnp.stack([sums / count, live * lax.rsqrt(within / count + EPSILON)])
    their_stats = to_core(stats)

    sigmas = sigma.reshape(1, factors_n)
    *ready, done = ready_rows(chosen, theirs, stats, levels, sigmas, ordered[0], terms[0])

    tile = tile_of(CAP, per_node)
    *rest, low, high = first_chunk(
        chosen, theirs, their_stats, levels, sigmas, done, ordered[0], terms[0]
    )

    def chunk(k, *after):
        kept, _ = lax.optimization_barrier((tuple(rest), after))
        return next_chunk(tile, ready, kept, ordered[k], terms[k])

    def plus(x, y):
        return x + y.astype(F32)

    if relayed:
        a3, b3 = low.astype(F16), high.astype(F16)
        from_b3, from_a3 = to_chip(b3, 1), to_chip(a3, 2)
        b1, b2 = chunk(1, a3, b3)
        b1, b2 = b1.astype(F16), plus(b2, from_b3).astype(F16)
        b1, b2 = lax.optimization_barrier((b1, b2))
        from_b1, from_b2 = to_chip(b1, 1), to_chip(b2, 2)
        a0, b0 = chunk(2, b1, b2)
        a2, a1 = chunk(3, a0, b0, from_a3)
        a2, a1 = a2.astype(F16), plus(a1, from_a3).astype(F16)
        from_a2, from_a1 = to_chip(a2, 2), to_chip(a1, 1)
        b0, _ = lax.optimization_barrier((b0, (a2, a1)))
        kept = (plus(plus(a0, from_a2), from_a1), plus(plus(b0, from_b1), from_b2))
        part = lambda s: kept[s // half][s % half * rows :][:rows]
    else:
        arrived = []
        for k in range(1, chips):
            sent = jnp.concatenate([low, high]).astype(F16)
            arrived.append(to_chip(sent, chips - k))
            low, high = chunk(k, sent)
        kept = jnp.concatenate([low, high])
        for item in arrived:
            kept = plus(kept, item)
        part = lambda s: kept[s * rows :][:rows]
    owned = part(0)
    for s in sorted(range(1, groups), key=lambda s: (s < groups // 2, s)):
        owned = plus(owned, to_group(part(s).astype(F16), s))
    return gain * owned


def solution(mesh):
    placed = (P("outer", "inner", None), P("outer", None), P(), P(), P(), P(), P())
    return jax.shard_map(
        body, mesh=mesh, in_specs=placed, out_specs=P(("outer", "inner"), None), check_vma=False
    )
```

```python
import functools

import jax
import jax.numpy as jnp
from jax import lax
from jax.experimental import pallas as pl
from jax.experimental.pallas import tpu as pltpu
from jax.sharding import PartitionSpec as P

CAP = 80
EPSILON = 1e-06
VMEM = pl.BlockSpec(memory_space=pltpu.VMEM)
SMEM = pl.BlockSpec(memory_space=pltpu.SMEM)
HBM = pl.BlockSpec(memory_space=pltpu.HBM)
F32 = jnp.float32
BF16 = jnp.bfloat16
F16 = jnp.float16


def split_of(count, most):
    for size in range(min(count, most), 0, -1):
        if count % size == 0:
            return size
    return 1


def small(mebibytes):
    return pltpu.CompilerParams(vmem_limit_bytes=mebibytes << 20)


def first_of(tail, base):
    count = tail.shape[0]
    first = jnp.int32(0)
    for bit in range(count.bit_length() - 1, -1, -1):
        ahead = first + (1 << bit)
        below = tail[jnp.minimum(ahead, count) - 1] < base
        first = jnp.where((ahead <= count) & below, ahead, first)
    return first


def place_of(tail, first, base, slot):
    at = slot + lax.rem(lax.axis_index("inner"), 2) * (CAP // 2)
    at = first + jnp.where(at >= CAP, at - CAP, at)
    node = tail[jnp.minimum(at, tail.shape[0] - 1)] - base
    return node, at < tail.shape[0]


def gather_kernel(
    part, tail_hbm, normals, chosen_hbm, mine, other,
    tail, chosen, tail_sem, sems, out_sem,
):
    node_count = normals.shape[0]
    tail_copy = pltpu.make_async_copy(tail_hbm, tail, tail_sem)
    tail_copy.start()
    base = lax.axis_index("outer") * node_count
    tail_copy.wait()
    first = first_of(tail, base)
    parts = CAP // part

    @pl.loop(0, parts)
    def _(p):
        for k in range(part):
            slot = p * part + k
            node, inside = place_of(tail, first, base, slot)
            used = inside & (node >= 0) & (node < node_count)
            node = jnp.where(used, node, lax.rem(slot, node_count))
            pltpu.make_async_copy(normals.at[node], chosen.at[slot], sems.at[p]).start()

    out_copy = pltpu.make_async_copy(chosen, chosen_hbm, out_sem)
    for begin, sums in ((0, mine), (parts // 2, other)):

        @pl.loop(0, parts // 2)
        def _(p):
            piece = chosen.at[pl.ds((begin + p) * part, part)]
            pltpu.make_async_copy(piece, piece, sems.at[begin + p]).wait()
            there = chosen_hbm.at[pl.ds((begin + p) * part, part)]
            pltpu.make_async_copy(piece, there, out_sem).start()
            values = piece[...].astype(F32)
            rows = pl.ds(pl.multiple_of(p * part, part), part)
            sums[0, rows, :] = jnp.sum(values, axis=1)
            sums[1, rows, :] = jnp.sum(values * values, axis=1)

    out_copy.wait()


def gather_nodes(tail, normals):
    _, paths, factors_n = normals.shape
    part = split_of(CAP // 2, 8)
    sums = jax.ShapeDtypeStruct((2, CAP // 2, factors_n), F32)
    chosen = (CAP, paths, factors_n)
    return pl.pallas_call(
        functools.partial(gather_kernel, part),
        in_specs=[HBM, HBM],
        out_specs=[HBM, VMEM, VMEM],
        out_shape=[
            pltpu.HBM(chosen, BF16),
            sums,
            sums,
        ],
        scratch_shapes=[
            pltpu.SMEM(tail.shape, jnp.int32),
            pltpu.VMEM(chosen, BF16),
            pltpu.SemaphoreType.DMA,
            pltpu.SemaphoreType.DMA((CAP // part,)),
            pltpu.SemaphoreType.DMA,
        ],
        compiler_params=small(8),
        cost_estimate=pl.CostEstimate(flops=0, bytes_accessed=0, transcendentals=0),
        name="gather_nodes",
    )(tail, normals)


def to_message(sums, within):
    high = sums.astype(F16)
    low = (sums - high.astype(F32)).astype(F16)
    return jnp.stack([high, low, within.astype(F16)])


def pooled(parts, count):
    total = sum(s for s, _ in parts)
    center = total / (count * len(parts))
    return total, sum(w + (s / count - center) ** 2 * count for s, w in parts)


def of_message(message):
    high, low, within = message.astype(F32)
    return high + low, within


def order_kernel(
    unit, bound, plan, far, tail_hbm, states_hbm, loadings_hbm, strikes, hedge,
    levels, live, gain, *refs,
):
    chunks, steps, rows = len(plan), len(plan[0]), gain.shape[0]
    ordered, terms = refs[:chunks], refs[chunks : 2 * chunks]
    tail, states, onehot, own, tail_sem, states_sem, sems = refs[2 * chunks :]
    node_count = states.shape[0]
    position = lax.axis_index("inner")
    group, chip, core = lax.axis_index("outer"), position // 2, lax.rem(position, 2)
    tail_copy = pltpu.make_async_copy(tail_hbm, tail, tail_sem)
    states_copy = pltpu.make_async_copy(states_hbm, states, states_sem)
    tail_copy.start()
    states_copy.start()
    blocks, copies = [], []
    for chunk in range(chunks):
        for step in range(steps):
            d, away = plan[chunk][step]
            to_chip, to_group = far(chip, d, group, away)
            block = (to_group * chunks + to_chip) * 2 + core
            k = chunk * steps + step
            copy = pltpu.make_async_copy(loadings_hbm.at[block], own.at[k], sems.at[k])
            copy.start()
            blocks.append(block)
            copies.append(copy)
    wide = strikes.shape[1]
    lanes = lax.broadcasted_iota(jnp.int32, (rows, wide), 1)
    lines = lax.broadcasted_iota(jnp.int32, (rows, wide), 0)

    def column(ref, block):
        line = ref[pl.ds(block * rows // wide, 1), :]
        here = lanes == lines + lax.rem(block * rows, wide)
        return jnp.sum(jnp.where(here, line, 0.0), axis=1, keepdims=True)

    for k, block in enumerate(blocks):
        chunk, step = k // steps, k % steps
        at = slice(step * rows, (step + 1) * rows)
        size = column(hedge, block)
        scale = jnp.abs(size)
        terms[chunk][at, 0:1] = column(strikes, block) * 0.5
        terms[chunk][at, 1:2] = size * 0.5
        terms[chunk][at, 2:3] = jnp.where(
            scale > 1e-30, bound / jnp.maximum(scale, 1e-30), 0.0
        )
        if plan[chunk][step] == (0, 0):
            owned = scale * unit
    tail_copy.wait()
    base = group * node_count
    first = first_of(tail, base)
    nodes = lax.broadcasted_iota(jnp.int32, (1, node_count), 1)
    for slot in range(CAP):
        node, inside = place_of(tail, first, base, slot)
        used = inside & (node >= 0) & (node < node_count)
        onehot[slot : slot + 1, :] = ((nodes == node) & used).astype(F32)
        if slot < CAP // 2:
            live[slot : slot + 1, :] = jnp.full((1, live.shape[1]), used.astype(F32))
    states_copy.wait()
    levels[...] = jnp.dot(
        onehot[...].astype(BF16), states[...], preferred_element_type=F32
    )
    for k, copy in enumerate(copies):
        copy.wait()
        values = own[k].astype(F32)
        if plan[k // steps][k % steps] == (0, 0):
            gain[...] = values * owned
        ordered[k // steps][k % steps] = (values * 0.5).astype(BF16)


def order(unit, bound, plan, far, tail, states, loadings, strikes, hedge):
    chunks, steps = len(plan), len(plan[0])
    _, rows, factors_n = loadings.shape
    return pl.pallas_call(
        functools.partial(order_kernel, unit, bound, plan, far),
        in_specs=[HBM] * 3 + [VMEM] * 2,
        out_specs=[VMEM] * (2 * chunks + 3),
        out_shape=[
            jax.ShapeDtypeStruct((count, factors_n), F32) for count in (CAP, CAP // 2, rows)
        ]
        + [jax.ShapeDtypeStruct((steps, rows, factors_n), BF16)] * chunks
        + [jax.ShapeDtypeStruct((steps * rows, 3), F32)] * chunks,
        scratch_shapes=[
            pltpu.SMEM(tail.shape, jnp.int32),
            pltpu.VMEM(states.shape, BF16),
            pltpu.VMEM((CAP, states.shape[0]), F32),
            pltpu.VMEM((chunks * steps, rows, factors_n), BF16),
            pltpu.SemaphoreType.DMA,
            pltpu.SemaphoreType.DMA,
            pltpu.SemaphoreType.DMA((chunks * steps,)),
        ],
        compiler_params=small(12),
        cost_estimate=pl.CostEstimate(flops=0, bytes_accessed=1 << 20, transcendentals=0),
        name="order_instruments",
    )(tail, states, loadings, strikes, hedge)


def prepare(own, theirs, stats, levels, sigma, scaled, factors, ready, begin, end):
    slots, paths, factors_n = own.shape
    half = slots // 2
    shape = (paths, factors_n)
    sigmas = jnp.broadcast_to(sigma[...], shape)
    for at in range(begin, end):
        mine, row = at < half, at % half
        slot = row if mine == ready else row + half
        source = own if mine else theirs
        place = slot if mine else (slot + half) % slots
        center = jnp.broadcast_to(stats[0, row : row + 1, :], shape)
        rstd = jnp.broadcast_to(stats[1, row : row + 1, :], shape)
        level = jnp.broadcast_to(levels[place : place + 1, :], shape)
        unit = ((source[slot].astype(F32) - center) * rstd).astype(BF16)
        rows = slice(at * paths, (at + 1) * paths)
        scaled[rows, :] = unit
        factors[rows, :] = (level + sigmas * unit.astype(F32)).astype(BF16)


def ready_kernel(own, theirs, stats, levels, sigma, loadings, terms, scaled, factors, out):
    slots, paths, _ = own.shape
    prepare(own, theirs, stats, levels, sigma, scaled, factors, True, 0, slots)
    out[...] = cross_of(slots * paths, ((scaled, factors),), loadings, terms)


def ready_rows(own, theirs, stats, levels, sigma, ordered, terms):
    slots, paths, factors_n = own.shape
    rows = slots * paths
    count = ordered.shape[0]
    half = jax.ShapeDtypeStruct((rows, factors_n), BF16)
    return pl.pallas_call(
        ready_kernel,
        in_specs=[VMEM] * 7,
        out_specs=[VMEM] * 3,
        out_shape=[half, half, jax.ShapeDtypeStruct((count, factors_n), F32)],
        compiler_params=small(16),
        cost_estimate=cost_of(rows, count, factors_n),
        name="ready_rows",
    )(own, theirs, stats, levels, sigma, ordered, terms)


def cross_of(tile, halves, loadings, terms):
    strikes, hedge, scale = terms[:, 0:1], terms[:, 1:2], terms[:, 2:3]
    part = loadings[...]
    each = halves[0][0].shape[0] // tile
    places = [(half, r * tile) for half in range(len(halves)) for r in range(each)]

    def level(half, at):
        rows = halves[half][1][at : at + tile, :]
        return lax.dot_general(
            part, rows, (((1,), (1,)), ((), ())), preferred_element_type=F32
        )

    total = None
    current = level(*places[0])
    for k, (half, at) in enumerate(places):
        after = level(*places[k + 1]) if k + 1 < len(places) else None
        weight = (jnp.tanh(current - strikes) * hedge + hedge).astype(BF16)
        cross = jnp.dot(
            weight, halves[half][0][at : at + tile, :], preferred_element_type=F32
        )
        total = cross if total is None else total + cross
        current = after
    return total * scale


def first_kernel(
    own, theirs, stats, levels, sigma, done, loadings, terms, scaled, factors, low, high
):
    slots, paths, _ = own.shape
    prepare(own, theirs, stats, levels, sigma, scaled, factors, False, 0, slots)
    sums = cross_of(slots * paths, ((scaled, factors),), loadings, terms)
    give(done[...] + sums, low, high)


def next_kernel(tile, s0, f0, s1, f1, loadings, terms, low, high):
    give(cross_of(tile, ((s0, f0), (s1, f1)), loadings, terms), low, high)


def give(sums, low, high):
    half = low.shape[0]
    low[...] = sums[:half]
    high[...] = sums[half:]


def halves_of(count, factors_n):
    return [
        jax.ShapeDtypeStruct((size, factors_n), F32) for size in (count // 2, count - count // 2)
    ]


def cost_of(rows, count, factors_n):
    return pl.CostEstimate(
        flops=2 * rows * count * factors_n,
        bytes_accessed=4 * count * factors_n,
        transcendentals=0,
    )


def tile_of(slots, paths):
    return paths * split_of(slots, max(1, 1280 // paths))


def first_chunk(own, theirs, stats, levels, sigma, done, ordered, terms):
    slots, paths, factors_n = own.shape
    count = ordered.shape[0]
    half = jax.ShapeDtypeStruct((slots * paths, factors_n), BF16)
    return pl.pallas_call(
        first_kernel,
        in_specs=[VMEM] * 8,
        out_specs=[VMEM] * 4,
        out_shape=[half, half, *halves_of(count, factors_n)],
        compiler_params=small(16),
        cost_estimate=cost_of(slots * paths, count, factors_n),
        name="first_chunk",
    )(own, theirs, stats, levels, sigma, done, ordered, terms)


def next_chunk(tile, ready, rest, ordered, terms):
    rows, factors_n = ready[0].shape
    count = ordered.shape[0]
    return pl.pallas_call(
        functools.partial(next_kernel, tile),
        in_specs=[VMEM] * 6,
        out_specs=[VMEM] * 2,
        out_shape=halves_of(count, factors_n),
        compiler_params=small(16),
        cost_estimate=cost_of(2 * rows, count, factors_n),
        name="next_chunk",
    )(*ready, *rest, ordered, terms)


def body(normals, states, loadings, strikes, hedge, sigma, tail):
    groups = lax.axis_size("outer")
    inner = lax.axis_size("inner")
    chips = inner // 2
    _, per_node, factors_n = normals.shape
    instruments = loadings.shape[0]
    tail_count = tail.shape[0]
    paths = per_node * inner
    rows = instruments // (groups * inner)
    paired = chips & (chips - 1) == 0

    def partner(of, d):
        return of ^ d if paired else (of + d) % chips

    def beyond(of, s):
        return of ^ s if groups & (groups - 1) == 0 else (of + s) % groups

    def to_core(x):
        return lax.ppermute(x, "inner", [(i, i ^ 1) for i in range(inner)])

    def to_chip(x, d):
        return lax.ppermute(
            x, "inner", [(i, partner(i // 2, d) * 2 + i % 2) for i in range(inner)]
        )

    def to_group(x, s):
        return lax.ppermute(x, "outer", [(g, beyond(g, s)) for g in range(groups)])

    bound = 32768.0 / (tail_count * paths)
    unit = 1.0 / (bound * tail_count * paths)

    tail, normals, states, loadings = (
        pltpu.with_memory_space_constraint(x, pltpu.HBM)
        for x in (tail, normals, states, loadings.reshape(groups * inner, rows, factors_n))
    )
    wide = 128 if 128 % rows == 0 else rows
    strikes, hedge = strikes.reshape(-1, wide), hedge.reshape(-1, wide)

    chosen, mine, other = gather_nodes(tail, normals)
    sums, squares = mine + to_core(other)
    count = 2 * per_node
    within = squares - sums * sums / count
    message = to_message(sums, within)
    chosen, message, strikes = lax.optimization_barrier((chosen, message, strikes))
    rounds = [1 << k for k in range(chips.bit_length() - 1)] if paired and chips > 4 else []
    if not rounds:
        arrived = [of_message(to_chip(message, d)) for d in range(chips - 1, 0, -1)]
        sums, within = pooled([(sums, within), *arrived], count)
        count *= chips
    for d in rounds:
        arrived = to_chip(message, d)
        sums, within = pooled([(sums, within), of_message(arrived)], count)
        count *= 2
        if d != rounds[-1]:
            message = to_message(sums, within)
    theirs = to_core(chosen)
    steps = range(groups)
    relayed = chips == 4 and groups % 2 == 0
    if relayed:
        half = groups // 2
        low, high = steps[:half], steps[half:]
        plan = [
            [(3, s) for s in steps],
            [(1, s) for s in high] + [(2, s) for s in high],
            [(0, s) for s in steps],
            [(2, s) for s in low] + [(1, s) for s in low],
        ]
    else:
        plan = [[(d, s) for s in steps] for d in range(chips - 1, -1, -1)]
    far = lambda chip, d, group, s: (partner(chip, d), beyond(group, s))
    levels, live, gain, *parts = order(
        unit, bound, plan, far, tail, states, loadings, strikes, hedge
    )
    ordered = [part.reshape(groups * rows, factors_n) for part in parts[: len(plan)]]
    terms = parts[len(plan) :]
    sums, within, theirs, levels, live, gain, ordered, terms = lax.optimization_barrier(
        (sums, within, theirs, levels, live, gain, ordered, terms)
    )
    stats = jnp.stack([sums / count, live * lax.rsqrt(within / count + EPSILON)])
    their_stats = to_core(stats)

    sigmas = sigma.reshape(1, factors_n)
    *ready, done = ready_rows(chosen, theirs, stats, levels, sigmas, ordered[0], terms[0])

    tile = tile_of(CAP, per_node)
    *rest, low, high = first_chunk(
        chosen, theirs, their_stats, levels, sigmas, done, ordered[0], terms[0]
    )

    def chunk(k, *after):
        kept, _ = lax.optimization_barrier((tuple(rest), after))
        return next_chunk(tile, ready, kept, ordered[k], terms[k])

    def plus(x, y):
        return x + y.astype(F32)

    if relayed:
        a3, b3 = low.astype(F16), high.astype(F16)
        from_b3, from_a3 = to_chip(b3, 1), to_chip(a3, 2)
        b1, b2 = chunk(1, a3, b3)
        b1, b2 = b1.astype(F16), plus(b2, from_b3).astype(F16)
        from_b1, from_b2 = to_chip(b1, 1), to_chip(b2, 2)
        a0, b0 = chunk(2, b1, b2)
        a2, a1 = chunk(3, a0, b0, from_a3)
        a2, a1 = a2.astype(F16), plus(a1, from_a3).astype(F16)
        from_a2, from_a1 = to_chip(a2, 2), to_chip(a1, 1)
        b0, _ = lax.optimization_barrier((b0, (a2, a1)))
        kept = (plus(plus(a0, from_a2), from_a1), plus(plus(b0, from_b1), from_b2))
        part = lambda s: kept[s // half][s % half * rows :][:rows]
    else:
        arrived = []
        for k in range(1, chips):
            sent = jnp.concatenate([low, high]).astype(F16)
            arrived.append(to_chip(sent, chips - k))
            low, high = chunk(k, sent)
        kept = jnp.concatenate([low, high])
        for item in arrived:
            kept = plus(kept, item)
        part = lambda s: kept[s * rows :][:rows]
    owned = part(0)
    for s in sorted(range(1, groups), key=lambda s: (s < groups // 2, s)):
        owned = plus(owned, to_group(part(s).astype(F16), s))
    return gain * owned


def solution(mesh):
    placed = (P("outer", "inner", None), P("outer", None), P(), P(), P(), P(), P())
    return jax.shard_map(
        body, mesh=mesh, in_specs=placed, out_specs=P(("outer", "inner"), None), check_vma=False
    )
```

```python
import functools

import jax
import jax.numpy as jnp
from jax import lax
from jax.experimental import pallas as pl
from jax.experimental.pallas import tpu as pltpu
from jax.sharding import PartitionSpec as P

CAP = 80
EPSILON = 1e-06
VMEM = pl.BlockSpec(memory_space=pltpu.VMEM)
SMEM = pl.BlockSpec(memory_space=pltpu.SMEM)
HBM = pl.BlockSpec(memory_space=pltpu.HBM)
F32 = jnp.float32
BF16 = jnp.bfloat16
F16 = jnp.float16


def split_of(count, most):
    for size in range(min(count, most), 0, -1):
        if count % size == 0:
            return size
    return 1


def small(mebibytes):
    return pltpu.CompilerParams(vmem_limit_bytes=mebibytes << 20)


def first_of(tail, base):
    count = tail.shape[0]
    first = jnp.int32(0)
    for bit in range(count.bit_length() - 1, -1, -1):
        ahead = first + (1 << bit)
        below = tail[jnp.minimum(ahead, count) - 1] < base
        first = jnp.where((ahead <= count) & below, ahead, first)
    return first


def place_of(tail, first, base, slot):
    at = slot + lax.rem(lax.axis_index("inner"), 2) * (CAP // 2)
    at = first + jnp.where(at >= CAP, at - CAP, at)
    node = tail[jnp.minimum(at, tail.shape[0] - 1)] - base
    return node, at < tail.shape[0]


def gather_kernel(
    part, tail_hbm, normals, chosen_hbm, mine, other,
    tail, chosen, tail_sem, sems, out_sem,
):
    node_count = normals.shape[0]
    tail_copy = pltpu.make_async_copy(tail_hbm, tail, tail_sem)
    tail_copy.start()
    base = lax.axis_index("outer") * node_count
    tail_copy.wait()
    first = first_of(tail, base)
    parts = CAP // part

    @pl.loop(0, parts)
    def _(p):
        for k in range(part):
            slot = p * part + k
            node, inside = place_of(tail, first, base, slot)
            used = inside & (node >= 0) & (node < node_count)
            node = jnp.where(used, node, lax.rem(slot, node_count))
            pltpu.make_async_copy(normals.at[node], chosen.at[slot], sems.at[p]).start()

    out_copy = pltpu.make_async_copy(chosen, chosen_hbm, out_sem)
    for begin, sums in ((0, mine), (parts // 2, other)):

        @pl.loop(0, parts // 2)
        def _(p):
            piece = chosen.at[pl.ds((begin + p) * part, part)]
            pltpu.make_async_copy(piece, piece, sems.at[begin + p]).wait()
            there = chosen_hbm.at[pl.ds((begin + p) * part, part)]
            pltpu.make_async_copy(piece, there, out_sem).start()
            values = piece[...].astype(F32)
            rows = pl.ds(pl.multiple_of(p * part, part), part)
            sums[0, rows, :] = jnp.sum(values, axis=1)
            sums[1, rows, :] = jnp.sum(values * values, axis=1)

    out_copy.wait()


def gather_nodes(tail, normals):
    _, paths, factors_n = normals.shape
    part = split_of(CAP // 2, 8)
    sums = jax.ShapeDtypeStruct((2, CAP // 2, factors_n), F32)
    chosen = (CAP, paths, factors_n)
    return pl.pallas_call(
        functools.partial(gather_kernel, part),
        in_specs=[HBM, HBM],
        out_specs=[HBM, VMEM, VMEM],
        out_shape=[
            pltpu.HBM(chosen, BF16),
            sums,
            sums,
        ],
        scratch_shapes=[
            pltpu.SMEM(tail.shape, jnp.int32),
            pltpu.VMEM(chosen, BF16),
            pltpu.SemaphoreType.DMA,
            pltpu.SemaphoreType.DMA((CAP // part,)),
            pltpu.SemaphoreType.DMA,
        ],
        compiler_params=small(8),
        cost_estimate=pl.CostEstimate(flops=0, bytes_accessed=0, transcendentals=0),
        name="gather_nodes",
    )(tail, normals)


def to_message(sums, within):
    high = sums.astype(F16)
    low = (sums - high.astype(F32)).astype(F16)
    return jnp.stack([high, low, within.astype(F16)])


def pooled(parts, count):
    total = sum(s for s, _ in parts)
    center = total / (count * len(parts))
    return total, sum(w + (s / count - center) ** 2 * count for s, w in parts)


def of_message(message):
    high, low, within = message.astype(F32)
    return high + low, within


def order_kernel(
    unit, bound, plan, far, tail_hbm, states_hbm, loadings_hbm, strikes, hedge,
    levels, live, gain, *refs,
):
    chunks, steps, rows = len(plan), len(plan[0]), gain.shape[0]
    ordered, terms = refs[:chunks], refs[chunks : 2 * chunks]
    tail, states, onehot, own, tail_sem, states_sem, sems = refs[2 * chunks :]
    node_count = states.shape[0]
    position = lax.axis_index("inner")
    group, chip, core = lax.axis_index("outer"), position // 2, lax.rem(position, 2)
    tail_copy = pltpu.make_async_copy(tail_hbm, tail, tail_sem)
    states_copy = pltpu.make_async_copy(states_hbm, states, states_sem)
    tail_copy.start()
    states_copy.start()
    blocks, copies = [], []
    for chunk in range(chunks):
        for step in range(steps):
            d, away = plan[chunk][step]
            to_chip, to_group = far(chip, d, group, away)
            block = (to_group * chunks + to_chip) * 2 + core
            k = chunk * steps + step
            copy = pltpu.make_async_copy(loadings_hbm.at[block], own.at[k], sems.at[k])
            copy.start()
            blocks.append(block)
            copies.append(copy)
    wide = strikes.shape[1]
    lanes = lax.broadcasted_iota(jnp.int32, (rows, wide), 1)
    lines = lax.broadcasted_iota(jnp.int32, (rows, wide), 0)

    def column(ref, block):
        line = ref[pl.ds(block * rows // wide, 1), :]
        here = lanes == lines + lax.rem(block * rows, wide)
        return jnp.sum(jnp.where(here, line, 0.0), axis=1, keepdims=True)

    for k, block in enumerate(blocks):
        chunk, step = k // steps, k % steps
        at = slice(step * rows, (step + 1) * rows)
        size = column(hedge, block)
        scale = jnp.abs(size)
        terms[chunk][at, 0:1] = column(strikes, block) * 0.5
        terms[chunk][at, 1:2] = size * 0.5
        terms[chunk][at, 2:3] = jnp.where(
            scale > 1e-30, bound / jnp.maximum(scale, 1e-30), 0.0
        )
        if plan[chunk][step] == (0, 0):
            owned = scale * unit
    tail_copy.wait()
    base = group * node_count
    first = first_of(tail, base)
    nodes = lax.broadcasted_iota(jnp.int32, (1, node_count), 1)
    for slot in range(CAP):
        node, inside = place_of(tail, first, base, slot)
        used = inside & (node >= 0) & (node < node_count)
        onehot[slot : slot + 1, :] = ((nodes == node) & used).astype(F32)
        if slot < CAP // 2:
            live[slot : slot + 1, :] = jnp.full((1, live.shape[1]), used.astype(F32))
    states_copy.wait()
    levels[...] = jnp.dot(
        onehot[...].astype(BF16), states[...], preferred_element_type=F32
    )
    for k, copy in enumerate(copies):
        copy.wait()
        values = own[k].astype(F32)
        if plan[k // steps][k % steps] == (0, 0):
            gain[...] = values * owned
        ordered[k // steps][k % steps] = (values * 0.5).astype(BF16)


def order(unit, bound, plan, far, tail, states, loadings, strikes, hedge):
    chunks, steps = len(plan), len(plan[0])
    _, rows, factors_n = loadings.shape
    return pl.pallas_call(
        functools.partial(order_kernel, unit, bound, plan, far),
        in_specs=[HBM] * 3 + [VMEM] * 2,
        out_specs=[VMEM] * (2 * chunks + 3),
        out_shape=[
            jax.ShapeDtypeStruct((count, factors_n), F32) for count in (CAP, CAP // 2, rows)
        ]
        + [jax.ShapeDtypeStruct((steps, rows, factors_n), BF16)] * chunks
        + [jax.ShapeDtypeStruct((steps * rows, 3), F32)] * chunks,
        scratch_shapes=[
            pltpu.SMEM(tail.shape, jnp.int32),
            pltpu.VMEM(states.shape, BF16),
            pltpu.VMEM((CAP, states.shape[0]), F32),
            pltpu.VMEM((chunks * steps, rows, factors_n), BF16),
            pltpu.SemaphoreType.DMA,
            pltpu.SemaphoreType.DMA,
            pltpu.SemaphoreType.DMA((chunks * steps,)),
        ],
        compiler_params=small(12),
        cost_estimate=pl.CostEstimate(flops=0, bytes_accessed=1 << 20, transcendentals=0),
        name="order_instruments",
    )(tail, states, loadings, strikes, hedge)


def prepare(own, theirs, stats, levels, sigma, scaled, factors, ready, begin, end):
    slots, paths, factors_n = own.shape
    half = slots // 2
    shape = (paths, factors_n)
    sigmas = jnp.broadcast_to(sigma[...], shape)
    for at in range(begin, end):
        mine, row = at < half, at % half
        slot = row if mine == ready else row + half
        source = own if mine else theirs
        place = slot if mine else (slot + half) % slots
        center = jnp.broadcast_to(stats[0, row : row + 1, :], shape)
        rstd = jnp.broadcast_to(stats[1, row : row + 1, :], shape)
        level = jnp.broadcast_to(levels[place : place + 1, :], shape)
        unit = ((source[slot].astype(F32) - center) * rstd).astype(BF16)
        rows = slice(at * paths, (at + 1) * paths)
        scaled[rows, :] = unit
        factors[rows, :] = (level + sigmas * unit.astype(F32)).astype(BF16)


def ready_kernel(own, theirs, stats, levels, sigma, loadings, terms, scaled, factors, out):
    slots, paths, _ = own.shape
    prepare(own, theirs, stats, levels, sigma, scaled, factors, True, 0, slots)
    out[...] = cross_of(slots * paths, ((scaled, factors),), loadings, terms)


def ready_rows(own, theirs, stats, levels, sigma, ordered, terms):
    slots, paths, factors_n = own.shape
    rows = slots * paths
    count = ordered.shape[0]
    half = jax.ShapeDtypeStruct((rows, factors_n), BF16)
    return pl.pallas_call(
        ready_kernel,
        in_specs=[VMEM] * 7,
        out_specs=[VMEM] * 3,
        out_shape=[half, half, jax.ShapeDtypeStruct((count, factors_n), F32)],
        compiler_params=small(16),
        cost_estimate=cost_of(rows, count, factors_n),
        name="ready_rows",
    )(own, theirs, stats, levels, sigma, ordered, terms)


def cross_of(tile, halves, loadings, terms):
    strikes, hedge, scale = terms[:, 0:1], terms[:, 1:2], terms[:, 2:3]
    part = loadings[...]
    each = halves[0][0].shape[0] // tile
    places = [(half, r * tile) for half in range(len(halves)) for r in range(each)]

    def level(half, at):
        rows = halves[half][1][at : at + tile, :]
        return lax.dot_general(
            part, rows, (((1,), (1,)), ((), ())), preferred_element_type=F32
        )

    total = None
    current = level(*places[0])
    for k, (half, at) in enumerate(places):
        after = level(*places[k + 1]) if k + 1 < len(places) else None
        weight = (jnp.tanh(current - strikes) * hedge + hedge).astype(BF16)
        cross = jnp.dot(
            weight, halves[half][0][at : at + tile, :], preferred_element_type=F32
        )
        total = cross if total is None else total + cross
        current = after
    return total * scale


def first_kernel(
    own, theirs, stats, levels, sigma, done, loadings, terms, scaled, factors, low, high
):
    slots, paths, _ = own.shape
    prepare(own, theirs, stats, levels, sigma, scaled, factors, False, 0, slots)
    sums = cross_of(slots * paths, ((scaled, factors),), loadings, terms)
    give(done[...] + sums, low, high)


def next_kernel(tile, s0, f0, s1, f1, loadings, terms, low, high):
    give(cross_of(tile, ((s0, f0), (s1, f1)), loadings, terms), low, high)


def give(sums, low, high):
    half = low.shape[0]
    low[...] = sums[:half]
    high[...] = sums[half:]


def halves_of(count, factors_n):
    return [
        jax.ShapeDtypeStruct((size, factors_n), F32) for size in (count // 2, count - count // 2)
    ]


def cost_of(rows, count, factors_n):
    return pl.CostEstimate(
        flops=2 * rows * count * factors_n,
        bytes_accessed=4 * count * factors_n,
        transcendentals=0,
    )


def tile_of(slots, paths):
    return paths * split_of(slots, max(1, 1280 // paths))


def first_chunk(own, theirs, stats, levels, sigma, done, ordered, terms):
    slots, paths, factors_n = own.shape
    count = ordered.shape[0]
    half = jax.ShapeDtypeStruct((slots * paths, factors_n), BF16)
    return pl.pallas_call(
        first_kernel,
        in_specs=[VMEM] * 8,
        out_specs=[VMEM] * 4,
        out_shape=[half, half, *halves_of(count, factors_n)],
        compiler_params=small(16),
        cost_estimate=cost_of(slots * paths, count, factors_n),
        name="first_chunk",
    )(own, theirs, stats, levels, sigma, done, ordered, terms)


def next_chunk(tile, ready, rest, ordered, terms):
    rows, factors_n = ready[0].shape
    count = ordered.shape[0]
    return pl.pallas_call(
        functools.partial(next_kernel, tile),
        in_specs=[VMEM] * 6,
        out_specs=[VMEM] * 2,
        out_shape=halves_of(count, factors_n),
        compiler_params=small(16),
        cost_estimate=cost_of(2 * rows, count, factors_n),
        name="next_chunk",
    )(*ready, *rest, ordered, terms)


def body(normals, states, loadings, strikes, hedge, sigma, tail):
    groups = lax.axis_size("outer")
    inner = lax.axis_size("inner")
    chips = inner // 2
    _, per_node, factors_n = normals.shape
    instruments = loadings.shape[0]
    tail_count = tail.shape[0]
    paths = per_node * inner
    rows = instruments // (groups * inner)
    paired = chips & (chips - 1) == 0

    def partner(of, d):
        return of ^ d if paired else (of + d) % chips

    def beyond(of, s):
        return of ^ s if groups & (groups - 1) == 0 else (of + s) % groups

    def to_core(x):
        return lax.ppermute(x, "inner", [(i, i ^ 1) for i in range(inner)])

    def to_chip(x, d):
        return lax.ppermute(
            x, "inner", [(i, partner(i // 2, d) * 2 + i % 2) for i in range(inner)]
        )

    def to_group(x, s):
        return lax.ppermute(x, "outer", [(g, beyond(g, s)) for g in range(groups)])

    bound = 32768.0 / (tail_count * paths)
    unit = 1.0 / (bound * tail_count * paths)

    tail, normals, states, loadings = (
        pltpu.with_memory_space_constraint(x, pltpu.HBM)
        for x in (tail, normals, states, loadings.reshape(groups * inner, rows, factors_n))
    )
    wide = 128 if 128 % rows == 0 else rows
    strikes, hedge = strikes.reshape(-1, wide), hedge.reshape(-1, wide)

    chosen, mine, other = gather_nodes(tail, normals)
    sums, squares = mine + to_core(other)
    count = 2 * per_node
    within = squares - sums * sums / count
    message = to_message(sums, within)
    chosen, message, strikes = lax.optimization_barrier((chosen, message, strikes))
    rounds = [1 << k for k in range(chips.bit_length() - 1)] if paired and chips > 4 else []
    if not rounds:
        arrived = [of_message(to_chip(message, d)) for d in range(chips - 1, 0, -1)]
        sums, within = pooled([(sums, within), *arrived], count)
        count *= chips
    for d in rounds:
        arrived = to_chip(message, d)
        sums, within = pooled([(sums, within), of_message(arrived)], count)
        count *= 2
        if d != rounds[-1]:
            message = to_message(sums, within)
    theirs = to_core(chosen)
    steps = range(groups)
    relayed = chips == 4 and groups % 2 == 0
    if relayed:
        half = groups // 2
        low, high = steps[:half], steps[half:]
        plan = [
            [(3, s) for s in steps],
            [(1, s) for s in high] + [(2, s) for s in high],
            [(2, s) for s in low] + [(1, s) for s in low],
            [(0, s) for s in steps],
        ]
    else:
        plan = [[(d, s) for s in steps] for d in range(chips - 1, -1, -1)]
    far = lambda chip, d, group, s: (partner(chip, d), beyond(group, s))
    levels, live, gain, *parts = order(
        unit, bound, plan, far, tail, states, loadings, strikes, hedge
    )
    ordered = [part.reshape(groups * rows, factors_n) for part in parts[: len(plan)]]
    terms = parts[len(plan) :]
    sums, within, theirs, levels, live, gain, ordered, terms = lax.optimization_barrier(
        (sums, within, theirs, levels, live, gain, ordered, terms)
    )
    stats = jnp.stack([sums / count, live * lax.rsqrt(within / count + EPSILON)])
    their_stats = to_core(stats)

    sigmas = sigma.reshape(1, factors_n)
    *ready, done = ready_rows(chosen, theirs, stats, levels, sigmas, ordered[0], terms[0])

    tile = tile_of(CAP, per_node)
    *rest, low, high = first_chunk(
        chosen, theirs, their_stats, levels, sigmas, done, ordered[0], terms[0]
    )

    def chunk(k, *after):
        kept, _ = lax.optimization_barrier((tuple(rest), after))
        return next_chunk(tile, ready, kept, ordered[k], terms[k])

    def plus(x, y):
        return x + y.astype(F32)

    if relayed:
        a3, b3 = low.astype(F16), high.astype(F16)
        from_b3, from_a3 = to_chip(b3, 1), to_chip(a3, 2)
        b1, b2 = chunk(1, a3, b3)
        a2, a1 = chunk(2, b1, b2)
        b2, b1 = plus(b2, from_b3).astype(F16), b1.astype(F16)
        a2, a1 = a2.astype(F16), plus(a1, from_a3).astype(F16)
        b2, b1, a2, a1 = lax.optimization_barrier((b2, b1, a2, a1))
        from_b2, from_b1 = to_chip(b2, 2), to_chip(b1, 1)
        from_a2, from_a1 = to_chip(a2, 2), to_chip(a1, 1)
        a0, b0 = chunk(3, b2, b1, a2, a1)
        kept = (plus(plus(a0, from_a2), from_a1), plus(plus(b0, from_b1), from_b2))
        part = lambda s: kept[s // half][s % half * rows :][:rows]
    else:
        arrived = []
        for k in range(1, chips):
            sent = jnp.concatenate([low, high]).astype(F16)
            arrived.append(to_chip(sent, chips - k))
            low, high = chunk(k, sent)
        kept = jnp.concatenate([low, high])
        for item in arrived:
            kept = plus(kept, item)
        part = lambda s: kept[s * rows :][:rows]
    owned = part(0)
    for s in sorted(range(1, groups), key=lambda s: (s < groups // 2, s)):
        owned = plus(owned, to_group(part(s).astype(F16), s))
    return gain * owned


def solution(mesh):
    placed = (P("outer", "inner", None), P("outer", None), P(), P(), P(), P(), P())
    return jax.shard_map(
        body, mesh=mesh, in_specs=placed, out_specs=P(("outer", "inner"), None), check_vma=False
    )
```

```python
import functools

import jax
import jax.numpy as jnp
from jax import lax
from jax.experimental import pallas as pl
from jax.experimental.pallas import tpu as pltpu
from jax.sharding import PartitionSpec as P

CAP = 80
EPSILON = 1e-06
VMEM = pl.BlockSpec(memory_space=pltpu.VMEM)
SMEM = pl.BlockSpec(memory_space=pltpu.SMEM)
HBM = pl.BlockSpec(memory_space=pltpu.HBM)
F32 = jnp.float32
BF16 = jnp.bfloat16
F16 = jnp.float16


def split_of(count, most):
    for size in range(min(count, most), 0, -1):
        if count % size == 0:
            return size
    return 1


def small(mebibytes):
    return pltpu.CompilerParams(vmem_limit_bytes=mebibytes << 20)


def first_of(tail, base):
    count = tail.shape[0]
    first = jnp.int32(0)
    for bit in range(count.bit_length() - 1, -1, -1):
        ahead = first + (1 << bit)
        below = tail[jnp.minimum(ahead, count) - 1] < base
        first = jnp.where((ahead <= count) & below, ahead, first)
    return first


def place_of(tail, first, base, slot):
    at = slot + lax.rem(lax.axis_index("inner"), 2) * (CAP // 2)
    at = first + jnp.where(at >= CAP, at - CAP, at)
    node = tail[jnp.minimum(at, tail.shape[0] - 1)] - base
    return node, at < tail.shape[0]


def gather_kernel(
    part, tail_hbm, normals, chosen_hbm, mine, other,
    tail, chosen, tail_sem, sems, out_sem,
):
    node_count = normals.shape[0]
    tail_copy = pltpu.make_async_copy(tail_hbm, tail, tail_sem)
    tail_copy.start()
    base = lax.axis_index("outer") * node_count
    tail_copy.wait()
    first = first_of(tail, base)
    parts = CAP // part

    @pl.loop(0, parts)
    def _(p):
        for k in range(part):
            slot = p * part + k
            node, inside = place_of(tail, first, base, slot)
            used = inside & (node >= 0) & (node < node_count)
            node = jnp.where(used, node, lax.rem(slot, node_count))
            pltpu.make_async_copy(normals.at[node], chosen.at[slot], sems.at[p]).start()

    out_copy = pltpu.make_async_copy(chosen, chosen_hbm, out_sem)
    for begin, sums in ((0, mine), (parts // 2, other)):

        @pl.loop(0, parts // 2)
        def _(p):
            piece = chosen.at[pl.ds((begin + p) * part, part)]
            pltpu.make_async_copy(piece, piece, sems.at[begin + p]).wait()
            there = chosen_hbm.at[pl.ds((begin + p) * part, part)]
            pltpu.make_async_copy(piece, there, out_sem).start()
            values = piece[...].astype(F32)
            rows = pl.ds(pl.multiple_of(p * part, part), part)
            sums[0, rows, :] = jnp.sum(values, axis=1)
            sums[1, rows, :] = jnp.sum(values * values, axis=1)

    out_copy.wait()


def gather_nodes(tail, normals):
    _, paths, factors_n = normals.shape
    part = split_of(CAP // 2, 8)
    sums = jax.ShapeDtypeStruct((2, CAP // 2, factors_n), F32)
    chosen = (CAP, paths, factors_n)
    return pl.pallas_call(
        functools.partial(gather_kernel, part),
        in_specs=[HBM, HBM],
        out_specs=[HBM, VMEM, VMEM],
        out_shape=[
            pltpu.HBM(chosen, BF16),
            sums,
            sums,
        ],
        scratch_shapes=[
            pltpu.SMEM(tail.shape, jnp.int32),
            pltpu.VMEM(chosen, BF16),
            pltpu.SemaphoreType.DMA,
            pltpu.SemaphoreType.DMA((CAP // part,)),
            pltpu.SemaphoreType.DMA,
        ],
        compiler_params=small(8),
        cost_estimate=pl.CostEstimate(flops=0, bytes_accessed=0, transcendentals=0),
        name="gather_nodes",
    )(tail, normals)


def to_message(sums, within):
    high = sums.astype(F16)
    low = (sums - high.astype(F32)).astype(F16)
    return jnp.stack([high, low, within.astype(F16)])


def pooled(parts, count):
    total = sum(s for s, _ in parts)
    center = total / (count * len(parts))
    return total, sum(w + (s / count - center) ** 2 * count for s, w in parts)


def of_message(message):
    high, low, within = message.astype(F32)
    return high + low, within


def order_kernel(
    unit, bound, plan, far, tail_hbm, states_hbm, loadings_hbm, strikes, hedge,
    levels, live, gain, *refs,
):
    chunks, rows = len(plan), gain.shape[0]
    cells = [(chunk, step) for chunk in range(chunks) for step in range(len(plan[chunk]))]
    ordered, terms = refs[:chunks], refs[chunks : 2 * chunks]
    tail, states, onehot, own, tail_sem, states_sem, sems = refs[2 * chunks :]
    node_count = states.shape[0]
    position = lax.axis_index("inner")
    group, chip, core = lax.axis_index("outer"), position // 2, lax.rem(position, 2)
    tail_copy = pltpu.make_async_copy(tail_hbm, tail, tail_sem)
    states_copy = pltpu.make_async_copy(states_hbm, states, states_sem)
    tail_copy.start()
    states_copy.start()
    blocks, copies = [], []
    for k, (chunk, step) in enumerate(cells):
        d, away = plan[chunk][step]
        to_chip, to_group = far(chip, d, group, away)
        block = (to_group * (lax.axis_size("inner") // 2) + to_chip) * 2 + core
        copy = pltpu.make_async_copy(loadings_hbm.at[block], own.at[k], sems.at[k])
        copy.start()
        blocks.append(block)
        copies.append(copy)
    wide = strikes.shape[1]
    lanes = lax.broadcasted_iota(jnp.int32, (rows, wide), 1)
    lines = lax.broadcasted_iota(jnp.int32, (rows, wide), 0)

    def column(ref, block):
        line = ref[pl.ds(block * rows // wide, 1), :]
        here = lanes == lines + lax.rem(block * rows, wide)
        return jnp.sum(jnp.where(here, line, 0.0), axis=1, keepdims=True)

    for k, block in enumerate(blocks):
        chunk, step = cells[k]
        at = slice(step * rows, (step + 1) * rows)
        size = column(hedge, block)
        scale = jnp.abs(size)
        terms[chunk][at, 0:1] = column(strikes, block) * 0.5
        terms[chunk][at, 1:2] = size * 0.5
        terms[chunk][at, 2:3] = jnp.where(
            scale > 1e-30, bound / jnp.maximum(scale, 1e-30), 0.0
        )
        if plan[chunk][step] == (0, 0):
            owned = scale * unit
    tail_copy.wait()
    base = group * node_count
    first = first_of(tail, base)
    nodes = lax.broadcasted_iota(jnp.int32, (1, node_count), 1)
    for slot in range(CAP):
        node, inside = place_of(tail, first, base, slot)
        used = inside & (node >= 0) & (node < node_count)
        onehot[slot : slot + 1, :] = ((nodes == node) & used).astype(F32)
        if slot < CAP // 2:
            live[slot : slot + 1, :] = jnp.full((1, live.shape[1]), used.astype(F32))
    states_copy.wait()
    levels[...] = jnp.dot(
        onehot[...].astype(BF16), states[...], preferred_element_type=F32
    )
    for k, copy in enumerate(copies):
        copy.wait()
        values = own[k].astype(F32)
        chunk, step = cells[k]
        if plan[chunk][step] == (0, 0):
            gain[...] = values * owned
        ordered[chunk][step] = (values * 0.5).astype(BF16)


def order(unit, bound, plan, far, tail, states, loadings, strikes, hedge):
    chunks, cells = len(plan), sum(len(part) for part in plan)
    _, rows, factors_n = loadings.shape
    return pl.pallas_call(
        functools.partial(order_kernel, unit, bound, plan, far),
        in_specs=[HBM] * 3 + [VMEM] * 2,
        out_specs=[VMEM] * (2 * chunks + 3),
        out_shape=[
            jax.ShapeDtypeStruct((count, factors_n), F32) for count in (CAP, CAP // 2, rows)
        ]
        + [jax.ShapeDtypeStruct((len(part), rows, factors_n), BF16) for part in plan]
        + [jax.ShapeDtypeStruct((len(part) * rows, 3), F32) for part in plan],
        scratch_shapes=[
            pltpu.SMEM(tail.shape, jnp.int32),
            pltpu.VMEM(states.shape, BF16),
            pltpu.VMEM((CAP, states.shape[0]), F32),
            pltpu.VMEM((cells, rows, factors_n), BF16),
            pltpu.SemaphoreType.DMA,
            pltpu.SemaphoreType.DMA,
            pltpu.SemaphoreType.DMA((cells,)),
        ],
        compiler_params=small(12),
        cost_estimate=pl.CostEstimate(flops=0, bytes_accessed=1 << 20, transcendentals=0),
        name="order_instruments",
    )(tail, states, loadings, strikes, hedge)


def prepare(own, theirs, stats, levels, sigma, scaled, factors, ready, begin, end):
    slots, paths, factors_n = own.shape
    half = slots // 2
    shape = (paths, factors_n)
    sigmas = jnp.broadcast_to(sigma[...], shape)
    for at in range(begin, end):
        mine, row = at < half, at % half
        slot = row if mine == ready else row + half
        source = own if mine else theirs
        place = slot if mine else (slot + half) % slots
        center = jnp.broadcast_to(stats[0, row : row + 1, :], shape)
        rstd = jnp.broadcast_to(stats[1, row : row + 1, :], shape)
        level = jnp.broadcast_to(levels[place : place + 1, :], shape)
        unit = ((source[slot].astype(F32) - center) * rstd).astype(BF16)
        rows = slice(at * paths, (at + 1) * paths)
        scaled[rows, :] = unit
        factors[rows, :] = (level + sigmas * unit.astype(F32)).astype(BF16)


def ready_kernel(own, theirs, stats, levels, sigma, loadings, terms, scaled, factors, out):
    slots, paths, _ = own.shape
    prepare(own, theirs, stats, levels, sigma, scaled, factors, True, 0, slots)
    out[...] = cross_of(slots * paths, ((scaled, factors),), loadings, terms)


def ready_rows(own, theirs, stats, levels, sigma, ordered, terms):
    slots, paths, factors_n = own.shape
    rows = slots * paths
    count = ordered.shape[0]
    half = jax.ShapeDtypeStruct((rows, factors_n), BF16)
    return pl.pallas_call(
        ready_kernel,
        in_specs=[VMEM] * 7,
        out_specs=[VMEM] * 3,
        out_shape=[half, half, jax.ShapeDtypeStruct((count, factors_n), F32)],
        compiler_params=small(16),
        cost_estimate=cost_of(rows, count, factors_n),
        name="ready_rows",
    )(own, theirs, stats, levels, sigma, ordered, terms)


def cross_of(tile, halves, loadings, terms):
    strikes, hedge, scale = terms[:, 0:1], terms[:, 1:2], terms[:, 2:3]
    part = loadings[...]
    each = halves[0][0].shape[0] // tile
    places = [(half, r * tile) for half in range(len(halves)) for r in range(each)]

    def level(half, at):
        rows = halves[half][1][at : at + tile, :]
        return lax.dot_general(
            part, rows, (((1,), (1,)), ((), ())), preferred_element_type=F32
        )

    total = None
    current = level(*places[0])
    for k, (half, at) in enumerate(places):
        after = level(*places[k + 1]) if k + 1 < len(places) else None
        weight = (jnp.tanh(current - strikes) * hedge + hedge).astype(BF16)
        cross = jnp.dot(
            weight, halves[half][0][at : at + tile, :], preferred_element_type=F32
        )
        total = cross if total is None else total + cross
        current = after
    return total * scale


def first_kernel(
    own, theirs, stats, levels, sigma, done, loadings, terms, scaled, factors, *outs
):
    slots, paths, _ = own.shape
    prepare(own, theirs, stats, levels, sigma, scaled, factors, False, 0, slots)
    sums = cross_of(slots * paths, ((scaled, factors),), loadings, terms)
    give(done[...] + sums, *outs)


def next_kernel(tile, s0, f0, s1, f1, loadings, terms, *outs):
    give(cross_of(tile, ((s0, f0), (s1, f1)), loadings, terms), *outs)


def give(sums, *outs):
    at = 0
    for out in outs:
        out[...] = sums[at : at + out.shape[0]]
        at += out.shape[0]


def cost_of(rows, count, factors_n):
    return pl.CostEstimate(
        flops=2 * rows * count * factors_n,
        bytes_accessed=4 * count * factors_n,
        transcendentals=0,
    )


def tile_of(slots, paths):
    return paths * split_of(slots, max(1, 1280 // paths))


def first_chunk(sizes, own, theirs, stats, levels, sigma, done, ordered, terms):
    slots, paths, factors_n = own.shape
    count = ordered.shape[0]
    half = jax.ShapeDtypeStruct((slots * paths, factors_n), BF16)
    return pl.pallas_call(
        first_kernel,
        in_specs=[VMEM] * 8,
        out_specs=[VMEM] * (2 + len(sizes)),
        out_shape=[half, half] + [jax.ShapeDtypeStruct((n, factors_n), F32) for n in sizes],
        compiler_params=small(16),
        cost_estimate=cost_of(slots * paths, count, factors_n),
        name="first_chunk",
    )(own, theirs, stats, levels, sigma, done, ordered, terms)


def next_chunk(sizes, tile, ready, rest, ordered, terms):
    rows, factors_n = ready[0].shape
    count = ordered.shape[0]
    return pl.pallas_call(
        functools.partial(next_kernel, tile),
        in_specs=[VMEM] * 6,
        out_specs=[VMEM] * len(sizes),
        out_shape=[jax.ShapeDtypeStruct((n, factors_n), F32) for n in sizes],
        compiler_params=small(16),
        cost_estimate=cost_of(2 * rows, count, factors_n),
        name="next_chunk",
    )(*ready, *rest, ordered, terms)


def body(normals, states, loadings, strikes, hedge, sigma, tail):
    groups = lax.axis_size("outer")
    inner = lax.axis_size("inner")
    chips = inner // 2
    _, per_node, factors_n = normals.shape
    instruments = loadings.shape[0]
    tail_count = tail.shape[0]
    paths = per_node * inner
    rows = instruments // (groups * inner)
    paired = chips & (chips - 1) == 0

    def partner(of, d):
        return of ^ d if paired else (of + d) % chips

    def beyond(of, s):
        return of ^ s if groups & (groups - 1) == 0 else (of + s) % groups

    def to_core(x):
        return lax.ppermute(x, "inner", [(i, i ^ 1) for i in range(inner)])

    def to_chip(x, d):
        return lax.ppermute(
            x, "inner", [(i, partner(i // 2, d) * 2 + i % 2) for i in range(inner)]
        )

    def to_group(x, s):
        return lax.ppermute(x, "outer", [(g, beyond(g, s)) for g in range(groups)])

    bound = 32768.0 / (tail_count * paths)
    unit = 1.0 / (bound * tail_count * paths)

    tail, normals, states, loadings = (
        pltpu.with_memory_space_constraint(x, pltpu.HBM)
        for x in (tail, normals, states, loadings.reshape(groups * inner, rows, factors_n))
    )
    wide = 128 if 128 % rows == 0 else rows
    strikes, hedge = strikes.reshape(-1, wide), hedge.reshape(-1, wide)

    chosen, mine, other = gather_nodes(tail, normals)
    sums, squares = mine + to_core(other)
    count = 2 * per_node
    within = squares - sums * sums / count
    message = to_message(sums, within)
    chosen, message, strikes = lax.optimization_barrier((chosen, message, strikes))
    rounds = [1 << k for k in range(chips.bit_length() - 1)] if paired and chips > 4 else []
    if not rounds:
        arrived = [of_message(to_chip(message, d)) for d in range(chips - 1, 0, -1)]
        sums, within = pooled([(sums, within), *arrived], count)
        count *= chips
    for d in rounds:
        arrived = to_chip(message, d)
        sums, within = pooled([(sums, within), of_message(arrived)], count)
        count *= 2
        if d != rounds[-1]:
            message = to_message(sums, within)
    theirs = to_core(chosen)
    steps = range(groups)
    relayed = chips == 4 and groups % 2 == 0
    if relayed:
        half = groups // 2
        low, high = steps[:half], steps[half:]
        plan = [
            [(3, s) for s in low] + [(2, s) for s in low] + [(3, s) for s in high],
            [(1, s) for s in high] + [(2, s) for s in high],
            [(0, s) for s in steps],
            [(1, s) for s in low],
        ]
        first_sizes = (2 * half * rows, half * rows)
    else:
        plan = [[(d, s) for s in steps] for d in range(chips - 1, -1, -1)]
        first_sizes = (groups * rows,)
    far = lambda chip, d, group, s: (partner(chip, d), beyond(group, s))
    levels, live, gain, *parts = order(
        unit, bound, plan, far, tail, states, loadings, strikes, hedge
    )
    ordered = [part.reshape(-1, factors_n) for part in parts[: len(plan)]]
    terms = parts[len(plan) :]
    sums, within, theirs, levels, live, gain, ordered, terms = lax.optimization_barrier(
        (sums, within, theirs, levels, live, gain, ordered, terms)
    )
    stats = jnp.stack([sums / count, live * lax.rsqrt(within / count + EPSILON)])
    their_stats = to_core(stats)

    sigmas = sigma.reshape(1, factors_n)
    *ready, done = ready_rows(chosen, theirs, stats, levels, sigmas, ordered[0], terms[0])

    tile = tile_of(CAP, per_node)
    results = first_chunk(
        first_sizes, chosen, theirs, their_stats, levels, sigmas, done, ordered[0], terms[0]
    )
    rest, first = tuple(results[:2]), results[2:]

    def chunk(k, sizes, *after):
        kept, _ = lax.optimization_barrier((rest, after))
        return next_chunk(sizes, tile, ready, kept, ordered[k], terms[k])

    def plus(x, y):
        return x + y.astype(F32)

    if relayed:
        size = half * rows
        a32, b3 = (x.astype(F16) for x in first)
        from_b3, from_a32 = to_chip(b3, 1), to_chip(a32, 2)
        b1, b2 = chunk(1, (size, size), a32, b3)
        b1, b2 = b1.astype(F16), plus(b2, from_b3).astype(F16)
        from_b1, from_b2 = to_chip(b1, 1), to_chip(b2, 2)
        a0, b0 = chunk(2, (size, size), b1, b2)
        (a1,) = chunk(3, (size,), a0, b0, from_a32)
        from_a3, from_a2 = from_a32[:size], from_a32[size:]
        a1 = plus(a1, from_a3).astype(F16)
        from_a1 = to_chip(a1, 1)
        b0, _ = lax.optimization_barrier((b0, a1))
        kept = (plus(plus(a0, from_a2), from_a1), plus(plus(b0, from_b1), from_b2))
        part = lambda s: kept[s // half][s % half * rows :][:rows]
    else:
        arrived = []
        (kept,) = first
        for k in range(1, chips):
            sent = kept.astype(F16)
            arrived.append(to_chip(sent, chips - k))
            (kept,) = chunk(k, first_sizes, sent)
        for item in arrived:
            kept = plus(kept, item)
        part = lambda s: kept[s * rows :][:rows]
    owned = part(0)
    for s in sorted(range(1, groups), key=lambda s: (s < groups // 2, s)):
        owned = plus(owned, to_group(part(s).astype(F16), s))
    return gain * owned


def solution(mesh):
    placed = (P("outer", "inner", None), P("outer", None), P(), P(), P(), P(), P())
    return jax.shard_map(
        body, mesh=mesh, in_specs=placed, out_specs=P(("outer", "inner"), None), check_vma=False
    )
```

```python
import functools

import jax
import jax.numpy as jnp
from jax import lax
from jax.experimental import pallas as pl
from jax.experimental.pallas import tpu as pltpu
from jax.sharding import PartitionSpec as P

CAP = 80
EPSILON = 1e-06
VMEM = pl.BlockSpec(memory_space=pltpu.VMEM)
SMEM = pl.BlockSpec(memory_space=pltpu.SMEM)
HBM = pl.BlockSpec(memory_space=pltpu.HBM)
F32 = jnp.float32
BF16 = jnp.bfloat16
F16 = jnp.float16


def split_of(count, most):
    for size in range(min(count, most), 0, -1):
        if count % size == 0:
            return size
    return 1


def small(mebibytes):
    return pltpu.CompilerParams(vmem_limit_bytes=mebibytes << 20)


def first_of(tail, base):
    count = tail.shape[0]
    first = jnp.int32(0)
    for bit in range(count.bit_length() - 1, -1, -1):
        ahead = first + (1 << bit)
        below = tail[jnp.minimum(ahead, count) - 1] < base
        first = jnp.where((ahead <= count) & below, ahead, first)
    return first


def place_of(tail, first, base, slot):
    at = slot + lax.rem(lax.axis_index("inner"), 2) * (CAP // 2)
    at = first + jnp.where(at >= CAP, at - CAP, at)
    node = tail[jnp.minimum(at, tail.shape[0] - 1)] - base
    return node, at < tail.shape[0]


def gather_kernel(
    part, tail_hbm, normals, chosen_hbm, mine, other,
    tail, chosen, tail_sem, sems, out_sem,
):
    node_count = normals.shape[0]
    tail_copy = pltpu.make_async_copy(tail_hbm, tail, tail_sem)
    tail_copy.start()
    base = lax.axis_index("outer") * node_count
    tail_copy.wait()
    first = first_of(tail, base)
    parts = CAP // part

    @pl.loop(0, parts)
    def _(p):
        for k in range(part):
            slot = p * part + k
            node, inside = place_of(tail, first, base, slot)
            used = inside & (node >= 0) & (node < node_count)
            node = jnp.where(used, node, lax.rem(slot, node_count))
            pltpu.make_async_copy(normals.at[node], chosen.at[slot], sems.at[p]).start()

    out_copy = pltpu.make_async_copy(chosen, chosen_hbm, out_sem)
    for begin, sums in ((0, mine), (parts // 2, other)):

        @pl.loop(0, parts // 2)
        def _(p):
            piece = chosen.at[pl.ds((begin + p) * part, part)]
            pltpu.make_async_copy(piece, piece, sems.at[begin + p]).wait()
            there = chosen_hbm.at[pl.ds((begin + p) * part, part)]
            pltpu.make_async_copy(piece, there, out_sem).start()
            values = piece[...].astype(F32)
            rows = pl.ds(pl.multiple_of(p * part, part), part)
            sums[0, rows, :] = jnp.sum(values, axis=1)
            sums[1, rows, :] = jnp.sum(values * values, axis=1)

    out_copy.wait()


def gather_nodes(tail, normals):
    _, paths, factors_n = normals.shape
    part = split_of(CAP // 2, 8)
    sums = jax.ShapeDtypeStruct((2, CAP // 2, factors_n), F32)
    chosen = (CAP, paths, factors_n)
    return pl.pallas_call(
        functools.partial(gather_kernel, part),
        in_specs=[HBM, HBM],
        out_specs=[HBM, VMEM, VMEM],
        out_shape=[
            pltpu.HBM(chosen, BF16),
            sums,
            sums,
        ],
        scratch_shapes=[
            pltpu.SMEM(tail.shape, jnp.int32),
            pltpu.VMEM(chosen, BF16),
            pltpu.SemaphoreType.DMA,
            pltpu.SemaphoreType.DMA((CAP // part,)),
            pltpu.SemaphoreType.DMA,
        ],
        compiler_params=small(8),
        cost_estimate=pl.CostEstimate(flops=0, bytes_accessed=0, transcendentals=0),
        name="gather_nodes",
    )(tail, normals)


def to_message(sums, within):
    high = sums.astype(F16)
    low = (sums - high.astype(F32)).astype(F16)
    return jnp.stack([high, low, within.astype(F16)])


def pooled(parts, count):
    total = sum(s for s, _ in parts)
    center = total / (count * len(parts))
    return total, sum(w + (s / count - center) ** 2 * count for s, w in parts)


def of_message(message):
    high, low, within = message.astype(F32)
    return high + low, within


def order_kernel(
    unit, bound, plan, far, tail_hbm, states_hbm, loadings_hbm, strikes, hedge,
    levels, live, gain, *refs,
):
    chunks, rows = len(plan), gain.shape[0]
    cells = [(chunk, step) for chunk in range(chunks) for step in range(len(plan[chunk]))]
    ordered, terms = refs[:chunks], refs[chunks : 2 * chunks]
    tail, states, onehot, own, tail_sem, states_sem, sems = refs[2 * chunks :]
    node_count = states.shape[0]
    position = lax.axis_index("inner")
    group, chip, core = lax.axis_index("outer"), position // 2, lax.rem(position, 2)
    tail_copy = pltpu.make_async_copy(tail_hbm, tail, tail_sem)
    states_copy = pltpu.make_async_copy(states_hbm, states, states_sem)
    tail_copy.start()
    states_copy.start()
    blocks, copies = [], []
    for k, (chunk, step) in enumerate(cells):
        d, away = plan[chunk][step]
        to_chip, to_group = far(chip, d, group, away)
        block = (to_group * (lax.axis_size("inner") // 2) + to_chip) * 2 + core
        copy = pltpu.make_async_copy(loadings_hbm.at[block], own.at[k], sems.at[k])
        copy.start()
        blocks.append(block)
        copies.append(copy)
    wide = strikes.shape[1]
    lanes = lax.broadcasted_iota(jnp.int32, (rows, wide), 1)
    lines = lax.broadcasted_iota(jnp.int32, (rows, wide), 0)

    def column(ref, block):
        line = ref[pl.ds(block * rows // wide, 1), :]
        here = lanes == lines + lax.rem(block * rows, wide)
        return jnp.sum(jnp.where(here, line, 0.0), axis=1, keepdims=True)

    for k, block in enumerate(blocks):
        chunk, step = cells[k]
        at = slice(step * rows, (step + 1) * rows)
        size = column(hedge, block)
        scale = jnp.abs(size)
        terms[chunk][at, 0:1] = column(strikes, block) * 0.5
        terms[chunk][at, 1:2] = size * 0.5
        terms[chunk][at, 2:3] = jnp.where(
            scale > 1e-30, bound / jnp.maximum(scale, 1e-30), 0.0
        )
        if plan[chunk][step] == (0, 0):
            owned = scale * unit
    tail_copy.wait()
    base = group * node_count
    first = first_of(tail, base)
    nodes = lax.broadcasted_iota(jnp.int32, (1, node_count), 1)
    for slot in range(CAP):
        node, inside = place_of(tail, first, base, slot)
        used = inside & (node >= 0) & (node < node_count)
        onehot[slot : slot + 1, :] = ((nodes == node) & used).astype(F32)
        if slot < CAP // 2:
            live[slot : slot + 1, :] = jnp.full((1, live.shape[1]), used.astype(F32))
    states_copy.wait()
    levels[...] = jnp.dot(
        onehot[...].astype(BF16), states[...], preferred_element_type=F32
    )
    for k, copy in enumerate(copies):
        copy.wait()
        values = own[k].astype(F32)
        chunk, step = cells[k]
        if plan[chunk][step] == (0, 0):
            gain[...] = values * owned
        ordered[chunk][step] = (values * 0.5).astype(BF16)


def order(unit, bound, plan, far, tail, states, loadings, strikes, hedge):
    chunks, cells = len(plan), sum(len(part) for part in plan)
    _, rows, factors_n = loadings.shape
    return pl.pallas_call(
        functools.partial(order_kernel, unit, bound, plan, far),
        in_specs=[HBM] * 3 + [VMEM] * 2,
        out_specs=[VMEM] * (2 * chunks + 3),
        out_shape=[
            jax.ShapeDtypeStruct((count, factors_n), F32) for count in (CAP, CAP // 2, rows)
        ]
        + [jax.ShapeDtypeStruct((len(part), rows, factors_n), BF16) for part in plan]
        + [jax.ShapeDtypeStruct((len(part) * rows, 3), F32) for part in plan],
        scratch_shapes=[
            pltpu.SMEM(tail.shape, jnp.int32),
            pltpu.VMEM(states.shape, BF16),
            pltpu.VMEM((CAP, states.shape[0]), F32),
            pltpu.VMEM((cells, rows, factors_n), BF16),
            pltpu.SemaphoreType.DMA,
            pltpu.SemaphoreType.DMA,
            pltpu.SemaphoreType.DMA((cells,)),
        ],
        compiler_params=small(12),
        cost_estimate=pl.CostEstimate(flops=0, bytes_accessed=1 << 20, transcendentals=0),
        name="order_instruments",
    )(tail, states, loadings, strikes, hedge)


def prepare(own, theirs, stats, levels, sigma, scaled, factors, ready, begin, end):
    slots, paths, factors_n = own.shape
    half = slots // 2
    shape = (paths, factors_n)
    sigmas = jnp.broadcast_to(sigma[...], shape)
    for at in range(begin, end):
        mine, row = at < half, at % half
        slot = row if mine == ready else row + half
        source = own if mine else theirs
        place = slot if mine else (slot + half) % slots
        center = jnp.broadcast_to(stats[0, row : row + 1, :], shape)
        rstd = jnp.broadcast_to(stats[1, row : row + 1, :], shape)
        level = jnp.broadcast_to(levels[place : place + 1, :], shape)
        unit = ((source[slot].astype(F32) - center) * rstd).astype(BF16)
        rows = slice(at * paths, (at + 1) * paths)
        scaled[rows, :] = unit
        factors[rows, :] = (level + sigmas * unit.astype(F32)).astype(BF16)


def ready_kernel(own, theirs, stats, levels, sigma, loadings, terms, scaled, factors, out):
    slots, paths, _ = own.shape
    prepare(own, theirs, stats, levels, sigma, scaled, factors, True, 0, slots)
    out[...] = cross_of(slots * paths, ((scaled, factors),), loadings, terms)


def ready_rows(own, theirs, stats, levels, sigma, ordered, terms):
    slots, paths, factors_n = own.shape
    rows = slots * paths
    count = ordered.shape[0]
    half = jax.ShapeDtypeStruct((rows, factors_n), BF16)
    return pl.pallas_call(
        ready_kernel,
        in_specs=[VMEM] * 7,
        out_specs=[VMEM] * 3,
        out_shape=[half, half, jax.ShapeDtypeStruct((count, factors_n), F32)],
        compiler_params=small(16),
        cost_estimate=cost_of(rows, count, factors_n),
        name="ready_rows",
    )(own, theirs, stats, levels, sigma, ordered, terms)


def cross_of(tile, halves, loadings, terms):
    strikes, hedge, scale = terms[:, 0:1], terms[:, 1:2], terms[:, 2:3]
    part = loadings[...]
    each = halves[0][0].shape[0] // tile
    places = [(half, r * tile) for half in range(len(halves)) for r in range(each)]

    def level(half, at):
        rows = halves[half][1][at : at + tile, :]
        return lax.dot_general(
            part, rows, (((1,), (1,)), ((), ())), preferred_element_type=F32
        )

    total = None
    current = level(*places[0])
    for k, (half, at) in enumerate(places):
        after = level(*places[k + 1]) if k + 1 < len(places) else None
        weight = (jnp.tanh(current - strikes) * hedge + hedge).astype(BF16)
        cross = jnp.dot(
            weight, halves[half][0][at : at + tile, :], preferred_element_type=F32
        )
        total = cross if total is None else total + cross
        current = after
    return total * scale


def first_kernel(
    own, theirs, stats, levels, sigma, done, loadings, terms, scaled, factors, *outs
):
    slots, paths, _ = own.shape
    prepare(own, theirs, stats, levels, sigma, scaled, factors, False, 0, slots)
    sums = cross_of(slots * paths, ((scaled, factors),), loadings, terms)
    give(done[...] + sums, *outs)


def next_kernel(tile, s0, f0, s1, f1, loadings, terms, *outs):
    give(cross_of(tile, ((s0, f0), (s1, f1)), loadings, terms), *outs)


def give(sums, *outs):
    at = 0
    for out in outs:
        out[...] = sums[at : at + out.shape[0]]
        at += out.shape[0]


def cost_of(rows, count, factors_n):
    return pl.CostEstimate(
        flops=2 * rows * count * factors_n,
        bytes_accessed=4 * count * factors_n,
        transcendentals=0,
    )


def tile_of(slots, paths):
    return paths * split_of(slots, max(1, 1280 // paths))


def first_chunk(sizes, own, theirs, stats, levels, sigma, done, ordered, terms):
    slots, paths, factors_n = own.shape
    count = ordered.shape[0]
    half = jax.ShapeDtypeStruct((slots * paths, factors_n), BF16)
    return pl.pallas_call(
        first_kernel,
        in_specs=[VMEM] * 8,
        out_specs=[VMEM] * (2 + len(sizes)),
        out_shape=[half, half] + [jax.ShapeDtypeStruct((n, factors_n), F32) for n in sizes],
        compiler_params=small(16),
        cost_estimate=cost_of(slots * paths, count, factors_n),
        name="first_chunk",
    )(own, theirs, stats, levels, sigma, done, ordered, terms)


def next_chunk(sizes, tile, ready, rest, ordered, terms):
    rows, factors_n = ready[0].shape
    count = ordered.shape[0]
    return pl.pallas_call(
        functools.partial(next_kernel, tile),
        in_specs=[VMEM] * 6,
        out_specs=[VMEM] * len(sizes),
        out_shape=[jax.ShapeDtypeStruct((n, factors_n), F32) for n in sizes],
        compiler_params=small(16),
        cost_estimate=cost_of(2 * rows, count, factors_n),
        name="next_chunk",
    )(*ready, *rest, ordered, terms)


def body(normals, states, loadings, strikes, hedge, sigma, tail):
    groups = lax.axis_size("outer")
    inner = lax.axis_size("inner")
    chips = inner // 2
    _, per_node, factors_n = normals.shape
    instruments = loadings.shape[0]
    tail_count = tail.shape[0]
    paths = per_node * inner
    rows = instruments // (groups * inner)
    paired = chips & (chips - 1) == 0

    def partner(of, d):
        return of ^ d if paired else (of + d) % chips

    def beyond(of, s):
        return of ^ s if groups & (groups - 1) == 0 else (of + s) % groups

    def to_core(x):
        return lax.ppermute(x, "inner", [(i, i ^ 1) for i in range(inner)])

    def to_chip(x, d):
        return lax.ppermute(
            x, "inner", [(i, partner(i // 2, d) * 2 + i % 2) for i in range(inner)]
        )

    def to_group(x, s):
        return lax.ppermute(x, "outer", [(g, beyond(g, s)) for g in range(groups)])

    bound = 32768.0 / (tail_count * paths)
    unit = 1.0 / (bound * tail_count * paths)

    tail, normals, states, loadings = (
        pltpu.with_memory_space_constraint(x, pltpu.HBM)
        for x in (tail, normals, states, loadings.reshape(groups * inner, rows, factors_n))
    )
    wide = 128 if 128 % rows == 0 else rows
    strikes, hedge = strikes.reshape(-1, wide), hedge.reshape(-1, wide)

    chosen, mine, other = gather_nodes(tail, normals)
    sums, squares = mine + to_core(other)
    count = 2 * per_node
    within = squares - sums * sums / count
    message = to_message(sums, within)
    chosen, message, strikes = lax.optimization_barrier((chosen, message, strikes))
    rounds = [1 << k for k in range(chips.bit_length() - 1)] if paired and chips > 4 else []
    if not rounds:
        arrived = [of_message(to_chip(message, d)) for d in range(chips - 1, 0, -1)]
        sums, within = pooled([(sums, within), *arrived], count)
        count *= chips
    for d in rounds:
        arrived = to_chip(message, d)
        sums, within = pooled([(sums, within), of_message(arrived)], count)
        count *= 2
        if d != rounds[-1]:
            message = to_message(sums, within)
    theirs = to_core(chosen)
    steps = range(groups)
    relayed = chips == 4 and groups % 2 == 0
    if relayed:
        half = groups // 2
        low, high = steps[:half], steps[half:]
        plan = [
            [(3, s) for s in steps],
            [(1, s) for s in high] + [(2, s) for s in high],
            [(0, s) for s in steps] + [(2, s) for s in low] + [(1, s) for s in low],
        ]
        first_sizes = (half * rows,) * 2
    else:
        plan = [[(d, s) for s in steps] for d in range(chips - 1, -1, -1)]
        first_sizes = (groups * rows,)
    far = lambda chip, d, group, s: (partner(chip, d), beyond(group, s))
    levels, live, gain, *parts = order(
        unit, bound, plan, far, tail, states, loadings, strikes, hedge
    )
    ordered = [part.reshape(-1, factors_n) for part in parts[: len(plan)]]
    terms = parts[len(plan) :]
    sums, within, theirs, levels, live, gain, ordered, terms = lax.optimization_barrier(
        (sums, within, theirs, levels, live, gain, ordered, terms)
    )
    stats = jnp.stack([sums / count, live * lax.rsqrt(within / count + EPSILON)])
    their_stats = to_core(stats)

    sigmas = sigma.reshape(1, factors_n)
    *ready, done = ready_rows(chosen, theirs, stats, levels, sigmas, ordered[0], terms[0])

    tile = tile_of(CAP, per_node)
    results = first_chunk(
        first_sizes, chosen, theirs, their_stats, levels, sigmas, done, ordered[0], terms[0]
    )
    rest, first = tuple(results[:2]), results[2:]

    def chunk(k, sizes, *after):
        kept, _ = lax.optimization_barrier((rest, after))
        return next_chunk(sizes, tile, ready, kept, ordered[k], terms[k])

    def plus(x, y):
        return x + y.astype(F32)

    if relayed:
        size = half * rows
        a3, b3 = (x.astype(F16) for x in first)
        from_b3, from_a3 = to_chip(b3, 1), to_chip(a3, 2)
        b1, b2 = chunk(1, (size,) * 2, a3, b3)
        b1, b2 = b1.astype(F16), plus(b2, from_b3).astype(F16)
        from_b1, from_b2 = to_chip(b1, 1), to_chip(b2, 2)
        a0, b0, a2, a1 = chunk(2, (size,) * 4, b1, b2)
        a2, a1 = a2.astype(F16), plus(a1, from_a3).astype(F16)
        from_a2, from_a1 = to_chip(a2, 2), to_chip(a1, 1)
        b0, _ = lax.optimization_barrier((b0, (a2, a1)))
        kept = (plus(plus(a0, from_a2), from_a1), plus(plus(b0, from_b1), from_b2))
        part = lambda s: kept[s // half][s % half * rows :][:rows]
    else:
        arrived = []
        (kept,) = first
        for k in range(1, chips):
            sent = kept.astype(F16)
            arrived.append(to_chip(sent, chips - k))
            (kept,) = chunk(k, first_sizes, sent)
        for item in arrived:
            kept = plus(kept, item)
        part = lambda s: kept[s * rows :][:rows]
    owned = part(0)
    for s in sorted(range(1, groups), key=lambda s: (s < groups // 2, s)):
        owned = plus(owned, to_group(part(s).astype(F16), s))
    return gain * owned


def solution(mesh):
    placed = (P("outer", "inner", None), P("outer", None), P(), P(), P(), P(), P())
    return jax.shard_map(
        body, mesh=mesh, in_specs=placed, out_specs=P(("outer", "inner"), None), check_vma=False
    )
```

```python
import functools

import jax
import jax.numpy as jnp
from jax import lax
from jax.experimental import pallas as pl
from jax.experimental.pallas import tpu as pltpu
from jax.sharding import PartitionSpec as P

CAP = 80
EPSILON = 1e-06
VMEM = pl.BlockSpec(memory_space=pltpu.VMEM)
SMEM = pl.BlockSpec(memory_space=pltpu.SMEM)
HBM = pl.BlockSpec(memory_space=pltpu.HBM)
F32 = jnp.float32
BF16 = jnp.bfloat16
F16 = jnp.float16


def split_of(count, most):
    for size in range(min(count, most), 0, -1):
        if count % size == 0:
            return size
    return 1


def small(mebibytes):
    return pltpu.CompilerParams(vmem_limit_bytes=mebibytes << 20)


def first_of(tail, base):
    count = tail.shape[0]
    first = jnp.int32(0)
    for bit in range(count.bit_length() - 1, -1, -1):
        ahead = first + (1 << bit)
        below = tail[jnp.minimum(ahead, count) - 1] < base
        first = jnp.where((ahead <= count) & below, ahead, first)
    return first


def place_of(tail, first, base, slot):
    at = slot + lax.rem(lax.axis_index("inner"), 2) * (CAP // 2)
    at = first + jnp.where(at >= CAP, at - CAP, at)
    node = tail[jnp.minimum(at, tail.shape[0] - 1)] - base
    return node, at < tail.shape[0]


def gather_kernel(
    part, tail_hbm, normals, chosen_hbm, mine, other,
    tail, chosen, tail_sem, sems, out_sem,
):
    node_count = normals.shape[0]
    tail_copy = pltpu.make_async_copy(tail_hbm, tail, tail_sem)
    tail_copy.start()
    base = lax.axis_index("outer") * node_count
    tail_copy.wait()
    first = first_of(tail, base)
    parts = CAP // part

    @pl.loop(0, parts)
    def _(p):
        for k in range(part):
            slot = p * part + k
            node, inside = place_of(tail, first, base, slot)
            used = inside & (node >= 0) & (node < node_count)
            node = jnp.where(used, node, lax.rem(slot, node_count))
            pltpu.make_async_copy(normals.at[node], chosen.at[slot], sems.at[p]).start()

    out_copy = pltpu.make_async_copy(chosen, chosen_hbm, out_sem)
    for begin, sums in ((0, mine), (parts // 2, other)):

        @pl.loop(0, parts // 2)
        def _(p):
            piece = chosen.at[pl.ds((begin + p) * part, part)]
            pltpu.make_async_copy(piece, piece, sems.at[begin + p]).wait()
            there = chosen_hbm.at[pl.ds((begin + p) * part, part)]
            pltpu.make_async_copy(piece, there, out_sem).start()
            values = piece[...].astype(F32)
            rows = pl.ds(pl.multiple_of(p * part, part), part)
            sums[0, rows, :] = jnp.sum(values, axis=1)
            sums[1, rows, :] = jnp.sum(values * values, axis=1)

    out_copy.wait()


def gather_nodes(tail, normals):
    _, paths, factors_n = normals.shape
    part = split_of(CAP // 2, 8)
    sums = jax.ShapeDtypeStruct((2, CAP // 2, factors_n), F32)
    chosen = (CAP, paths, factors_n)
    return pl.pallas_call(
        functools.partial(gather_kernel, part),
        in_specs=[HBM, HBM],
        out_specs=[HBM, VMEM, VMEM],
        out_shape=[
            pltpu.HBM(chosen, BF16),
            sums,
            sums,
        ],
        scratch_shapes=[
            pltpu.SMEM(tail.shape, jnp.int32),
            pltpu.VMEM(chosen, BF16),
            pltpu.SemaphoreType.DMA,
            pltpu.SemaphoreType.DMA((CAP // part,)),
            pltpu.SemaphoreType.DMA,
        ],
        compiler_params=small(8),
        cost_estimate=pl.CostEstimate(flops=0, bytes_accessed=0, transcendentals=0),
        name="gather_nodes",
    )(tail, normals)


def to_message(sums, within):
    high = sums.astype(F16)
    low = (sums - high.astype(F32)).astype(F16)
    return jnp.stack([high, low, within.astype(F16)])


def pooled(parts, count):
    total = sum(s for s, _ in parts)
    center = total / (count * len(parts))
    return total, sum(w + (s / count - center) ** 2 * count for s, w in parts)


def of_message(message):
    high, low, within = message.astype(F32)
    return high + low, within


def order_kernel(
    unit, bound, plan, far, tail_hbm, states_hbm, loadings_hbm, strikes, hedge,
    levels, live, gain, *refs,
):
    chunks, rows = len(plan), gain.shape[0]
    cells = [(chunk, step) for chunk in range(chunks) for step in range(len(plan[chunk]))]
    ordered, terms = refs[:chunks], refs[chunks : 2 * chunks]
    tail, states, onehot, own, tail_sem, states_sem, sems = refs[2 * chunks :]
    node_count = states.shape[0]
    position = lax.axis_index("inner")
    group, chip, core = lax.axis_index("outer"), position // 2, lax.rem(position, 2)
    tail_copy = pltpu.make_async_copy(tail_hbm, tail, tail_sem)
    states_copy = pltpu.make_async_copy(states_hbm, states, states_sem)
    tail_copy.start()
    states_copy.start()
    blocks, copies = [], []
    for k, (chunk, step) in enumerate(cells):
        d, away = plan[chunk][step]
        to_chip, to_group = far(chip, d, group, away)
        block = (to_group * (lax.axis_size("inner") // 2) + to_chip) * 2 + core
        copy = pltpu.make_async_copy(loadings_hbm.at[block], own.at[k], sems.at[k])
        copy.start()
        blocks.append(block)
        copies.append(copy)
    wide = strikes.shape[1]
    lanes = lax.broadcasted_iota(jnp.int32, (rows, wide), 1)
    lines = lax.broadcasted_iota(jnp.int32, (rows, wide), 0)

    def column(ref, block):
        line = ref[pl.ds(block * rows // wide, 1), :]
        here = lanes == lines + lax.rem(block * rows, wide)
        return jnp.sum(jnp.where(here, line, 0.0), axis=1, keepdims=True)

    for k, block in enumerate(blocks):
        chunk, step = cells[k]
        at = slice(step * rows, (step + 1) * rows)
        size = column(hedge, block)
        scale = jnp.abs(size)
        terms[chunk][at, 0:1] = column(strikes, block) * 0.5
        terms[chunk][at, 1:2] = size * 0.5
        terms[chunk][at, 2:3] = jnp.where(
            scale > 1e-30, bound / jnp.maximum(scale, 1e-30), 0.0
        )
        if plan[chunk][step] == (0, 0):
            owned = scale * unit
    tail_copy.wait()
    base = group * node_count
    first = first_of(tail, base)
    nodes = lax.broadcasted_iota(jnp.int32, (1, node_count), 1)
    for slot in range(CAP):
        node, inside = place_of(tail, first, base, slot)
        used = inside & (node >= 0) & (node < node_count)
        onehot[slot : slot + 1, :] = ((nodes == node) & used).astype(F32)
        if slot < CAP // 2:
            live[slot : slot + 1, :] = jnp.full((1, live.shape[1]), used.astype(F32))
    states_copy.wait()
    levels[...] = jnp.dot(
        onehot[...].astype(BF16), states[...], preferred_element_type=F32
    )
    for k, copy in enumerate(copies):
        copy.wait()
        values = own[k].astype(F32)
        chunk, step = cells[k]
        if plan[chunk][step] == (0, 0):
            gain[...] = values * owned
        ordered[chunk][step] = (values * 0.5).astype(BF16)


def order(unit, bound, plan, far, tail, states, loadings, strikes, hedge):
    chunks, cells = len(plan), sum(len(part) for part in plan)
    _, rows, factors_n = loadings.shape
    return pl.pallas_call(
        functools.partial(order_kernel, unit, bound, plan, far),
        in_specs=[HBM] * 3 + [VMEM] * 2,
        out_specs=[VMEM] * (2 * chunks + 3),
        out_shape=[
            jax.ShapeDtypeStruct((count, factors_n), F32) for count in (CAP, CAP // 2, rows)
        ]
        + [jax.ShapeDtypeStruct((len(part), rows, factors_n), BF16) for part in plan]
        + [jax.ShapeDtypeStruct((len(part) * rows, 3), F32) for part in plan],
        scratch_shapes=[
            pltpu.SMEM(tail.shape, jnp.int32),
            pltpu.VMEM(states.shape, BF16),
            pltpu.VMEM((CAP, states.shape[0]), F32),
            pltpu.VMEM((cells, rows, factors_n), BF16),
            pltpu.SemaphoreType.DMA,
            pltpu.SemaphoreType.DMA,
            pltpu.SemaphoreType.DMA((cells,)),
        ],
        compiler_params=small(12),
        cost_estimate=pl.CostEstimate(flops=0, bytes_accessed=1 << 20, transcendentals=0),
        name="order_instruments",
    )(tail, states, loadings, strikes, hedge)


def prepare(own, theirs, stats, levels, sigma, scaled, factors, ready, begin, end):
    slots, paths, factors_n = own.shape
    half = slots // 2
    shape = (paths, factors_n)
    sigmas = jnp.broadcast_to(sigma[...], shape)
    for at in range(begin, end):
        mine, row = at < half, at % half
        slot = row if mine == ready else row + half
        source = own if mine else theirs
        place = slot if mine else (slot + half) % slots
        center = jnp.broadcast_to(stats[0, row : row + 1, :], shape)
        rstd = jnp.broadcast_to(stats[1, row : row + 1, :], shape)
        level = jnp.broadcast_to(levels[place : place + 1, :], shape)
        unit = ((source[slot].astype(F32) - center) * rstd).astype(BF16)
        rows = slice(at * paths, (at + 1) * paths)
        scaled[rows, :] = unit
        factors[rows, :] = (level + sigmas * unit.astype(F32)).astype(BF16)


def ready_kernel(own, theirs, stats, levels, sigma, loadings, terms, scaled, factors, out):
    slots, paths, _ = own.shape
    prepare(own, theirs, stats, levels, sigma, scaled, factors, True, 0, slots)
    out[...] = cross_of(slots * paths, ((scaled, factors),), loadings, terms)


def ready_rows(own, theirs, stats, levels, sigma, ordered, terms):
    slots, paths, factors_n = own.shape
    rows = slots * paths
    count = ordered.shape[0]
    half = jax.ShapeDtypeStruct((rows, factors_n), BF16)
    return pl.pallas_call(
        ready_kernel,
        in_specs=[VMEM] * 7,
        out_specs=[VMEM] * 3,
        out_shape=[half, half, jax.ShapeDtypeStruct((count, factors_n), F32)],
        compiler_params=small(16),
        cost_estimate=cost_of(rows, count, factors_n),
        name="ready_rows",
    )(own, theirs, stats, levels, sigma, ordered, terms)


def cross_of(tile, halves, loadings, terms):
    strikes, hedge, scale = terms[:, 0:1], terms[:, 1:2], terms[:, 2:3]
    part = loadings[...]
    each = halves[0][0].shape[0] // tile
    places = [(half, r * tile) for half in range(len(halves)) for r in range(each)]

    def level(half, at):
        rows = halves[half][1][at : at + tile, :]
        return lax.dot_general(
            part, rows, (((1,), (1,)), ((), ())), preferred_element_type=F32
        )

    total = None
    current = level(*places[0])
    for k, (half, at) in enumerate(places):
        after = level(*places[k + 1]) if k + 1 < len(places) else None
        weight = (jnp.tanh(current - strikes) * hedge + hedge).astype(BF16)
        cross = jnp.dot(
            weight, halves[half][0][at : at + tile, :], preferred_element_type=F32
        )
        total = cross if total is None else total + cross
        current = after
    return total * scale


def first_kernel(
    own, theirs, stats, levels, sigma, done, loadings, terms, scaled, factors, *outs
):
    slots, paths, _ = own.shape
    prepare(own, theirs, stats, levels, sigma, scaled, factors, False, 0, slots)
    sums = cross_of(slots * paths, ((scaled, factors),), loadings, terms)
    give(done[...] + sums, *outs)


def next_kernel(tile, s0, f0, s1, f1, loadings, terms, *outs):
    give(cross_of(tile, ((s0, f0), (s1, f1)), loadings, terms), *outs)


def give(sums, *outs):
    at = 0
    for out in outs:
        out[...] = sums[at : at + out.shape[0]]
        at += out.shape[0]


def cost_of(rows, count, factors_n):
    return pl.CostEstimate(
        flops=2 * rows * count * factors_n,
        bytes_accessed=4 * count * factors_n,
        transcendentals=0,
    )


def tile_of(slots, paths):
    return paths * split_of(slots, max(1, 1280 // paths))


def first_chunk(sizes, own, theirs, stats, levels, sigma, done, ordered, terms):
    slots, paths, factors_n = own.shape
    count = ordered.shape[0]
    half = jax.ShapeDtypeStruct((slots * paths, factors_n), BF16)
    return pl.pallas_call(
        first_kernel,
        in_specs=[VMEM] * 8,
        out_specs=[VMEM] * (2 + len(sizes)),
        out_shape=[half, half] + [jax.ShapeDtypeStruct((n, factors_n), F32) for n in sizes],
        compiler_params=small(16),
        cost_estimate=cost_of(slots * paths, count, factors_n),
        name="first_chunk",
    )(own, theirs, stats, levels, sigma, done, ordered, terms)


def next_chunk(sizes, tile, ready, rest, ordered, terms):
    rows, factors_n = ready[0].shape
    count = ordered.shape[0]
    return pl.pallas_call(
        functools.partial(next_kernel, tile),
        in_specs=[VMEM] * 6,
        out_specs=[VMEM] * len(sizes),
        out_shape=[jax.ShapeDtypeStruct((n, factors_n), F32) for n in sizes],
        compiler_params=small(16),
        cost_estimate=cost_of(2 * rows, count, factors_n),
        name="next_chunk",
    )(*ready, *rest, ordered, terms)


def body(normals, states, loadings, strikes, hedge, sigma, tail):
    groups = lax.axis_size("outer")
    inner = lax.axis_size("inner")
    chips = inner // 2
    _, per_node, factors_n = normals.shape
    instruments = loadings.shape[0]
    tail_count = tail.shape[0]
    paths = per_node * inner
    rows = instruments // (groups * inner)
    paired = chips & (chips - 1) == 0

    def partner(of, d):
        return of ^ d if paired else (of + d) % chips

    def beyond(of, s):
        return of ^ s if groups & (groups - 1) == 0 else (of + s) % groups

    def to_core(x):
        return lax.ppermute(x, "inner", [(i, i ^ 1) for i in range(inner)])

    def to_chip(x, d):
        return lax.ppermute(
            x, "inner", [(i, partner(i // 2, d) * 2 + i % 2) for i in range(inner)]
        )

    def to_group(x, s):
        return lax.ppermute(x, "outer", [(g, beyond(g, s)) for g in range(groups)])

    bound = 32768.0 / (tail_count * paths)
    unit = 1.0 / (bound * tail_count * paths)

    tail, normals, states, loadings = (
        pltpu.with_memory_space_constraint(x, pltpu.HBM)
        for x in (tail, normals, states, loadings.reshape(groups * inner, rows, factors_n))
    )
    wide = 128 if 128 % rows == 0 else rows
    strikes, hedge = strikes.reshape(-1, wide), hedge.reshape(-1, wide)

    chosen, mine, other = gather_nodes(tail, normals)
    sums, squares = mine + to_core(other)
    count = 2 * per_node
    within = squares - sums * sums / count
    message = to_message(sums, within)
    chosen, message, strikes = lax.optimization_barrier((chosen, message, strikes))
    rounds = [1 << k for k in range(chips.bit_length() - 1)] if paired and chips > 4 else []
    if not rounds:
        arrived = [of_message(to_chip(message, d)) for d in range(chips - 1, 0, -1)]
        sums, within = pooled([(sums, within), *arrived], count)
        count *= chips
    for d in rounds:
        arrived = to_chip(message, d)
        sums, within = pooled([(sums, within), of_message(arrived)], count)
        count *= 2
        if d != rounds[-1]:
            message = to_message(sums, within)
    theirs = to_core(chosen)
    steps = range(groups)
    relayed = chips == 4 and groups % 2 == 0
    if relayed:
        half = groups // 2
        low, high = steps[:half], steps[half:]
        plan = [
            [(3, s) for s in steps],
            [(1, s) for s in high] + [(2, s) for s in high],
            [(0, s) for s in steps] + [(2, s) for s in low] + [(1, s) for s in low],
        ]
        first_sizes = (half * rows,) * 2
    else:
        plan = [[(d, s) for s in steps] for d in range(chips - 1, -1, -1)]
        first_sizes = (groups * rows,)
    far = lambda chip, d, group, s: (partner(chip, d), beyond(group, s))
    levels, live, gain, *parts = order(
        unit, bound, plan, far, tail, states, loadings, strikes, hedge
    )
    ordered = [part.reshape(-1, factors_n) for part in parts[: len(plan)]]
    terms = parts[len(plan) :]
    sums, within, theirs, levels, live, gain, ordered, terms = lax.optimization_barrier(
        (sums, within, theirs, levels, live, gain, ordered, terms)
    )
    stats = jnp.stack([sums / count, live * lax.rsqrt(within / count + EPSILON)])
    their_stats = to_core(stats)

    sigmas = sigma.reshape(1, factors_n)
    *ready, done = ready_rows(chosen, theirs, stats, levels, sigmas, ordered[0], terms[0])

    tile = tile_of(CAP, per_node)
    results = first_chunk(
        first_sizes, chosen, theirs, their_stats, levels, sigmas, done, ordered[0], terms[0]
    )
    rest, first = tuple(results[:2]), results[2:]

    def chunk(k, sizes, *after):
        kept, _ = lax.optimization_barrier((rest, after))
        return next_chunk(sizes, tile, ready, kept, ordered[k], terms[k])

    def plus(x, y):
        return x + y.astype(F32)

    if relayed:
        size = half * rows
        a3, b3 = first
        b3 = b3.astype(F16)
        from_b3 = to_chip(b3, 1)
        b1, b2 = chunk(1, (size,) * 2, b3)
        a3, b1, b2 = lax.optimization_barrier((a3, b1, b2))
        a3 = a3.astype(F16)
        from_a3 = to_chip(a3, 2)
        b1, b2 = b1.astype(F16), plus(b2, from_b3).astype(F16)
        from_b1, from_b2 = to_chip(b1, 1), to_chip(b2, 2)
        a0, b0, a2, a1 = chunk(2, (size,) * 4, a3, b1, b2)
        a2, a1 = a2.astype(F16), plus(a1, from_a3).astype(F16)
        from_a2, from_a1 = to_chip(a2, 2), to_chip(a1, 1)
        b0, _ = lax.optimization_barrier((b0, (a2, a1)))
        kept_b = plus(plus(b0, from_b1), from_b2)
        sent = [kept_b[k * rows :][:rows].astype(F16) for k in range(half)]
        sent, a0 = lax.optimization_barrier((sent, a0))
        kept_a = plus(plus(a0, from_a2), from_a1)
        sent = [kept_a[k * rows :][:rows].astype(F16) for k in range(1, half)] + sent
        owned = kept_a[:rows]
    else:
        arrived = []
        (kept,) = first
        for k in range(1, chips):
            sent = kept.astype(F16)
            arrived.append(to_chip(sent, chips - k))
            (kept,) = chunk(k, first_sizes, sent)
        for item in arrived:
            kept = plus(kept, item)
        sent = [kept[s * rows :][:rows].astype(F16) for s in range(1, groups)]
        owned = kept[:rows]
    far_sums = None
    for s in range(max(1, groups // 2), groups):
        item = to_group(sent[s - 1], s).astype(F32)
        far_sums = item if far_sums is None else far_sums + item
    far_sums = lax.optimization_barrier(far_sums)
    for s in range(1, max(1, groups // 2)):
        owned = plus(owned, to_group(sent[s - 1], s))
    owned = owned + far_sums
    return gain * owned


def solution(mesh):
    placed = (P("outer", "inner", None), P("outer", None), P(), P(), P(), P(), P())
    return jax.shard_map(
        body, mesh=mesh, in_specs=placed, out_specs=P(("outer", "inner"), None), check_vma=False
    )
```

```python
import functools

import jax
import jax.numpy as jnp
from jax import lax
from jax.experimental import pallas as pl
from jax.experimental.pallas import tpu as pltpu
from jax.sharding import PartitionSpec as P

CAP = 80
EPSILON = 1e-06
VMEM = pl.BlockSpec(memory_space=pltpu.VMEM)
SMEM = pl.BlockSpec(memory_space=pltpu.SMEM)
HBM = pl.BlockSpec(memory_space=pltpu.HBM)
F32 = jnp.float32
BF16 = jnp.bfloat16
F16 = jnp.float16


def split_of(count, most):
    for size in range(min(count, most), 0, -1):
        if count % size == 0:
            return size
    return 1


def small(mebibytes):
    return pltpu.CompilerParams(vmem_limit_bytes=mebibytes << 20)


def first_of(tail, base):
    count = tail.shape[0]
    first = jnp.int32(0)
    for bit in range(count.bit_length() - 1, -1, -1):
        ahead = first + (1 << bit)
        below = tail[jnp.minimum(ahead, count) - 1] < base
        first = jnp.where((ahead <= count) & below, ahead, first)
    return first


def place_of(tail, first, base, slot):
    at = slot + lax.rem(lax.axis_index("inner"), 2) * (CAP // 2)
    at = first + jnp.where(at >= CAP, at - CAP, at)
    node = tail[jnp.minimum(at, tail.shape[0] - 1)] - base
    return node, at < tail.shape[0]


def gather_kernel(
    part, tail_hbm, normals, chosen_hbm, mine, other,
    tail, chosen, tail_sem, sems, out_sem,
):
    node_count = normals.shape[0]
    tail_copy = pltpu.make_async_copy(tail_hbm, tail, tail_sem)
    tail_copy.start()
    base = lax.axis_index("outer") * node_count
    tail_copy.wait()
    first = first_of(tail, base)
    parts = CAP // part

    @pl.loop(0, parts)
    def _(p):
        for k in range(part):
            slot = p * part + k
            node, inside = place_of(tail, first, base, slot)
            used = inside & (node >= 0) & (node < node_count)
            node = jnp.where(used, node, lax.rem(slot, node_count))
            pltpu.make_async_copy(normals.at[node], chosen.at[slot], sems.at[p]).start()

    out_copy = pltpu.make_async_copy(chosen, chosen_hbm, out_sem)
    for begin, sums in ((0, mine), (parts // 2, other)):

        @pl.loop(0, parts // 2)
        def _(p):
            piece = chosen.at[pl.ds((begin + p) * part, part)]
            pltpu.make_async_copy(piece, piece, sems.at[begin + p]).wait()
            there = chosen_hbm.at[pl.ds((begin + p) * part, part)]
            pltpu.make_async_copy(piece, there, out_sem).start()
            values = piece[...].astype(F32)
            rows = pl.ds(pl.multiple_of(p * part, part), part)
            sums[0, rows, :] = jnp.sum(values, axis=1)
            sums[1, rows, :] = jnp.sum(values * values, axis=1)

    out_copy.wait()


def gather_nodes(tail, normals):
    _, paths, factors_n = normals.shape
    part = split_of(CAP // 2, 8)
    sums = jax.ShapeDtypeStruct((2, CAP // 2, factors_n), F32)
    chosen = (CAP, paths, factors_n)
    return pl.pallas_call(
        functools.partial(gather_kernel, part),
        in_specs=[HBM, HBM],
        out_specs=[HBM, VMEM, VMEM],
        out_shape=[
            pltpu.HBM(chosen, BF16),
            sums,
            sums,
        ],
        scratch_shapes=[
            pltpu.SMEM(tail.shape, jnp.int32),
            pltpu.VMEM(chosen, BF16),
            pltpu.SemaphoreType.DMA,
            pltpu.SemaphoreType.DMA((CAP // part,)),
            pltpu.SemaphoreType.DMA,
        ],
        compiler_params=small(8),
        cost_estimate=pl.CostEstimate(flops=0, bytes_accessed=0, transcendentals=0),
        name="gather_nodes",
    )(tail, normals)


def to_message(sums, within):
    high = sums.astype(F16)
    low = (sums - high.astype(F32)).astype(F16)
    return jnp.stack([high, low, within.astype(F16)])


def pooled(parts, count):
    total = sum(s for s, _ in parts)
    center = total / (count * len(parts))
    return total, sum(w + (s / count - center) ** 2 * count for s, w in parts)


def of_message(message):
    high, low, within = message.astype(F32)
    return high + low, within


def order_kernel(
    unit, bound, plan, far, tail_hbm, states_hbm, loadings_hbm, strikes, hedge,
    levels, live, gain, *refs,
):
    chunks, rows = len(plan), gain.shape[0]
    cells = [(chunk, step) for chunk in range(chunks) for step in range(len(plan[chunk]))]
    ordered, terms = refs[:chunks], refs[chunks : 2 * chunks]
    tail, states, onehot, own, tail_sem, states_sem, sems = refs[2 * chunks :]
    node_count = states.shape[0]
    position = lax.axis_index("inner")
    group, chip, core = lax.axis_index("outer"), position // 2, lax.rem(position, 2)
    tail_copy = pltpu.make_async_copy(tail_hbm, tail, tail_sem)
    states_copy = pltpu.make_async_copy(states_hbm, states, states_sem)
    tail_copy.start()
    states_copy.start()
    blocks, copies = [], []
    for k, (chunk, step) in enumerate(cells):
        d, away = plan[chunk][step]
        to_chip, to_group = far(chip, d, group, away)
        block = (to_group * (lax.axis_size("inner") // 2) + to_chip) * 2 + core
        copy = pltpu.make_async_copy(loadings_hbm.at[block], own.at[k], sems.at[k])
        copy.start()
        blocks.append(block)
        copies.append(copy)
    wide = strikes.shape[1]
    lanes = lax.broadcasted_iota(jnp.int32, (rows, wide), 1)
    lines = lax.broadcasted_iota(jnp.int32, (rows, wide), 0)

    def column(ref, block):
        line = ref[pl.ds(block * rows // wide, 1), :]
        here = lanes == lines + lax.rem(block * rows, wide)
        return jnp.sum(jnp.where(here, line, 0.0), axis=1, keepdims=True)

    for k, block in enumerate(blocks):
        chunk, step = cells[k]
        at = slice(step * rows, (step + 1) * rows)
        size = column(hedge, block)
        scale = jnp.abs(size)
        terms[chunk][at, 0:1] = column(strikes, block) * 0.5
        terms[chunk][at, 1:2] = size * 0.5
        terms[chunk][at, 2:3] = jnp.where(
            scale > 1e-30, bound / jnp.maximum(scale, 1e-30), 0.0
        )
        if plan[chunk][step] == (0, 0):
            owned = scale * unit
    tail_copy.wait()
    base = group * node_count
    first = first_of(tail, base)
    nodes = lax.broadcasted_iota(jnp.int32, (1, node_count), 1)
    for slot in range(CAP):
        node, inside = place_of(tail, first, base, slot)
        used = inside & (node >= 0) & (node < node_count)
        onehot[slot : slot + 1, :] = ((nodes == node) & used).astype(F32)
        if slot < CAP // 2:
            live[slot : slot + 1, :] = jnp.full((1, live.shape[1]), used.astype(F32))
    states_copy.wait()
    levels[...] = jnp.dot(
        onehot[...].astype(BF16), states[...], preferred_element_type=F32
    )
    for k, copy in enumerate(copies):
        copy.wait()
        values = own[k].astype(F32)
        chunk, step = cells[k]
        if plan[chunk][step] == (0, 0):
            gain[...] = values * owned
        ordered[chunk][step] = (values * 0.5).astype(BF16)


def order(unit, bound, plan, far, tail, states, loadings, strikes, hedge):
    chunks, cells = len(plan), sum(len(part) for part in plan)
    _, rows, factors_n = loadings.shape
    return pl.pallas_call(
        functools.partial(order_kernel, unit, bound, plan, far),
        in_specs=[HBM] * 3 + [VMEM] * 2,
        out_specs=[VMEM] * (2 * chunks + 3),
        out_shape=[
            jax.ShapeDtypeStruct((count, factors_n), F32) for count in (CAP, CAP // 2, rows)
        ]
        + [jax.ShapeDtypeStruct((len(part), rows, factors_n), BF16) for part in plan]
        + [jax.ShapeDtypeStruct((len(part) * rows, 3), F32) for part in plan],
        scratch_shapes=[
            pltpu.SMEM(tail.shape, jnp.int32),
            pltpu.VMEM(states.shape, BF16),
            pltpu.VMEM((CAP, states.shape[0]), F32),
            pltpu.VMEM((cells, rows, factors_n), BF16),
            pltpu.SemaphoreType.DMA,
            pltpu.SemaphoreType.DMA,
            pltpu.SemaphoreType.DMA((cells,)),
        ],
        compiler_params=small(12),
        cost_estimate=pl.CostEstimate(flops=0, bytes_accessed=1 << 20, transcendentals=0),
        name="order_instruments",
    )(tail, states, loadings, strikes, hedge)


def prepare(own, theirs, stats, levels, sigma, scaled, factors, ready, begin, end):
    slots, paths, factors_n = own.shape
    half = slots // 2
    shape = (paths, factors_n)
    sigmas = jnp.broadcast_to(sigma[...], shape)
    for at in range(begin, end):
        mine, row = at < half, at % half
        slot = row if mine == ready else row + half
        source = own if mine else theirs
        place = slot if mine else (slot + half) % slots
        center = jnp.broadcast_to(stats[0, row : row + 1, :], shape)
        rstd = jnp.broadcast_to(stats[1, row : row + 1, :], shape)
        level = jnp.broadcast_to(levels[place : place + 1, :], shape)
        unit = ((source[slot].astype(F32) - center) * rstd).astype(BF16)
        rows = slice(at * paths, (at + 1) * paths)
        scaled[rows, :] = unit
        factors[rows, :] = (level + sigmas * unit.astype(F32)).astype(BF16)


def ready_kernel(own, theirs, stats, levels, sigma, loadings, terms, scaled, factors, out):
    slots, paths, _ = own.shape
    prepare(own, theirs, stats, levels, sigma, scaled, factors, True, 0, slots)
    out[...] = cross_of(slots * paths, ((scaled, factors),), loadings, terms)


def ready_rows(own, theirs, stats, levels, sigma, ordered, terms):
    slots, paths, factors_n = own.shape
    rows = slots * paths
    count = ordered.shape[0]
    half = jax.ShapeDtypeStruct((rows, factors_n), BF16)
    return pl.pallas_call(
        ready_kernel,
        in_specs=[VMEM] * 7,
        out_specs=[VMEM] * 3,
        out_shape=[half, half, jax.ShapeDtypeStruct((count, factors_n), F32)],
        compiler_params=small(16),
        cost_estimate=cost_of(rows, count, factors_n),
        name="ready_rows",
    )(own, theirs, stats, levels, sigma, ordered, terms)


def cross_of(tile, halves, loadings, terms):
    strikes, hedge, scale = terms[:, 0:1], terms[:, 1:2], terms[:, 2:3]
    part = loadings[...]
    each = halves[0][0].shape[0] // tile
    places = [(half, r * tile) for half in range(len(halves)) for r in range(each)]

    def level(half, at):
        rows = halves[half][1][at : at + tile, :]
        return lax.dot_general(
            part, rows, (((1,), (1,)), ((), ())), preferred_element_type=F32
        )

    total = None
    current = level(*places[0])
    for k, (half, at) in enumerate(places):
        after = level(*places[k + 1]) if k + 1 < len(places) else None
        weight = (jnp.tanh(current - strikes) * hedge + hedge).astype(BF16)
        cross = jnp.dot(
            weight, halves[half][0][at : at + tile, :], preferred_element_type=F32
        )
        total = cross if total is None else total + cross
        current = after
    return total * scale


def first_kernel(
    own, theirs, stats, levels, sigma, done, loadings, terms, scaled, factors, *outs
):
    slots, paths, _ = own.shape
    prepare(own, theirs, stats, levels, sigma, scaled, factors, False, 0, slots)
    sums = cross_of(slots * paths, ((scaled, factors),), loadings, terms)
    give(done[...] + sums, *outs)


def next_kernel(tile, s0, f0, s1, f1, loadings, terms, *outs):
    give(cross_of(tile, ((s0, f0), (s1, f1)), loadings, terms), *outs)


def give(sums, *outs):
    at = 0
    for out in outs:
        out[...] = sums[at : at + out.shape[0]]
        at += out.shape[0]


def cost_of(rows, count, factors_n):
    return pl.CostEstimate(
        flops=2 * rows * count * factors_n,
        bytes_accessed=4 * count * factors_n,
        transcendentals=0,
    )


def tile_of(slots, paths):
    return paths * split_of(slots, max(1, 1280 // paths))


def first_chunk(sizes, own, theirs, stats, levels, sigma, done, ordered, terms):
    slots, paths, factors_n = own.shape
    count = ordered.shape[0]
    half = jax.ShapeDtypeStruct((slots * paths, factors_n), BF16)
    return pl.pallas_call(
        first_kernel,
        in_specs=[VMEM] * 8,
        out_specs=[VMEM] * (2 + len(sizes)),
        out_shape=[half, half] + [jax.ShapeDtypeStruct((n, factors_n), F32) for n in sizes],
        compiler_params=small(16),
        cost_estimate=cost_of(slots * paths, count, factors_n),
        name="first_chunk",
    )(own, theirs, stats, levels, sigma, done, ordered, terms)


def next_chunk(sizes, tile, ready, rest, ordered, terms):
    rows, factors_n = ready[0].shape
    count = ordered.shape[0]
    return pl.pallas_call(
        functools.partial(next_kernel, tile),
        in_specs=[VMEM] * 6,
        out_specs=[VMEM] * len(sizes),
        out_shape=[jax.ShapeDtypeStruct((n, factors_n), F32) for n in sizes],
        compiler_params=small(16),
        cost_estimate=cost_of(2 * rows, count, factors_n),
        name="next_chunk",
    )(*ready, *rest, ordered, terms)


def body(normals, states, loadings, strikes, hedge, sigma, tail):
    groups = lax.axis_size("outer")
    inner = lax.axis_size("inner")
    chips = inner // 2
    _, per_node, factors_n = normals.shape
    instruments = loadings.shape[0]
    tail_count = tail.shape[0]
    paths = per_node * inner
    rows = instruments // (groups * inner)
    paired = chips & (chips - 1) == 0

    def partner(of, d):
        return of ^ d if paired else (of + d) % chips

    def beyond(of, s):
        return of ^ s if groups & (groups - 1) == 0 else (of + s) % groups

    def to_core(x):
        return lax.ppermute(x, "inner", [(i, i ^ 1) for i in range(inner)])

    def to_chip(x, d):
        return lax.ppermute(
            x, "inner", [(i, partner(i // 2, d) * 2 + i % 2) for i in range(inner)]
        )

    def to_group(x, s):
        return lax.ppermute(x, "outer", [(g, beyond(g, s)) for g in range(groups)])

    bound = 32768.0 / (tail_count * paths)
    unit = 1.0 / (bound * tail_count * paths)

    tail, normals, states, loadings = (
        pltpu.with_memory_space_constraint(x, pltpu.HBM)
        for x in (tail, normals, states, loadings.reshape(groups * inner, rows, factors_n))
    )
    wide = 128 if 128 % rows == 0 else rows
    strikes, hedge = strikes.reshape(-1, wide), hedge.reshape(-1, wide)

    chosen, mine, other = gather_nodes(tail, normals)
    sums, squares = mine + to_core(other)
    count = 2 * per_node
    within = squares - sums * sums / count
    message = to_message(sums, within)
    chosen, message, strikes = lax.optimization_barrier((chosen, message, strikes))
    rounds = [1 << k for k in range(chips.bit_length() - 1)] if paired and chips > 4 else []
    if not rounds:
        arrived = [of_message(to_chip(message, d)) for d in range(chips - 1, 0, -1)]
        sums, within = pooled([(sums, within), *arrived], count)
        count *= chips
    for d in rounds:
        arrived = to_chip(message, d)
        sums, within = pooled([(sums, within), of_message(arrived)], count)
        count *= 2
        if d != rounds[-1]:
            message = to_message(sums, within)
    theirs = to_core(chosen)
    steps = range(groups)
    relayed = chips == 4 and groups % 2 == 0
    if relayed:
        half = groups // 2
        low, high = steps[:half], steps[half:]
        plan = [
            [(3, s) for s in steps],
            [(1, s) for s in high] + [(2, s) for s in high] + [(0, s) for s in steps],
            [(2, s) for s in low] + [(1, s) for s in low],
        ]
        first_sizes = (half * rows,) * 2
    else:
        plan = [[(d, s) for s in steps] for d in range(chips - 1, -1, -1)]
        first_sizes = (groups * rows,)
    far = lambda chip, d, group, s: (partner(chip, d), beyond(group, s))
    levels, live, gain, *parts = order(
        unit, bound, plan, far, tail, states, loadings, strikes, hedge
    )
    ordered = [part.reshape(-1, factors_n) for part in parts[: len(plan)]]
    terms = parts[len(plan) :]
    sums, within, theirs, levels, live, gain, ordered, terms = lax.optimization_barrier(
        (sums, within, theirs, levels, live, gain, ordered, terms)
    )
    stats = jnp.stack([sums / count, live * lax.rsqrt(within / count + EPSILON)])
    their_stats = to_core(stats)

    sigmas = sigma.reshape(1, factors_n)
    *ready, done = ready_rows(chosen, theirs, stats, levels, sigmas, ordered[0], terms[0])

    tile = tile_of(CAP, per_node)
    results = first_chunk(
        first_sizes, chosen, theirs, their_stats, levels, sigmas, done, ordered[0], terms[0]
    )
    rest, first = tuple(results[:2]), results[2:]

    def chunk(k, sizes, *after):
        kept, _ = lax.optimization_barrier((rest, after))
        return next_chunk(sizes, tile, ready, kept, ordered[k], terms[k])

    def plus(x, y):
        return x + y.astype(F32)

    if relayed:
        size = half * rows
        a3, b3 = (x.astype(F16) for x in first)
        from_b3, from_a3 = to_chip(b3, 1), to_chip(a3, 2)
        b1, b2, a0, b0 = chunk(1, (size,) * 4, a3, b3)
        b1, b2 = b1.astype(F16), plus(b2, from_b3).astype(F16)
        from_b1, from_b2 = to_chip(b1, 1), to_chip(b2, 2)
        a2, a1 = chunk(2, (size,) * 2, b1, b2)
        a2, a1 = a2.astype(F16), plus(a1, from_a3).astype(F16)
        from_a2, from_a1 = to_chip(a2, 2), to_chip(a1, 1)
        b0, _ = lax.optimization_barrier((b0, (a2, a1)))
        kept_b = plus(plus(b0, from_b1), from_b2)
        sent = [kept_b[k * rows :][:rows].astype(F16) for k in range(half)]
        sent, a0 = lax.optimization_barrier((sent, a0))
        kept_a = plus(plus(a0, from_a2), from_a1)
        sent = [kept_a[k * rows :][:rows].astype(F16) for k in range(1, half)] + sent
        owned = kept_a[:rows]
    else:
        arrived = []
        (kept,) = first
        for k in range(1, chips):
            sent = kept.astype(F16)
            arrived.append(to_chip(sent, chips - k))
            (kept,) = chunk(k, first_sizes, sent)
        for item in arrived:
            kept = plus(kept, item)
        sent = [kept[s * rows :][:rows].astype(F16) for s in range(1, groups)]
        owned = kept[:rows]
    far_sums = None
    for s in range(max(1, groups // 2), groups):
        item = to_group(sent[s - 1], s).astype(F32)
        far_sums = item if far_sums is None else far_sums + item
    far_sums = lax.optimization_barrier(far_sums)
    for s in range(1, max(1, groups // 2)):
        owned = plus(owned, to_group(sent[s - 1], s))
    owned = owned + far_sums
    return gain * owned


def solution(mesh):
    placed = (P("outer", "inner", None), P("outer", None), P(), P(), P(), P(), P())
    return jax.shard_map(
        body, mesh=mesh, in_specs=placed, out_specs=P(("outer", "inner"), None), check_vma=False
    )
```

```python
import functools

import jax
import jax.numpy as jnp
from jax import lax
from jax.experimental import pallas as pl
from jax.experimental.pallas import tpu as pltpu
from jax.sharding import PartitionSpec as P

CAP = 80
EPSILON = 1e-06
VMEM = pl.BlockSpec(memory_space=pltpu.VMEM)
SMEM = pl.BlockSpec(memory_space=pltpu.SMEM)
HBM = pl.BlockSpec(memory_space=pltpu.HBM)
F32 = jnp.float32
BF16 = jnp.bfloat16
F16 = jnp.float16


def split_of(count, most):
    for size in range(min(count, most), 0, -1):
        if count % size == 0:
            return size
    return 1


def small(mebibytes):
    return pltpu.CompilerParams(vmem_limit_bytes=mebibytes << 20)


def first_of(tail, base):
    count = tail.shape[0]
    first = jnp.int32(0)
    for bit in range(count.bit_length() - 1, -1, -1):
        ahead = first + (1 << bit)
        below = tail[jnp.minimum(ahead, count) - 1] < base
        first = jnp.where((ahead <= count) & below, ahead, first)
    return first


def place_of(tail, first, base, slot):
    at = slot + lax.rem(lax.axis_index("inner"), 2) * (CAP // 2)
    at = first + jnp.where(at >= CAP, at - CAP, at)
    node = tail[jnp.minimum(at, tail.shape[0] - 1)] - base
    return node, at < tail.shape[0]


def gather_kernel(
    part, tail_hbm, normals, chosen_hbm, mine, other,
    tail, chosen, tail_sem, sems, out_sem,
):
    node_count = normals.shape[0]
    tail_copy = pltpu.make_async_copy(tail_hbm, tail, tail_sem)
    tail_copy.start()
    base = lax.axis_index("outer") * node_count
    tail_copy.wait()
    first = first_of(tail, base)
    parts = CAP // part

    @pl.loop(0, parts)
    def _(p):
        for k in range(part):
            slot = p * part + k
            node, inside = place_of(tail, first, base, slot)
            used = inside & (node >= 0) & (node < node_count)
            node = jnp.where(used, node, lax.rem(slot, node_count))
            pltpu.make_async_copy(normals.at[node], chosen.at[slot], sems.at[p]).start()

    out_copy = pltpu.make_async_copy(chosen, chosen_hbm, out_sem)
    for begin, sums in ((0, mine), (parts // 2, other)):

        @pl.loop(0, parts // 2)
        def _(p):
            piece = chosen.at[pl.ds((begin + p) * part, part)]
            pltpu.make_async_copy(piece, piece, sems.at[begin + p]).wait()
            there = chosen_hbm.at[pl.ds((begin + p) * part, part)]
            pltpu.make_async_copy(piece, there, out_sem).start()
            values = piece[...].astype(F32)
            rows = pl.ds(pl.multiple_of(p * part, part), part)
            sums[0, rows, :] = jnp.sum(values, axis=1)
            sums[1, rows, :] = jnp.sum(values * values, axis=1)

    out_copy.wait()


def gather_nodes(tail, normals):
    _, paths, factors_n = normals.shape
    part = split_of(CAP // 2, 8)
    sums = jax.ShapeDtypeStruct((2, CAP // 2, factors_n), F32)
    chosen = (CAP, paths, factors_n)
    return pl.pallas_call(
        functools.partial(gather_kernel, part),
        in_specs=[HBM, HBM],
        out_specs=[HBM, VMEM, VMEM],
        out_shape=[
            pltpu.HBM(chosen, BF16),
            sums,
            sums,
        ],
        scratch_shapes=[
            pltpu.SMEM(tail.shape, jnp.int32),
            pltpu.VMEM(chosen, BF16),
            pltpu.SemaphoreType.DMA,
            pltpu.SemaphoreType.DMA((CAP // part,)),
            pltpu.SemaphoreType.DMA,
        ],
        compiler_params=small(8),
        cost_estimate=pl.CostEstimate(flops=0, bytes_accessed=0, transcendentals=0),
        name="gather_nodes",
    )(tail, normals)


def to_message(sums, within):
    high = sums.astype(F16)
    low = (sums - high.astype(F32)).astype(F16)
    return jnp.stack([high, low, within.astype(F16)])


def pooled(parts, count):
    total = sum(s for s, _ in parts)
    center = total / (count * len(parts))
    return total, sum(w + (s / count - center) ** 2 * count for s, w in parts)


def of_message(message):
    high, low, within = message.astype(F32)
    return high + low, within


def order_kernel(
    unit, bound, plan, far, tail_hbm, states_hbm, loadings_hbm, strikes, hedge,
    levels, live, gain, *refs,
):
    chunks, rows = len(plan), gain.shape[0]
    cells = [(chunk, step) for chunk in range(chunks) for step in range(len(plan[chunk]))]
    ordered, terms = refs[:chunks], refs[chunks : 2 * chunks]
    tail, states, onehot, own, tail_sem, states_sem, sems = refs[2 * chunks :]
    node_count = states.shape[0]
    position = lax.axis_index("inner")
    group, chip, core = lax.axis_index("outer"), position // 2, lax.rem(position, 2)
    tail_copy = pltpu.make_async_copy(tail_hbm, tail, tail_sem)
    states_copy = pltpu.make_async_copy(states_hbm, states, states_sem)
    tail_copy.start()
    states_copy.start()
    blocks, copies = [], []
    for k, (chunk, step) in enumerate(cells):
        d, away = plan[chunk][step]
        to_chip, to_group = far(chip, core, d, group, away)
        block = (to_group * (lax.axis_size("inner") // 2) + to_chip) * 2 + core
        copy = pltpu.make_async_copy(loadings_hbm.at[block], own.at[k], sems.at[k])
        copy.start()
        blocks.append(block)
        copies.append(copy)
    wide = strikes.shape[1]
    lanes = lax.broadcasted_iota(jnp.int32, (rows, wide), 1)
    lines = lax.broadcasted_iota(jnp.int32, (rows, wide), 0)

    def column(ref, block):
        line = ref[pl.ds(block * rows // wide, 1), :]
        here = lanes == lines + lax.rem(block * rows, wide)
        return jnp.sum(jnp.where(here, line, 0.0), axis=1, keepdims=True)

    for k, block in enumerate(blocks):
        chunk, step = cells[k]
        at = slice(step * rows, (step + 1) * rows)
        size = column(hedge, block)
        scale = jnp.abs(size)
        terms[chunk][at, 0:1] = column(strikes, block) * 0.5
        terms[chunk][at, 1:2] = size * 0.5
        terms[chunk][at, 2:3] = jnp.where(
            scale > 1e-30, bound / jnp.maximum(scale, 1e-30), 0.0
        )
        if plan[chunk][step] == (0, 0):
            owned = scale * unit
    tail_copy.wait()
    base = group * node_count
    first = first_of(tail, base)
    nodes = lax.broadcasted_iota(jnp.int32, (1, node_count), 1)
    for slot in range(CAP):
        node, inside = place_of(tail, first, base, slot)
        used = inside & (node >= 0) & (node < node_count)
        onehot[slot : slot + 1, :] = ((nodes == node) & used).astype(F32)
        if slot < CAP // 2:
            live[slot : slot + 1, :] = jnp.full((1, live.shape[1]), used.astype(F32))
    states_copy.wait()
    levels[...] = jnp.dot(
        onehot[...].astype(BF16), states[...], preferred_element_type=F32
    )
    for k, copy in enumerate(copies):
        copy.wait()
        values = own[k].astype(F32)
        chunk, step = cells[k]
        if plan[chunk][step] == (0, 0):
            gain[...] = values * owned
        ordered[chunk][step] = (values * 0.5).astype(BF16)


def order(unit, bound, plan, far, tail, states, loadings, strikes, hedge):
    chunks, cells = len(plan), sum(len(part) for part in plan)
    _, rows, factors_n = loadings.shape
    return pl.pallas_call(
        functools.partial(order_kernel, unit, bound, plan, far),
        in_specs=[HBM] * 3 + [VMEM] * 2,
        out_specs=[VMEM] * (2 * chunks + 3),
        out_shape=[
            jax.ShapeDtypeStruct((count, factors_n), F32) for count in (CAP, CAP // 2, rows)
        ]
        + [jax.ShapeDtypeStruct((len(part), rows, factors_n), BF16) for part in plan]
        + [jax.ShapeDtypeStruct((len(part) * rows, 3), F32) for part in plan],
        scratch_shapes=[
            pltpu.SMEM(tail.shape, jnp.int32),
            pltpu.VMEM(states.shape, BF16),
            pltpu.VMEM((CAP, states.shape[0]), F32),
            pltpu.VMEM((cells, rows, factors_n), BF16),
            pltpu.SemaphoreType.DMA,
            pltpu.SemaphoreType.DMA,
            pltpu.SemaphoreType.DMA((cells,)),
        ],
        compiler_params=small(12),
        cost_estimate=pl.CostEstimate(flops=0, bytes_accessed=1 << 20, transcendentals=0),
        name="order_instruments",
    )(tail, states, loadings, strikes, hedge)


def prepare(own, theirs, stats, levels, sigma, scaled, factors, ready, begin, end):
    slots, paths, factors_n = own.shape
    half = slots // 2
    shape = (paths, factors_n)
    sigmas = jnp.broadcast_to(sigma[...], shape)
    for at in range(begin, end):
        mine, row = at < half, at % half
        slot = row if mine == ready else row + half
        source = own if mine else theirs
        place = slot if mine else (slot + half) % slots
        center = jnp.broadcast_to(stats[0, row : row + 1, :], shape)
        rstd = jnp.broadcast_to(stats[1, row : row + 1, :], shape)
        level = jnp.broadcast_to(levels[place : place + 1, :], shape)
        unit = ((source[slot].astype(F32) - center) * rstd).astype(BF16)
        rows = slice(at * paths, (at + 1) * paths)
        scaled[rows, :] = unit
        factors[rows, :] = (level + sigmas * unit.astype(F32)).astype(BF16)


def ready_kernel(own, theirs, stats, levels, sigma, loadings, terms, scaled, factors, out):
    slots, paths, _ = own.shape
    prepare(own, theirs, stats, levels, sigma, scaled, factors, True, 0, slots)
    out[...] = cross_of(slots * paths, ((scaled, factors),), loadings, terms)


def ready_rows(own, theirs, stats, levels, sigma, ordered, terms):
    slots, paths, factors_n = own.shape
    rows = slots * paths
    count = ordered.shape[0]
    half = jax.ShapeDtypeStruct((rows, factors_n), BF16)
    return pl.pallas_call(
        ready_kernel,
        in_specs=[VMEM] * 7,
        out_specs=[VMEM] * 3,
        out_shape=[half, half, jax.ShapeDtypeStruct((count, factors_n), F32)],
        compiler_params=small(16),
        cost_estimate=cost_of(rows, count, factors_n),
        name="ready_rows",
    )(own, theirs, stats, levels, sigma, ordered, terms)


def cross_of(tile, halves, loadings, terms):
    strikes, hedge, scale = terms[:, 0:1], terms[:, 1:2], terms[:, 2:3]
    part = loadings[...]
    each = halves[0][0].shape[0] // tile
    places = [(half, r * tile) for half in range(len(halves)) for r in range(each)]

    def level(half, at):
        rows = halves[half][1][at : at + tile, :]
        return lax.dot_general(
            part, rows, (((1,), (1,)), ((), ())), preferred_element_type=F32
        )

    total = None
    current = level(*places[0])
    for k, (half, at) in enumerate(places):
        after = level(*places[k + 1]) if k + 1 < len(places) else None
        weight = (jnp.tanh(current - strikes) * hedge + hedge).astype(BF16)
        cross = jnp.dot(
            weight, halves[half][0][at : at + tile, :], preferred_element_type=F32
        )
        total = cross if total is None else total + cross
        current = after
    return total * scale


def first_kernel(
    own, theirs, stats, levels, sigma, done, loadings, terms, scaled, factors, *outs
):
    slots, paths, _ = own.shape
    prepare(own, theirs, stats, levels, sigma, scaled, factors, False, 0, slots)
    sums = cross_of(slots * paths, ((scaled, factors),), loadings, terms)
    give(done[...] + sums, *outs)


def next_kernel(tile, s0, f0, s1, f1, loadings, terms, *outs):
    give(cross_of(tile, ((s0, f0), (s1, f1)), loadings, terms), *outs)


def give(sums, *outs):
    at = 0
    for out in outs:
        out[...] = sums[at : at + out.shape[0]]
        at += out.shape[0]


def cost_of(rows, count, factors_n):
    return pl.CostEstimate(
        flops=2 * rows * count * factors_n,
        bytes_accessed=4 * count * factors_n,
        transcendentals=0,
    )


def tile_of(slots, paths):
    return paths * split_of(slots, max(1, 1280 // paths))


def first_chunk(sizes, own, theirs, stats, levels, sigma, done, ordered, terms):
    slots, paths, factors_n = own.shape
    count = ordered.shape[0]
    half = jax.ShapeDtypeStruct((slots * paths, factors_n), BF16)
    return pl.pallas_call(
        first_kernel,
        in_specs=[VMEM] * 8,
        out_specs=[VMEM] * (2 + len(sizes)),
        out_shape=[half, half] + [jax.ShapeDtypeStruct((n, factors_n), F32) for n in sizes],
        compiler_params=small(16),
        cost_estimate=cost_of(slots * paths, count, factors_n),
        name="first_chunk",
    )(own, theirs, stats, levels, sigma, done, ordered, terms)


def next_chunk(sizes, tile, ready, rest, ordered, terms):
    rows, factors_n = ready[0].shape
    count = ordered.shape[0]
    return pl.pallas_call(
        functools.partial(next_kernel, tile),
        in_specs=[VMEM] * 6,
        out_specs=[VMEM] * len(sizes),
        out_shape=[jax.ShapeDtypeStruct((n, factors_n), F32) for n in sizes],
        compiler_params=small(16),
        cost_estimate=cost_of(2 * rows, count, factors_n),
        name="next_chunk",
    )(*ready, *rest, ordered, terms)


def body(normals, states, loadings, strikes, hedge, sigma, tail):
    groups = lax.axis_size("outer")
    inner = lax.axis_size("inner")
    chips = inner // 2
    _, per_node, factors_n = normals.shape
    instruments = loadings.shape[0]
    tail_count = tail.shape[0]
    paths = per_node * inner
    rows = instruments // (groups * inner)
    paired = chips & (chips - 1) == 0

    relayed = chips == 4 and groups % 2 == 0

    def partner(of, core, d):
        if relayed and d in (1, 2):
            d = d + (3 - 2 * d) * core
        return of ^ d if paired else (of + d) % chips

    def beyond(of, s):
        return of ^ s if groups & (groups - 1) == 0 else (of + s) % groups

    def to_core(x):
        return lax.ppermute(x, "inner", [(i, i ^ 1) for i in range(inner)])

    def to_chip(x, d):
        return lax.ppermute(
            x, "inner", [(i, partner(i // 2, i % 2, d) * 2 + i % 2) for i in range(inner)]
        )

    def to_group(x, s):
        return lax.ppermute(x, "outer", [(g, beyond(g, s)) for g in range(groups)])

    bound = 32768.0 / (tail_count * paths)
    unit = 1.0 / (bound * tail_count * paths)

    tail, normals, states, loadings = (
        pltpu.with_memory_space_constraint(x, pltpu.HBM)
        for x in (tail, normals, states, loadings.reshape(groups * inner, rows, factors_n))
    )
    wide = 128 if 128 % rows == 0 else rows
    strikes, hedge = strikes.reshape(-1, wide), hedge.reshape(-1, wide)

    chosen, mine, other = gather_nodes(tail, normals)
    sums, squares = mine + to_core(other)
    count = 2 * per_node
    within = squares - sums * sums / count
    message = to_message(sums, within)
    chosen, message, strikes = lax.optimization_barrier((chosen, message, strikes))
    rounds = [1 << k for k in range(chips.bit_length() - 1)] if paired and chips > 4 else []
    if not rounds:
        arrived = [of_message(to_chip(message, d)) for d in range(chips - 1, 0, -1)]
        sums, within = pooled([(sums, within), *arrived], count)
        count *= chips
    for d in rounds:
        arrived = to_chip(message, d)
        sums, within = pooled([(sums, within), of_message(arrived)], count)
        count *= 2
        if d != rounds[-1]:
            message = to_message(sums, within)
    theirs = to_core(chosen)
    steps = range(groups)
    if relayed:
        half = groups // 2
        low, high = steps[:half], steps[half:]
        plan = [
            [(3, s) for s in steps],
            [(1, s) for s in high] + [(2, s) for s in high] + [(0, s) for s in steps],
            [(2, s) for s in low] + [(1, s) for s in low],
        ]
        first_sizes = (half * rows,) * 2
    else:
        plan = [[(d, s) for s in steps] for d in range(chips - 1, -1, -1)]
        first_sizes = (groups * rows,)
    far = lambda chip, core, d, group, s: (partner(chip, core, d), beyond(group, s))
    levels, live, gain, *parts = order(
        unit, bound, plan, far, tail, states, loadings, strikes, hedge
    )
    ordered = [part.reshape(-1, factors_n) for part in parts[: len(plan)]]
    terms = parts[len(plan) :]
    sums, within, theirs, levels, live, gain, ordered, terms = lax.optimization_barrier(
        (sums, within, theirs, levels, live, gain, ordered, terms)
    )
    stats = jnp.stack([sums / count, live * lax.rsqrt(within / count + EPSILON)])
    their_stats = to_core(stats)

    sigmas = sigma.reshape(1, factors_n)
    *ready, done = ready_rows(chosen, theirs, stats, levels, sigmas, ordered[0], terms[0])

    tile = tile_of(CAP, per_node)
    results = first_chunk(
        first_sizes, chosen, theirs, their_stats, levels, sigmas, done, ordered[0], terms[0]
    )
    rest, first = tuple(results[:2]), results[2:]

    def chunk(k, sizes, *after):
        kept, _ = lax.optimization_barrier((rest, after))
        return next_chunk(sizes, tile, ready, kept, ordered[k], terms[k])

    def plus(x, y):
        return x + y.astype(F32)

    if relayed:
        size = half * rows
        a3, b3 = (x.astype(F16) for x in first)
        from_b3, from_a3 = to_chip(b3, 1), to_chip(a3, 2)
        b1, b2, a0, b0 = chunk(1, (size,) * 4, a3, b3)
        b1, b2 = b1.astype(F16), plus(b2, from_b3).astype(F16)
        from_b1, from_b2 = to_chip(b1, 1), to_chip(b2, 2)
        a2, a1 = chunk(2, (size,) * 2, b1, b2)
        a2, a1 = a2.astype(F16), plus(a1, from_a3).astype(F16)
        from_a2, from_a1 = to_chip(a2, 2), to_chip(a1, 1)
        b0, _ = lax.optimization_barrier((b0, (a2, a1)))
        kept_b = plus(plus(b0, from_b1), from_b2)
        sent = [kept_b[k * rows :][:rows].astype(F16) for k in range(half)]
        sent, a0 = lax.optimization_barrier((sent, a0))
        kept_a = plus(plus(a0, from_a2), from_a1)
        sent = [kept_a[k * rows :][:rows].astype(F16) for k in range(1, half)] + sent
        owned = kept_a[:rows]
    else:
        arrived = []
        (kept,) = first
        for k in range(1, chips):
            sent = kept.astype(F16)
            arrived.append(to_chip(sent, chips - k))
            (kept,) = chunk(k, first_sizes, sent)
        for item in arrived:
            kept = plus(kept, item)
        sent = [kept[s * rows :][:rows].astype(F16) for s in range(1, groups)]
        owned = kept[:rows]
    far_sums = None
    for s in range(max(1, groups // 2), groups):
        item = to_group(sent[s - 1], s).astype(F32)
        far_sums = item if far_sums is None else far_sums + item
    far_sums = lax.optimization_barrier(far_sums)
    for s in range(1, max(1, groups // 2)):
        owned = plus(owned, to_group(sent[s - 1], s))
    owned = owned + far_sums
    return gain * owned


def solution(mesh):
    placed = (P("outer", "inner", None), P("outer", None), P(), P(), P(), P(), P())
    return jax.shard_map(
        body, mesh=mesh, in_specs=placed, out_specs=P(("outer", "inner"), None), check_vma=False
    )
```

```python
import functools

import jax
import jax.numpy as jnp
from jax import lax
from jax.experimental import pallas as pl
from jax.experimental.pallas import tpu as pltpu
from jax.sharding import PartitionSpec as P

CAP = 80
EPSILON = 1e-06
VMEM = pl.BlockSpec(memory_space=pltpu.VMEM)
SMEM = pl.BlockSpec(memory_space=pltpu.SMEM)
HBM = pl.BlockSpec(memory_space=pltpu.HBM)
F32 = jnp.float32
BF16 = jnp.bfloat16
F16 = jnp.float16


def split_of(count, most):
    for size in range(min(count, most), 0, -1):
        if count % size == 0:
            return size
    return 1


def small(mebibytes):
    return pltpu.CompilerParams(vmem_limit_bytes=mebibytes << 20)


def first_of(tail, base):
    count = tail.shape[0]
    first = jnp.int32(0)
    for bit in range(count.bit_length() - 1, -1, -1):
        ahead = first + (1 << bit)
        below = tail[jnp.minimum(ahead, count) - 1] < base
        first = jnp.where((ahead <= count) & below, ahead, first)
    return first


def place_of(tail, first, base, slot):
    at = slot + lax.rem(lax.axis_index("inner"), 2) * (CAP // 2)
    at = first + jnp.where(at >= CAP, at - CAP, at)
    node = tail[jnp.minimum(at, tail.shape[0] - 1)] - base
    return node, at < tail.shape[0]


def gather_kernel(
    part, tail_hbm, normals, chosen_hbm, mine, other,
    tail, chosen, tail_sem, sems, out_sem,
):
    node_count = normals.shape[0]
    tail_copy = pltpu.make_async_copy(tail_hbm, tail, tail_sem)
    tail_copy.start()
    base = lax.axis_index("outer") * node_count
    tail_copy.wait()
    first = first_of(tail, base)
    parts = CAP // part

    @pl.loop(0, parts)
    def _(p):
        for k in range(part):
            slot = p * part + k
            node, inside = place_of(tail, first, base, slot)
            used = inside & (node >= 0) & (node < node_count)
            node = jnp.where(used, node, lax.rem(slot, node_count))
            pltpu.make_async_copy(normals.at[node], chosen.at[slot], sems.at[p]).start()

    out_copy = pltpu.make_async_copy(chosen, chosen_hbm, out_sem)
    for begin, sums in ((0, mine), (parts // 2, other)):

        @pl.loop(0, parts // 2)
        def _(p):
            piece = chosen.at[pl.ds((begin + p) * part, part)]
            pltpu.make_async_copy(piece, piece, sems.at[begin + p]).wait()
            there = chosen_hbm.at[pl.ds((begin + p) * part, part)]
            pltpu.make_async_copy(piece, there, out_sem).start()
            values = piece[...].astype(F32)
            rows = pl.ds(pl.multiple_of(p * part, part), part)
            sums[0, rows, :] = jnp.sum(values, axis=1)
            sums[1, rows, :] = jnp.sum(values * values, axis=1)

    out_copy.wait()


def gather_nodes(tail, normals):
    _, paths, factors_n = normals.shape
    part = split_of(CAP // 2, 8)
    sums = jax.ShapeDtypeStruct((2, CAP // 2, factors_n), F32)
    chosen = (CAP, paths, factors_n)
    return pl.pallas_call(
        functools.partial(gather_kernel, part),
        in_specs=[HBM, HBM],
        out_specs=[HBM, VMEM, VMEM],
        out_shape=[
            pltpu.HBM(chosen, BF16),
            sums,
            sums,
        ],
        scratch_shapes=[
            pltpu.SMEM(tail.shape, jnp.int32),
            pltpu.VMEM(chosen, BF16),
            pltpu.SemaphoreType.DMA,
            pltpu.SemaphoreType.DMA((CAP // part,)),
            pltpu.SemaphoreType.DMA,
        ],
        compiler_params=small(8),
        cost_estimate=pl.CostEstimate(flops=0, bytes_accessed=0, transcendentals=0),
        name="gather_nodes",
    )(tail, normals)


def to_message(sums, within):
    high = sums.astype(F16)
    low = (sums - high.astype(F32)).astype(F16)
    return jnp.stack([high, low, within.astype(F16)])


def pooled(parts, count):
    total = sum(s for s, _ in parts)
    center = total / (count * len(parts))
    return total, sum(w + (s / count - center) ** 2 * count for s, w in parts)


def of_message(message):
    high, low, within = message.astype(F32)
    return high + low, within


def order_kernel(
    unit, bound, plan, far, tail_hbm, states_hbm, loadings_hbm, strikes, hedge,
    levels, live, gain, *refs,
):
    chunks, rows = len(plan), gain.shape[0]
    cells = [(chunk, step) for chunk in range(chunks) for step in range(len(plan[chunk]))]
    ordered, terms = refs[:chunks], refs[chunks : 2 * chunks]
    tail, states, onehot, own, tail_sem, states_sem, sems = refs[2 * chunks :]
    node_count = states.shape[0]
    position = lax.axis_index("inner")
    group, chip, core = lax.axis_index("outer"), position // 2, lax.rem(position, 2)
    tail_copy = pltpu.make_async_copy(tail_hbm, tail, tail_sem)
    states_copy = pltpu.make_async_copy(states_hbm, states, states_sem)
    tail_copy.start()
    states_copy.start()
    blocks, copies = [], []
    for k, (chunk, step) in enumerate(cells):
        d, away = plan[chunk][step]
        to_chip, to_group = far(chip, d, group, away)
        block = (to_group * (lax.axis_size("inner") // 2) + to_chip) * 2 + core
        copy = pltpu.make_async_copy(loadings_hbm.at[block], own.at[k], sems.at[k])
        copy.start()
        blocks.append(block)
        copies.append(copy)
    wide = strikes.shape[1]
    lanes = lax.broadcasted_iota(jnp.int32, (rows, wide), 1)
    lines = lax.broadcasted_iota(jnp.int32, (rows, wide), 0)

    def column(ref, block):
        line = ref[pl.ds(block * rows // wide, 1), :]
        here = lanes == lines + lax.rem(block * rows, wide)
        return jnp.sum(jnp.where(here, line, 0.0), axis=1, keepdims=True)

    for k, block in enumerate(blocks):
        chunk, step = cells[k]
        at = slice(step * rows, (step + 1) * rows)
        size = column(hedge, block)
        scale = jnp.abs(size)
        terms[chunk][at, 0:1] = column(strikes, block) * 0.5
        terms[chunk][at, 1:2] = size * 0.5
        terms[chunk][at, 2:3] = jnp.where(
            scale > 1e-30, bound / jnp.maximum(scale, 1e-30), 0.0
        )
        if plan[chunk][step] == (0, 0):
            owned = scale * unit
    tail_copy.wait()
    base = group * node_count
    first = first_of(tail, base)
    nodes = lax.broadcasted_iota(jnp.int32, (1, node_count), 1)
    for slot in range(CAP):
        node, inside = place_of(tail, first, base, slot)
        used = inside & (node >= 0) & (node < node_count)
        onehot[slot : slot + 1, :] = ((nodes == node) & used).astype(F32)
        if slot < CAP // 2:
            live[slot : slot + 1, :] = jnp.full((1, live.shape[1]), used.astype(F32))
    states_copy.wait()
    levels[...] = jnp.dot(
        onehot[...].astype(BF16), states[...], preferred_element_type=F32
    )
    for k, copy in enumerate(copies):
        copy.wait()
        values = own[k].astype(F32)
        chunk, step = cells[k]
        if plan[chunk][step] == (0, 0):
            gain[...] = values * owned
        ordered[chunk][step] = (values * 0.5).astype(BF16)


def order(unit, bound, plan, far, tail, states, loadings, strikes, hedge):
    chunks, cells = len(plan), sum(len(part) for part in plan)
    _, rows, factors_n = loadings.shape
    return pl.pallas_call(
        functools.partial(order_kernel, unit, bound, plan, far),
        in_specs=[HBM] * 3 + [VMEM] * 2,
        out_specs=[VMEM] * (2 * chunks + 3),
        out_shape=[
            jax.ShapeDtypeStruct((count, factors_n), F32) for count in (CAP, CAP // 2, rows)
        ]
        + [jax.ShapeDtypeStruct((len(part), rows, factors_n), BF16) for part in plan]
        + [jax.ShapeDtypeStruct((len(part) * rows, 3), F32) for part in plan],
        scratch_shapes=[
            pltpu.SMEM(tail.shape, jnp.int32),
            pltpu.VMEM(states.shape, BF16),
            pltpu.VMEM((CAP, states.shape[0]), F32),
            pltpu.VMEM((cells, rows, factors_n), BF16),
            pltpu.SemaphoreType.DMA,
            pltpu.SemaphoreType.DMA,
            pltpu.SemaphoreType.DMA((cells,)),
        ],
        compiler_params=small(12),
        cost_estimate=pl.CostEstimate(flops=0, bytes_accessed=1 << 20, transcendentals=0),
        name="order_instruments",
    )(tail, states, loadings, strikes, hedge)


def prepare(own, theirs, stats, levels, sigma, scaled, factors, ready, begin, end):
    slots, paths, factors_n = own.shape
    half = slots // 2
    shape = (paths, factors_n)
    sigmas = jnp.broadcast_to(sigma[...], shape)
    for at in range(begin, end):
        mine, row = at < half, at % half
        slot = row if mine == ready else row + half
        source = own if mine else theirs
        place = slot if mine else (slot + half) % slots
        center = jnp.broadcast_to(stats[0, row : row + 1, :], shape)
        rstd = jnp.broadcast_to(stats[1, row : row + 1, :], shape)
        level = jnp.broadcast_to(levels[place : place + 1, :], shape)
        unit = ((source[slot].astype(F32) - center) * rstd).astype(BF16)
        rows = slice(at * paths, (at + 1) * paths)
        scaled[rows, :] = unit
        factors[rows, :] = (level + sigmas * unit.astype(F32)).astype(BF16)


def ready_kernel(own, theirs, stats, levels, sigma, loadings, terms, scaled, factors, out):
    slots, paths, _ = own.shape
    prepare(own, theirs, stats, levels, sigma, scaled, factors, True, 0, slots)
    out[...] = cross_of(slots * paths, ((scaled, factors),), loadings, terms)


def ready_rows(own, theirs, stats, levels, sigma, ordered, terms):
    slots, paths, factors_n = own.shape
    rows = slots * paths
    count = ordered.shape[0]
    half = jax.ShapeDtypeStruct((rows, factors_n), BF16)
    return pl.pallas_call(
        ready_kernel,
        in_specs=[VMEM] * 7,
        out_specs=[VMEM] * 3,
        out_shape=[half, half, jax.ShapeDtypeStruct((count, factors_n), F32)],
        compiler_params=small(16),
        cost_estimate=cost_of(rows, count, factors_n),
        name="ready_rows",
    )(own, theirs, stats, levels, sigma, ordered, terms)


def cross_of(tile, halves, loadings, terms):
    strikes, hedge, scale = terms[:, 0:1], terms[:, 1:2], terms[:, 2:3]
    part = loadings[...]
    each = halves[0][0].shape[0] // tile
    places = [(half, r * tile) for half in range(len(halves)) for r in range(each)]

    def level(half, at):
        rows = halves[half][1][at : at + tile, :]
        return lax.dot_general(
            part, rows, (((1,), (1,)), ((), ())), preferred_element_type=F32
        )

    total = None
    current = level(*places[0])
    for k, (half, at) in enumerate(places):
        after = level(*places[k + 1]) if k + 1 < len(places) else None
        weight = (jnp.tanh(current - strikes) * hedge + hedge).astype(BF16)
        cross = jnp.dot(
            weight, halves[half][0][at : at + tile, :], preferred_element_type=F32
        )
        total = cross if total is None else total + cross
        current = after
    return total * scale


def first_kernel(
    own, theirs, stats, levels, sigma, done, loadings, terms, scaled, factors, *outs
):
    slots, paths, _ = own.shape
    prepare(own, theirs, stats, levels, sigma, scaled, factors, False, 0, slots)
    sums = cross_of(slots * paths, ((scaled, factors),), loadings, terms)
    give(done[...] + sums, *outs)


def next_kernel(tile, s0, f0, s1, f1, loadings, terms, *outs):
    give(cross_of(tile, ((s0, f0), (s1, f1)), loadings, terms), *outs)


def give(sums, *outs):
    at = 0
    for out in outs:
        out[...] = sums[at : at + out.shape[0]]
        at += out.shape[0]


def cost_of(rows, count, factors_n):
    return pl.CostEstimate(
        flops=2 * rows * count * factors_n,
        bytes_accessed=4 * count * factors_n,
        transcendentals=0,
    )


def tile_of(slots, paths):
    return paths * split_of(slots, max(1, 1280 // paths))


def first_chunk(sizes, own, theirs, stats, levels, sigma, done, ordered, terms):
    slots, paths, factors_n = own.shape
    count = ordered.shape[0]
    half = jax.ShapeDtypeStruct((slots * paths, factors_n), BF16)
    return pl.pallas_call(
        first_kernel,
        in_specs=[VMEM] * 8,
        out_specs=[VMEM] * (2 + len(sizes)),
        out_shape=[half, half] + [jax.ShapeDtypeStruct((n, factors_n), F32) for n in sizes],
        compiler_params=small(16),
        cost_estimate=cost_of(slots * paths, count, factors_n),
        name="first_chunk",
    )(own, theirs, stats, levels, sigma, done, ordered, terms)


def next_chunk(sizes, tile, ready, rest, ordered, terms):
    rows, factors_n = ready[0].shape
    count = ordered.shape[0]
    return pl.pallas_call(
        functools.partial(next_kernel, tile),
        in_specs=[VMEM] * 6,
        out_specs=[VMEM] * len(sizes),
        out_shape=[jax.ShapeDtypeStruct((n, factors_n), F32) for n in sizes],
        compiler_params=small(16),
        cost_estimate=cost_of(2 * rows, count, factors_n),
        name="next_chunk",
    )(*ready, *rest, ordered, terms)


def body(normals, states, loadings, strikes, hedge, sigma, tail):
    groups = lax.axis_size("outer")
    inner = lax.axis_size("inner")
    chips = inner // 2
    _, per_node, factors_n = normals.shape
    instruments = loadings.shape[0]
    tail_count = tail.shape[0]
    paths = per_node * inner
    rows = instruments // (groups * inner)
    paired = chips & (chips - 1) == 0

    def partner(of, d):
        return of ^ d if paired else (of + d) % chips

    def beyond(of, s):
        return of ^ s if groups & (groups - 1) == 0 else (of + s) % groups

    def to_core(x):
        return lax.ppermute(x, "inner", [(i, i ^ 1) for i in range(inner)])

    def to_chip(x, d):
        return lax.ppermute(
            x, "inner", [(i, partner(i // 2, d) * 2 + i % 2) for i in range(inner)]
        )

    def to_group(x, s):
        return lax.ppermute(x, "outer", [(g, beyond(g, s)) for g in range(groups)])

    bound = 32768.0 / (tail_count * paths)
    unit = 1.0 / (bound * tail_count * paths)

    tail, normals, states, loadings = (
        pltpu.with_memory_space_constraint(x, pltpu.HBM)
        for x in (tail, normals, states, loadings.reshape(groups * inner, rows, factors_n))
    )
    wide = 128 if 128 % rows == 0 else rows
    strikes, hedge = strikes.reshape(-1, wide), hedge.reshape(-1, wide)

    chosen, mine, other = gather_nodes(tail, normals)
    sums, squares = mine + to_core(other)
    count = 2 * per_node
    within = squares - sums * sums / count
    message = to_message(sums, within)
    chosen, message, strikes = lax.optimization_barrier((chosen, message, strikes))
    rounds = [1 << k for k in range(chips.bit_length() - 1)] if paired and chips > 4 else []
    if not rounds:
        arrived = [of_message(to_chip(message, d)) for d in range(chips - 1, 0, -1)]
        sums, within = pooled([(sums, within), *arrived], count)
        count *= chips
    for d in rounds:
        arrived = to_chip(message, d)
        sums, within = pooled([(sums, within), of_message(arrived)], count)
        count *= 2
        if d != rounds[-1]:
            message = to_message(sums, within)
    theirs = to_core(chosen)
    steps = range(groups)
    relayed = chips == 4 and groups % 2 == 0
    if relayed:
        half = groups // 2
        low, high = steps[:half], steps[half:]
        plan = [
            [(3, s) for s in steps],
            [(1, s) for s in high] + [(2, s) for s in high] + [(0, s) for s in steps],
            [(2, s) for s in low] + [(1, s) for s in low],
        ]
        first_sizes = (half * rows,) * 2
    else:
        plan = [[(d, s) for s in steps] for d in range(chips - 1, -1, -1)]
        first_sizes = (groups * rows,)
    far = lambda chip, d, group, s: (partner(chip, d), beyond(group, s))
    levels, live, gain, *parts = order(
        unit, bound, plan, far, tail, states, loadings, strikes, hedge
    )
    ordered = [part.reshape(-1, factors_n) for part in parts[: len(plan)]]
    terms = parts[len(plan) :]
    sums, within, theirs, levels, live, gain, ordered, terms = lax.optimization_barrier(
        (sums, within, theirs, levels, live, gain, ordered, terms)
    )
    stats = jnp.stack([sums / count, live * lax.rsqrt(within / count + EPSILON)])
    their_stats = to_core(stats)

    sigmas = sigma.reshape(1, factors_n)
    *ready, done = ready_rows(chosen, theirs, stats, levels, sigmas, ordered[0], terms[0])

    tile = tile_of(CAP, per_node)
    results = first_chunk(
        first_sizes, chosen, theirs, their_stats, levels, sigmas, done, ordered[0], terms[0]
    )
    rest, first = tuple(results[:2]), results[2:]

    def chunk(k, sizes, *after):
        kept, _ = lax.optimization_barrier((rest, after))
        return next_chunk(sizes, tile, ready, kept, ordered[k], terms[k])

    def plus(x, y):
        return x + y.astype(F32)

    if relayed:
        size = half * rows
        a3, b3 = first
        b3 = b3.astype(F16)
        from_b3 = to_chip(b3, 1)
        b1, b2, a0, b0 = chunk(1, (size,) * 4, b3)
        a3, b1, b2 = lax.optimization_barrier((a3, b1, b2))
        a3 = a3.astype(F16)
        from_a3 = to_chip(a3, 2)
        b1, b2 = b1.astype(F16), plus(b2, from_b3).astype(F16)
        from_b1, from_b2 = to_chip(b1, 1), to_chip(b2, 2)
        a2, a1 = chunk(2, (size,) * 2, a3, b1, b2)
        a2, a1 = a2.astype(F16), plus(a1, from_a3).astype(F16)
        from_a2, from_a1 = to_chip(a2, 2), to_chip(a1, 1)
        b0, _ = lax.optimization_barrier((b0, (a2, a1)))
        kept_b = plus(plus(b0, from_b1), from_b2)
        sent = [kept_b[k * rows :][:rows].astype(F16) for k in range(half)]
        sent, a0 = lax.optimization_barrier((sent, a0))
        kept_a = plus(plus(a0, from_a2), from_a1)
        sent = [kept_a[k * rows :][:rows].astype(F16) for k in range(1, half)] + sent
        owned = kept_a[:rows]
    else:
        arrived = []
        (kept,) = first
        for k in range(1, chips):
            sent = kept.astype(F16)
            arrived.append(to_chip(sent, chips - k))
            (kept,) = chunk(k, first_sizes, sent)
        for item in arrived:
            kept = plus(kept, item)
        sent = [kept[s * rows :][:rows].astype(F16) for s in range(1, groups)]
        owned = kept[:rows]
    far_sums = None
    for s in range(max(1, groups // 2), groups):
        item = to_group(sent[s - 1], s).astype(F32)
        far_sums = item if far_sums is None else far_sums + item
    far_sums = lax.optimization_barrier(far_sums)
    for s in range(1, max(1, groups // 2)):
        owned = plus(owned, to_group(sent[s - 1], s))
    owned = owned + far_sums
    return gain * owned


def solution(mesh):
    placed = (P("outer", "inner", None), P("outer", None), P(), P(), P(), P(), P())
    return jax.shard_map(
        body, mesh=mesh, in_specs=placed, out_specs=P(("outer", "inner"), None), check_vma=False
    )
```
